256 devices in a mesh: lon: 16 (over z, core), lat: 16 (over x, y).
Axes of the slice: x: 4, y: 4, z: 8, core: 2. Of those that a mesh axis runs over, the one named last changes fastest.
Arguments:
- state: float32 [3, 16, 512, 4096], P(None, None, 'lat', 'lon'), may hold values from -6 to 6
- kmt: int32 [512, 4096], P('lat', 'lon'), may hold values from 0 to 16, as said below
- first_guess: float32 [512, 4096], P('lat', 'lon'), may hold values from -6 to 6
Outputs:
- next_state: float32 [3, 16, 512, 4096], P(None, None, 'lat', 'lon')
- pressure: float32 [512, 4096], P('lat', 'lon')
The draws below stay inside these ranges and needn't reach their ends.
Inputs may be any that keep to these rules, and one draw needn't show every extreme that they name: `kmt`: 0 marks a land column.
All inputs are finite; a program needn't handle non-finite values.
Results may differ from the reference program's by a relative error of at most 0.0001.
Values sent between devices are 32-bit elements; how exact they have to be, the bound alone decides.
No kernel may reach another device: no remote copies, remote signals or barrier semaphores. Data moves between devices by JAX's collectives and lax.ppermute only.
A program may use at most 64 MiB of HBM per device.

```python
import jax
import jax.numpy as jnp
from jax import lax

LEVELS = 16
CY = 32
CX = 256
ITERS = 4
NY = 512
NX = 4096


def draw_kmt(key, part):
    key = jax.random.fold_in(key, 7)
    node_key, rough_key = jax.random.split(key)
    node_cols = max(NX // (2 * CX), 2)
    node_rows = max(NY // (2 * CY), 1) + 1
    spread = max(1, LEVELS // 4)
    node_values = jax.random.randint(node_key, (node_rows, node_cols), -LEVELS, 2 * LEVELS + 1)
    node_index = lax.broadcasted_iota(jnp.int32, (node_rows, node_cols), 0)
    node_values = jnp.where(node_index == 0, -LEVELS, jnp.where(node_index == node_rows - 1, 2 * LEVELS, node_values))
    place_cols = jnp.arange(NX, dtype=jnp.int32) * node_cols
    west_node = place_cols // NX
    col_frac = place_cols % NX
    east_node = (west_node + 1) % node_cols
    across = (node_values[:, west_node] * (NX - col_frac)[None, :] + node_values[:, east_node] * col_frac[None, :]) // NX
    place_rows = jnp.arange(NY, dtype=jnp.int32) * (node_rows - 1)
    south_node = place_rows // NY
    row_frac = place_rows % NY
    north_node = jnp.minimum(south_node + 1, node_rows - 1)
    smooth = (across[south_node] * (NY - row_frac)[:, None] + across[north_node] * row_frac[:, None]) // NY
    rough_part = jax.random.randint(rough_key, (NY, NX), -spread, spread + 1)
    return jnp.clip(smooth + rough_part, 0, LEVELS).astype(jnp.int32)


def levels(rng, dims, cuts, low, top_value):
    def one(dim, blocks):
        steps = jax.random.uniform(jax.random.fold_in(jax.random.fold_in(rng, 6), dim), (blocks,), jnp.float32, low / len(cuts), top_value / len(cuts))
        return jnp.repeat(jnp.exp(steps), dims[dim] // blocks).reshape((-1,) + (1,) * (len(dims) - dim - 1))

    loudness = one(*cuts[0])
    for cut in cuts[1:]:
        loudness = loudness * one(*cut)
    return loudness


def bell_draw(stream_key, dims, scale, bound, cuts=(), held_as=jnp.bfloat16):
    drawn = scale * jax.random.normal(stream_key, dims, jnp.float32)
    if cuts:
        drawn = drawn * levels(stream_key, dims, cuts, -0.22, 0.18)
    return jnp.clip(drawn, -bound, bound).astype(held_as)


def setup_inputs(seed: int = 0) -> dict:
    streams_of = jax.random.split(jax.random.key(seed), 4)
    return {
        "state": bell_draw(streams_of[0], (3, LEVELS, NY, NX), 1.0, 6.0, ((2, 16), (3, 16)), jnp.float32),
        "kmt": draw_kmt(jax.random.fold_in(streams_of[3], 71), 0),
        "first_guess": bell_draw(streams_of[2], (NY, NX), 1.0, 6.0, ((0, 16), (1, 16)), jnp.float32),
    }


viscosity = 0.12
diffusivity = 0.1
advection_scale = 0.5
vertical_mix = 0.2
coriolis_scale = 0.6
time_step = 0.5
storage = 0.5
gravity = 1.5
neighbours = ((0, 1, 2.0 / 3.0), (0, -1, 2.0 / 3.0), (1, 0, 2.0 / 3.0), (-1, 0, 2.0 / 3.0), (1, 1, 1.0 / 6.0), (1, -1, 1.0 / 6.0), (-1, 1, 1.0 / 6.0), (-1, -1, 1.0 / 6.0))


def beside(padded, row_shift, col_shift):
    height = padded.shape[-2]
    breadth = padded.shape[-1]
    return padded[..., 1 + row_shift:height - 1 + row_shift, 1 + col_shift:breadth - 1 + col_shift]


def pad_grid(field, width):
    spec = [(0, 0)] * (field.ndim - 2) + [(width, width), (0, 0)]
    field = jnp.pad(field, spec)
    return jnp.concatenate([field[..., -width:], field, field[..., :width]], axis=-1)


def coriolis_rows(first_row, count, total_rows):
    rows = jnp.arange(count).astype(jnp.float32) + first_row
    angle = (jnp.pi / 180.0) * (-80.0 + 160.0 * (rows + 0.5) / total_rows)
    return coriolis_scale * jnp.sin(angle)


def tendencies(padded_state, padded_wet, coriolis):
    centre = beside(padded_state, 0, 0)
    wet_centre = beside(padded_wet, 0, 0)
    wet_east = beside(padded_wet, 0, 1)
    wet_west = beside(padded_wet, 0, -1)
    wet_north = beside(padded_wet, 1, 0)
    wet_south = beside(padded_wet, -1, 0)
    east_vals = beside(padded_state, 0, 1) * wet_east
    west_vals = beside(padded_state, 0, -1) * wet_west
    north_vals = beside(padded_state, 1, 0) * wet_north
    south_vals = beside(padded_state, -1, 0) * wet_south
    laplace = east_vals + west_vals + north_vals + south_vals - (wet_east + wet_west + wet_north + wet_south) * centre
    grad_east = 0.5 * (east_vals - west_vals)
    grad_north = 0.5 * (north_vals - south_vals)
    zonal = centre[0]
    merid = centre[1]
    tracer = centre[2]
    carried = zonal * grad_east + merid * grad_north
    rotation = coriolis[:, None]
    zonal_tend = viscosity * laplace[0] + rotation * merid - advection_scale * carried[0]
    merid_tend = viscosity * laplace[1] - rotation * zonal - advection_scale * carried[1]
    level_zero = jnp.zeros_like(tracer[:1])
    tracer_above = jnp.concatenate([level_zero, tracer[:-1]], axis=0)
    tracer_below = jnp.concatenate([tracer[1:], level_zero], axis=0)
    wet_above = jnp.concatenate([level_zero, wet_centre[:-1]], axis=0)
    wet_below = jnp.concatenate([wet_centre[1:], level_zero], axis=0)
    vertical = wet_above * (tracer_above - tracer) + wet_below * (tracer_below - tracer)
    tracer_tend = diffusivity * laplace[2] - advection_scale * carried[2] + vertical_mix * vertical
    return jnp.stack([zonal_tend, merid_tend, tracer_tend]) * wet_centre


def couplings(padded_depth):
    centre = beside(padded_depth, 0, 0)
    terms = jnp.stack([weight * jnp.minimum(centre, beside(padded_depth, row_shift, col_shift)) for row_shift, col_shift, weight in neighbours])
    return terms, storage + jnp.sum(terms, axis=0)


def operate(padded, terms, diagonal):
    total = diagonal * beside(padded, 0, 0)
    for number, (row_shift, col_shift, weight) in enumerate(neighbours):
        total = total - terms[number] * beside(padded, row_shift, col_shift)
    return total


def reference(state, kmt, first_guess):
    wet = (jnp.arange(LEVELS, dtype=jnp.int32)[:, None, None] < kmt[None]).astype(jnp.float32)
    coriolis = coriolis_rows(0, NY, NY)
    tend = tendencies(pad_grid(state, 1), pad_grid(wet, 1), coriolis)
    advanced = state + time_step * tend
    transports = jnp.sum(advanced[:2] * wet[None], axis=1)
    padded_flow = pad_grid(transports, 1)
    divergence = 0.5 * (beside(padded_flow[0], 0, 1) - beside(padded_flow[0], 0, -1)) + 0.5 * (beside(padded_flow[1], 1, 0) - beside(padded_flow[1], -1, 0))
    ocean = (kmt > 0).astype(jnp.float32)
    depth = kmt.astype(jnp.float32) / LEVELS
    terms, diagonal = couplings(pad_grid(depth, 1))
    start = first_guess * ocean
    rhs = storage * ocean * (start - time_step * divergence)
    iterate = start
    residual = rhs - operate(pad_grid(iterate, 1), terms, diagonal)
    scaled = residual / diagonal
    direction = scaled
    norm_now = jnp.sum(residual * scaled)
    for sweep in range(ITERS):
        image = operate(pad_grid(direction, 1), terms, diagonal)
        step_size = norm_now / jnp.sum(direction * image)
        iterate = iterate + step_size * direction
        residual = residual - step_size * image
        if sweep + 1 < ITERS:
            scaled = residual / diagonal
            norm_next = jnp.sum(residual * scaled)
            direction = scaled + (norm_next / norm_now) * direction
            norm_now = norm_next
    padded_height = pad_grid(iterate, 1)
    slope_east = 0.5 * (beside(padded_height, 0, 1) - beside(padded_height, 0, -1))
    slope_north = 0.5 * (beside(padded_height, 1, 0) - beside(padded_height, -1, 0))
    correction = jnp.stack([slope_east, slope_north, jnp.zeros_like(slope_east)]) * (time_step * gravity)
    next_state = (advanced - correction[:, None]) * wet[None]
    return next_state, gravity * iterate
```

```python
import functools

import jax
import jax.numpy as jnp
from jax import lax
from jax.experimental import pallas as pl
from jax.experimental.pallas import tpu as pltpu
from jax.sharding import PartitionSpec as P

ITERS = 4
F32 = jnp.float32

viscosity = 0.12
diffusivity = 0.1
advection_scale = 0.5
vertical_mix = 0.2
coriolis_scale = 0.6
time_step = 0.5
storage = 0.5
gravity = 1.5
edge_weight = 2.0 / 3.0
corner_weight = 1.0 / 6.0

TILE = 8
LANES = 128
HALO = 6

LOWEST = storage / (storage + 4 * edge_weight + 4 * corner_weight)
HIGHEST = 2.0 - LOWEST
VMEM_LIMIT = 48 * 1024 * 1024


def params():
    return pltpu.CompilerParams(vmem_limit_bytes=VMEM_LIMIT)


def turn(x, shift, axis):
    return pltpu.roll(x, shift % x.shape[axis], axis)


def east_of(x):
    return turn(x, -1, 1)


def west_of(x):
    return turn(x, 1, 1)


def north_of(x):
    return turn(x, -1, 0)


def south_of(x):
    return turn(x, 1, 0)


def lane_of(shape):
    return lax.broadcasted_iota(jnp.int32, shape, len(shape) - 1)


def is_even(axis):
    return lax.rem(lax.axis_index(axis), 2) == 0


def swap(first, a, b):
    return jnp.where(first, a, b), jnp.where(first, b, a)


def pack_rows(
    low, high, kmt_low, kmt_high, guess_low, guess_high, msg_even, msg_odd
):
    levels = low.shape[1]
    even = is_even("lat")
    row = lax.broadcasted_iota(jnp.int32, low.shape[2:], 0)

    def put(slot, to_north, to_south):
        a, b = swap(even, to_north, to_south)
        msg_even[slot] = a
        msg_odd[slot] = b

    for k in range(levels):
        north = jnp.where(row == 0, turn(high[2, k], 1, 0), high[0, k])
        south = jnp.where(row == TILE - 1, turn(low[2, k], -1, 0), low[0, k])
        put(k, north, south)
        put(levels + k, high[1, k], low[1, k])
    put(2 * levels, kmt_high[...].astype(F32), kmt_low[...].astype(F32))
    put(2 * levels + 1, guess_high[...], guess_low[...])


def stacked(south, own, north):
    return jnp.concatenate([south, own, north], axis=0)


def pack_cols(first, last, kmt, guess, rows_even, rows_odd, msg_even, msg_odd):
    levels = first.shape[1]
    tall = first.shape[2] + 2 * TILE
    lat_even = is_even("lat")
    lon_even = is_even("lon")
    group = lane_of((tall, LANES)) // TILE
    breadth = kmt.shape[1]

    def halos(slot, cols):
        north, south = swap(lat_even, rows_even[slot, :, cols], rows_odd[slot, :, cols])
        return south, north

    west_cols = slice(0, LANES)
    east_cols = slice(breadth - LANES, breadth)

    def columns(field, k):
        out = []
        for edge, cols in ((first, west_cols), (last, east_cols)):
            own = edge[field, k]
            south, north = halos(k if field != 1 else levels + k, cols)
            if field == 2:
                south, north = (turn(south, -1, 0), turn(north, 1, 0))
            out.append(stacked(south, own, north))
        return out

    def place(k, west, east, acc):
        to_west, to_east = acc
        to_west = jnp.where(group == k, pltpu.roll(west, 2 + TILE * k, 1), to_west)
        to_east = jnp.where(
            group == k, pltpu.roll(east, lax.rem(HALO + TILE * k, LANES), 1), to_east
        )
        return to_west, to_east

    def put(slot, acc):
        to_west, to_east = acc
        a, b = swap(lon_even, to_east, to_west)
        msg_even[slot] = a
        msg_odd[slot] = b

    blank = (jnp.zeros((tall, LANES), F32),) * 2
    for field in range(3):

        def body(k, acc, field=field):
            west, east = columns(field, k)
            return place(k, west, east, acc)

        put(field, lax.fori_loop(0, levels, body, blank, unroll=4))
    acc = blank
    for number, own in enumerate((kmt[...].astype(F32), guess[...])):
        sides = []
        for cols in (west_cols, east_cols):
            south, north = halos(2 * levels + number, cols)
            sides.append(stacked(south, own[:, cols], north))
        acc = place(jnp.int32(number), sides[0], sides[1], acc)
    put(3, acc)


def rotation_rows(tall, lanes, rows_here):
    total_rows = rows_here * lax.axis_size("lat")
    row = lax.broadcasted_iota(jnp.int32, (tall, lanes), 0)
    row = (row - TILE + lax.axis_index("lat") * rows_here).astype(F32)
    angle = jnp.pi / 180.0 * (-80.0 + 160.0 * (row + 0.5) / total_rows)
    return coriolis_scale * jnp.sin(angle)


def around(x):
    return east_of(x), west_of(x), north_of(x), south_of(x)


def count_wet(sides, level):
    total = None
    for side in sides:
        term = jnp.where(side > level, 1.0, 0.0)
        total = term if total is None else total + term
    return total


def spread(x, sides, count, coefficient, zonal, merid):
    east, west, north, south = sides
    laplace = east + west + north + south - count * x
    return (
        (time_step * coefficient) * laplace
        - zonal * (east - west)
        - merid * (north - south)
    )


carry = 0.5 * time_step * advection_scale


def advance_flow(u, v, wet, count, half_turn):
    zonal, merid = (carry * u, carry * v)
    new_u = u + (spread(u, around(u), count, viscosity, zonal, merid) + half_turn * v)
    new_v = v + (spread(v, around(v), count, viscosity, zonal, merid) - half_turn * u)
    return jnp.where(wet, new_u, 0.0), jnp.where(wet, new_v, 0.0)


def advance_inner(state, kmt, rows_even, rows_odd, out, flow_u, flow_v, turning):
    levels, rows_here, breadth = state.shape[1:]
    tall = rows_here + 2 * TILE
    lat_even = is_even("lat")

    def halos(slot):
        north, south = swap(lat_even, rows_even[slot], rows_odd[slot])
        return south, north

    south, north = halos(2 * levels)
    depth = stacked(south, kmt[...].astype(F32), north)
    beside = around(depth)
    rotation = rotation_rows(tall, LANES, rows_here)
    turning[...] = rotation
    half_turn = time_step * rotation[:, :1]
    own = slice(TILE, TILE + rows_here)
    flow_u[...] = jnp.zeros_like(flow_u)
    flow_v[...] = jnp.zeros_like(flow_v)

    def body(k, _):
        level = k.astype(F32)
        wet = depth > level
        count = count_wet(beside, level)
        u_south, u_north = halos(k)
        v_south, v_north = halos(levels + k)
        u = jnp.where(wet, stacked(u_south, state[0, k], u_north), 0.0)
        v = jnp.where(wet, stacked(v_south, state[1, k], v_north), 0.0)
        new_u, new_v = advance_flow(u, v, wet, count, half_turn)
        flow_u[...] += new_u
        flow_v[...] += new_v
        out[0, k] = new_u[own]
        out[1, k] = new_v[own]
        here = state[2, k]
        tracer = jnp.where(
            wet, stacked(turn(u_south, -1, 0), here, turn(u_north, 1, 0)), 0.0
        )
        east, west = (east_of(tracer[own]), west_of(tracer[own]))
        north, south = (north_of(tracer)[own], south_of(tracer)[own])
        change = spread(
            tracer[own],
            (east, west, north, south),
            count[own],
            diffusivity,
            carry * u[own],
            carry * v[own],
        )
        above = state[2, jnp.maximum(k - 1, 0)]
        below = state[2, jnp.minimum(k + 1, levels - 1)]
        vertical = (above - here) + jnp.where(depth[own] > level + 1.0, below - here, 0.0)
        out[2, k] = jnp.where(
            wet[own], here + (change + (time_step * vertical_mix) * vertical), 0.0
        )
        return 0

    lax.fori_loop(0, levels, body, 0)


def over_groups(x):
    for step in (TILE, 2 * TILE, 4 * TILE, 8 * TILE):
        x = x + pltpu.roll(x, step, 1)
    return x


def krylov(
    sent_even, sent_odd, got_even, got_odd, flow_u, flow_v, kmt, guess,
    rows_even, rows_odd, turning, edges, basis, moments,
):
    levels = (rows_even.shape[0] - 2) // 2
    rows_here, breadth = kmt.shape
    tall = rows_here + 2 * TILE
    lat_even = is_even("lat")
    lon_even = is_even("lon")
    lane = lane_of((tall, LANES))
    place = lax.rem(lane, TILE)
    group = lane // TILE
    level = group.astype(F32)
    own = slice(TILE, TILE + rows_here)
    half_turn = time_step * turning[...]

    def strips(slot):
        to_east, to_west = swap(lon_even, sent_even[slot], sent_odd[slot])
        from_east, from_west = swap(lon_even, got_even[slot], got_odd[slot])
        west = jnp.where(place < HALO, from_west, turn(to_west, 4, 1))
        east = jnp.where(place >= TILE - HALO, from_east, turn(to_east, -4, 1))
        return west, east

    u_sides, v_sides, t_sides, other = [strips(slot) for slot in range(4)]
    sums = []
    for side in range(2):
        depth = over_groups(jnp.where(group == 0, other[side], 0.0))
        start = over_groups(jnp.where(group == 1, other[side], 0.0))
        wet = depth > level
        count = count_wet(around(depth), level)
        u = jnp.where(wet, u_sides[side], 0.0)
        v = jnp.where(wet, v_sides[side], 0.0)
        new_u, new_v = advance_flow(u, v, wet, count, half_turn)
        here = jnp.where(wet, t_sides[side], 0.0)
        change = spread(here, around(here), count, diffusivity, carry * u, carry * v)
        above = jnp.where(group > 0, turn(here, TILE, 1) - here, 0.0)
        below = jnp.where(depth > level + 1.0, turn(here, -TILE, 1) - here, 0.0)
        new_t = jnp.where(
            wet, here + (change + (time_step * vertical_mix) * (above + below)), 0.0
        )
        edges[side, 0] = new_u[own]
        edges[side, 1] = new_v[own]
        edges[side, 2] = new_t[own]
        sums.append((over_groups(new_u), over_groups(new_v), depth, start))

    def assemble(field, number, seam):
        west = turn(sums[0][number], 2, 1)
        east = turn(sums[1][number], -2, 1)
        halo = jnp.where(lane < LANES // 2, east, west)
        tiles = [field[:, i : i + LANES] for i in range(0, breadth, LANES)]
        if seam:
            tiles[0] = jnp.where(lane == 0, west, tiles[0])
            tiles[-1] = jnp.where(lane == LANES - 1, east, tiles[-1])
        return jnp.concatenate(tiles + [halo], axis=1)

    def tall_field(slot, value):
        north, south = swap(lat_even, rows_even[slot], rows_odd[slot])
        return stacked(south, value, north)

    wide_u = assemble(flow_u[...], 0, True)
    wide_v = assemble(flow_v[...], 1, True)
    wet_levels = assemble(tall_field(2 * levels, kmt[...].astype(F32)), 2, False)
    first = assemble(tall_field(2 * levels + 1, guess[...]), 3, False)

    divergence = 0.5 * (east_of(wide_u) - west_of(wide_u)) + 0.5 * (
        north_of(wide_v) - south_of(wide_v)
    )
    depth = wet_levels * (1.0 / levels)
    ocean = wet_levels > 0.0
    to_east = edge_weight * jnp.minimum(depth, east_of(depth))
    to_north = edge_weight * jnp.minimum(depth, north_of(depth))
    depth_north = north_of(depth)
    to_ne = corner_weight * jnp.minimum(depth, east_of(depth_north))
    to_nw = corner_weight * jnp.minimum(depth, west_of(depth_north))
    to_west = west_of(to_east)
    to_south = south_of(to_north)
    to_sw = south_of(west_of(to_ne))
    to_se = south_of(east_of(to_nw))
    diagonal = storage + (
        (to_east + to_west) + (to_north + to_south) + ((to_ne + to_nw) + (to_se + to_sw))
    )

    def neighbours(x):
        up, down = (north_of(x), south_of(x))
        eastern = to_east * x + to_ne_w * up + to_se_w * down
        western = to_west * x + to_nw_e * up + to_sw_e * down
        return to_north * up + to_south * down + (east_of(eastern) + west_of(western))

    to_ne_w = west_of(to_ne)
    to_se_w = west_of(to_se)
    to_nw_e = east_of(to_nw)
    to_sw_e = east_of(to_sw)
    to_east, to_west = (west_of(to_east), east_of(to_west))

    start = jnp.where(ocean, first, 0.0)
    rhs = jnp.where(ocean, storage * (start - time_step * divergence), 0.0)
    residual = rhs - (diagonal * start - neighbours(start))
    inverse = 1.0 / diagonal
    vectors = [residual * inverse]
    basis[0] = start
    basis[1] = vectors[0]
    for k in range(1, ITERS):
        vectors.append(neighbours(vectors[-1]) * inverse)
        basis[k + 1] = vectors[k]
    last = neighbours(vectors[-1])

    def inner(x):
        return x[own, :breadth]

    weighted = [inner(diagonal * x) for x in vectors] + [inner(last)]
    held = [inner(x) for x in vectors]
    slot = lane_of((1, LANES))
    total = jnp.zeros((1, LANES), F32)
    for m in range(2 * ITERS):
        product = held[m // 2] * weighted[(m + 1) // 2]
        total = jnp.where(slot == m, jnp.sum(product), total)
    moments[...] = total


def finish(shares, basis, edges, kmt, advanced, out, pressure):
    levels, rows_here, breadth = advanced.shape[1:]
    own = slice(TILE, TILE + rows_here)
    sums = jnp.sum(shares[...], axis=0, keepdims=True)
    size = 2 * ITERS
    res = [sums[:, m : m + 1] for m in range(size)]
    dirn = list(res)
    one, zero = (jnp.ones((1, 1), F32), jnp.zeros((1, 1), F32))
    res_in = [one] + [zero] * (ITERS - 1)
    dir_in = list(res_in)
    height_in = [zero] * ITERS
    for k in range(ITERS):
        step = res[k] / (dirn[k] - dirn[k + 1])
        step = jnp.clip(step, 1.0 / HIGHEST, 1.0 / LOWEST)
        height_in = [h + step * d for h, d in zip(height_in, dir_in)]
        if k + 1 < ITERS:
            new = [res[m] - step * (dirn[m] - dirn[m + 1]) for m in range(len(dirn) - 1)]
            ratio = jnp.clip(step * new[k + 1] / res[k], 0.0, HIGHEST / LOWEST)
            dirn = [n + ratio * d for n, d in zip(new, dirn)]
            res = new
            moved = [zero] + dir_in[:-1]
            res_in = [r - step * (d - m) for r, d, m in zip(res_in, dir_in, moved)]
            dir_in = [r + ratio * d for r, d in zip(res_in, dir_in)]
    height = basis[0]
    for k in range(ITERS):
        height = height + height_in[k] * basis[k + 1]
    pressure[...] = gravity * height[own, :breadth]
    pull = 0.5 * time_step * gravity
    slope_east = pull * (east_of(height) - west_of(height))[own, :breadth]
    slope_north = pull * (north_of(height) - south_of(height))[own, :breadth]
    wet_levels = kmt[...]
    lane = lane_of((rows_here, LANES))

    def body(k, _):
        wet = wet_levels > k
        for field, slope in ((0, slope_east), (1, slope_north), (2, None)):
            value = advanced[field, k]
            west = pltpu.roll(edges[0, field], lax.rem(2 * LANES - HALO - TILE * k, LANES), 1)
            east = pltpu.roll(
                edges[1, field], lax.rem(2 * LANES - 2 - TILE * k, LANES), 1
            )
            tiles = [value[:, i : i + LANES] for i in range(0, breadth, LANES)]
            tiles[0] = jnp.where(lane == 0, west, tiles[0])
            tiles[-1] = jnp.where(lane == LANES - 1, east, tiles[-1])
            value = jnp.concatenate(tiles, axis=1)
            if slope is not None:
                value = jnp.where(wet, value - slope, 0.0)
            out[field, k] = value
        return 0

    lax.fori_loop(0, levels, body, 0, unroll=2)


def pairs(axis):
    peers = lax.axis_size(axis)
    even = [(i, i ^ 1) for i in range(peers)]
    odd = [(i, ((i + 1) ^ 1) - 1) for i in range(1, peers - 1)]
    if axis == "lon":
        odd += [(0, peers - 1), (peers - 1, 0)]
    return even, odd


def exchange(axis, to_even, to_odd):
    even, odd = pairs(axis)
    return lax.ppermute(to_even, axis, even), lax.ppermute(to_odd, axis, odd)


def on_device(state, kmt, first_guess):
    _, levels, rows_here, breadth = state.shape
    tall = rows_here + 2 * TILE
    wide = breadth + LANES
    shape = lambda *dims: jax.ShapeDtypeStruct(dims, F32)

    last_row = rows_here // TILE - 1
    edge = lambda row: pl.BlockSpec((3, levels, TILE, breadth), lambda i: (0, 0, row, 0))
    flat = lambda row: pl.BlockSpec((TILE, breadth), lambda i: (row, 0))
    slots = 2 * levels + 2
    whole = lambda *dims: pl.BlockSpec(dims, lambda i: (0,) * len(dims))
    to_even, to_odd = pl.pallas_call(
        pack_rows,
        grid=(1,),
        in_specs=[edge(0), edge(last_row)] + [flat(0), flat(last_row)] * 2,
        out_specs=[whole(slots, TILE, breadth)] * 2,
        out_shape=[shape(slots, TILE, breadth)] * 2,
        compiler_params=params(),
    )(state, state, kmt, kmt, first_guess, first_guess)
    rows_even, rows_odd = exchange("lat", to_even, to_odd)

    last_lane = breadth // LANES - 1
    edge_cols = lambda col: pl.BlockSpec((3, levels, rows_here, LANES), lambda i: (0, 0, 0, col))
    rows_spec = whole(slots, TILE, breadth)
    field_spec = whole(rows_here, breadth)
    sent_even, sent_odd = pl.pallas_call(
        pack_cols,
        grid=(1,),
        in_specs=[edge_cols(0), edge_cols(last_lane), field_spec, field_spec, rows_spec, rows_spec],
        out_specs=[whole(4, tall, LANES)] * 2,
        out_shape=[shape(4, tall, LANES)] * 2,
        compiler_params=params(),
    )(state, state, kmt, first_guess, rows_even, rows_odd)
    got_even, got_odd = exchange("lon", sent_even, sent_odd)

    advanced, flow_u, flow_v, turning = pl.pallas_call(
        advance_inner,
        out_shape=[
            shape(3, levels, rows_here, breadth),
            shape(tall, breadth),
            shape(tall, breadth),
            shape(tall, LANES),
        ],
        compiler_params=params(),
        cost_estimate=pl.CostEstimate(
            flops=60 * state.size, bytes_accessed=8 * state.size, transcendentals=0
        ),
    )(state, kmt, rows_even, rows_odd)

    edges, basis, moments = pl.pallas_call(
        krylov,
        out_shape=[
            shape(2, 3, rows_here, LANES),
            shape(ITERS + 1, tall, wide),
            shape(1, LANES),
        ],
        compiler_params=params(),
    )(
        sent_even, sent_odd, got_even, got_odd, flow_u, flow_v, kmt, first_guess,
        rows_even, rows_odd, turning,
    )

    devices = lax.axis_size("lon") * lax.axis_size("lat")
    shares = jnp.broadcast_to(moments[None], (devices, 1, LANES))
    shares = lax.all_to_all(shares, ("lon", "lat"), 0, 0)
    next_state, pressure = pl.pallas_call(
        finish,
        out_shape=[shape(3, levels, rows_here, breadth), shape(rows_here, breadth)],
        compiler_params=params(),
    )(shares.reshape(devices, LANES), basis, edges, kmt, advanced)
    return next_state, pressure


def solution(mesh):
    placed = (P(None, None, "lat", "lon"), P("lat", "lon"), P("lat", "lon"))
    return jax.shard_map(
        on_device,
        mesh=mesh,
        in_specs=placed,
        out_specs=(P(None, None, "lat", "lon"), P("lat", "lon")),
        check_vma=False,
    )
```

```python
import jax
import jax.numpy as jnp
from jax import lax
from jax.experimental import pallas as pl
from jax.experimental.pallas import tpu as pltpu
from jax.sharding import PartitionSpec as P

ITERS = 4
F32 = jnp.float32

viscosity = 0.12
diffusivity = 0.1
advection_scale = 0.5
vertical_mix = 0.2
coriolis_scale = 0.6
time_step = 0.5
storage = 0.5
gravity = 1.5
edge_weight = 2.0 / 3.0
corner_weight = 1.0 / 6.0

TILE = 8
LANES = 128
HALO = 6

LOWEST = storage / (storage + 4 * edge_weight + 4 * corner_weight)
HIGHEST = 2.0 - LOWEST
VMEM_LIMIT = 16 * 1024 * 1024
VMEM_FIRST = 64520000


def params(limit=VMEM_LIMIT):
    return pltpu.CompilerParams(vmem_limit_bytes=limit)


def cost(size):
    return pl.CostEstimate(flops=60 * size, bytes_accessed=8 * size, transcendentals=0)


def turn(x, shift, axis):
    return pltpu.roll(x, shift % x.shape[axis], axis)


def east_of(x):
    return turn(x, -1, 1)


def west_of(x):
    return turn(x, 1, 1)


def north_of(x):
    return turn(x, -1, 0)


def south_of(x):
    return turn(x, 1, 0)


def lane_of(shape):
    return lax.broadcasted_iota(jnp.int32, shape, len(shape) - 1)


def is_even(axis):
    return lax.rem(lax.axis_index(axis), 2) == 0


def swap(first, a, b):
    return jnp.where(first, a, b), jnp.where(first, b, a)


def pack_rows(state, kmt, guess, msg_odd, msg_even, tracer, levels_wet, sems):
    levels, rows_here, breadth = state.shape[1:]
    odd = lax.rem(lax.axis_index("lat"), 2)
    sides = ((msg_even, odd), (msg_odd, 1 - odd))
    copies = []

    def copy(source, target):
        copies.append(pltpu.make_async_copy(source, target, sems.at[len(copies)]))
        copies[-1].start()

    for number, (msg, southern) in enumerate(sides):
        rows = pl.ds(pl.multiple_of((1 - southern) * (rows_here - TILE), TILE), TILE)
        copy(state.at[0, :, rows, :], msg.at[0:levels])
        copy(state.at[1, :, rows, :], msg.at[levels : 2 * levels])
        copy(state.at[2, :, rows, :], tracer.at[number])
        copy(kmt.at[rows, :], levels_wet.at[number])
        copy(guess.at[rows, :], msg.at[2 * levels + 1])
    row = lax.broadcasted_iota(jnp.int32, (TILE, breadth), 0)
    for item in copies:
        item.wait()
    for number, (msg, southern) in enumerate(sides):
        slot = row == southern * (TILE - 1)
        msg[2 * levels] = levels_wet[number].astype(F32)
        for k in range(levels):
            value = tracer[number, k]
            value = jnp.where(southern == 0, turn(value, 1, 0), turn(value, -1, 0))
            msg[k] = jnp.where(slot, value, msg[k])


def stacked(south, own, north):
    return jnp.concatenate([south, own, north], axis=0)


def place(group, k, west, east, acc):
    to_west, to_east = acc
    to_west = jnp.where(group == k, pltpu.roll(west, 2 + TILE * k, 1), to_west)
    to_east = jnp.where(
        group == k, pltpu.roll(east, lax.rem(HALO + TILE * k, LANES), 1), to_east
    )
    return to_west, to_east


def pack_own(state, kmt, guess, strips):
    levels, rows_here, breadth = state.shape[1:]
    group = lane_of((rows_here, LANES)) // TILE
    ends = slice(0, LANES), slice(breadth - LANES, breadth)
    blank = (jnp.zeros((rows_here, LANES), F32),) * 2
    for field in range(3):

        def body(k, acc, field=field):
            west, east = [state[field, k, :, cols] for cols in ends]
            return place(group, k, west, east, acc)

        acc = lax.fori_loop(0, levels, body, blank, unroll=4)
        strips[0, field], strips[1, field] = acc
    acc = blank
    for number, own in enumerate((kmt[...].astype(F32), guess[...])):
        west, east = [own[:, cols] for cols in ends]
        acc = place(group, jnp.int32(number), west, east, acc)
    strips[0, 3], strips[1, 3] = acc


def pack_cols(strips, rows_odd, rows_even, msg_odd, msg_even):
    rows_here = strips.shape[2]
    tall = rows_here + 2 * TILE
    levels = (rows_even.shape[0] - 2) // 2
    breadth = rows_even.shape[2]
    lat_even = is_even("lat")
    lon_even = is_even("lon")
    group = lane_of((2 * TILE, LANES)) // TILE
    ends = slice(0, LANES), slice(breadth - LANES, breadth)
    blank = (jnp.zeros((2 * TILE, LANES), F32),) * 2

    def halos(slot):
        out = []
        for cols in ends:
            north, south = swap(lat_even, rows_even[slot, :, cols], rows_odd[slot, :, cols])
            out.append(jnp.concatenate([south, north], axis=0))
        return out

    def put(number, acc, field):
        base = number * tall
        to_west, to_east = (
            stacked(acc[i][:TILE], strips[i, field], acc[i][TILE:]) for i in range(2)
        )
        a, b = swap(lon_even, to_east, to_west)
        msg_even[base : base + tall] = a
        msg_odd[base : base + tall] = b

    flow_strips = []
    for field in range(2):

        def body(k, acc, field=field):
            return place(group, k, *halos(field * levels + k), acc)

        flow_strips.append(lax.fori_loop(0, levels, body, blank, unroll=4))
        put(field, flow_strips[field], field)
    acc = blank
    for number in range(2):
        acc = place(group, jnp.int32(number), *halos(2 * levels + number), acc)
    put(2, acc, 3)
    acc = [
        jnp.concatenate([turn(x[:TILE], -1, 0), turn(x[TILE:], 1, 0)], axis=0)
        for x in flow_strips[0]
    ]
    put(3, acc, 2)


def rotation_rows(tall, lanes, rows_here):
    total_rows = rows_here * lax.axis_size("lat")
    row = lax.broadcasted_iota(jnp.int32, (tall, lanes), 0)
    row = (row - TILE + lax.axis_index("lat") * rows_here).astype(F32)
    angle = jnp.pi / 180.0 * (-80.0 + 160.0 * (row + 0.5) / total_rows)
    return coriolis_scale * jnp.sin(angle)


def around(x):
    return east_of(x), west_of(x), north_of(x), south_of(x)


def count_wet(sides, level):
    total = None
    for side in sides:
        term = jnp.where(side > level, 1.0, 0.0)
        total = term if total is None else total + term
    return total


def spread(x, sides, count, coefficient, zonal, merid):
    east, west, north, south = sides
    laplace = east + west + north + south - count * x
    return (
        (time_step * coefficient) * laplace
        - zonal * (east - west)
        - merid * (north - south)
    )


carry = 0.5 * time_step * advection_scale


def advance_flow(u, v, wet, count, half_turn):
    zonal, merid = (carry * u, carry * v)
    new_u = u + (spread(u, around(u), count, viscosity, zonal, merid) + half_turn * v)
    new_v = v + (spread(v, around(v), count, viscosity, zonal, merid) - half_turn * u)
    return jnp.where(wet, new_u, 0.0), jnp.where(wet, new_v, 0.0)


def advance_inner(state, kmt, rows_odd, rows_even, flow, tracer, flow_u, flow_v, turning):
    levels, rows_here, breadth = state.shape[1:]
    tall = rows_here + 2 * TILE
    lat_even = is_even("lat")

    def halos(slot):
        north, south = swap(lat_even, rows_even[slot], rows_odd[slot])
        return south, north

    south, north = halos(2 * levels)
    depth = stacked(south, kmt[...].astype(F32), north)
    beside = around(depth)
    rotation = rotation_rows(tall, LANES, rows_here)
    turning[...] = rotation
    half_turn = time_step * rotation[:, :1]
    own = slice(TILE, TILE + rows_here)
    flow_u[...] = jnp.zeros_like(flow_u)
    flow_v[...] = jnp.zeros_like(flow_v)

    def body(k, _):
        level = k.astype(F32)
        wet = depth > level
        count = count_wet(beside, level)
        u_south, u_north = halos(k)
        v_south, v_north = halos(levels + k)
        u = jnp.where(wet, stacked(u_south, state[0, k], u_north), 0.0)
        v = jnp.where(wet, stacked(v_south, state[1, k], v_north), 0.0)
        new_u, new_v = advance_flow(u, v, wet, count, half_turn)
        flow_u[...] += new_u
        flow_v[...] += new_v
        flow[0, k] = new_u[own]
        flow[1, k] = new_v[own]
        here = state[2, k]
        stack_t = jnp.where(
            wet, stacked(turn(u_south, -1, 0), here, turn(u_north, 1, 0)), 0.0
        )
        middle = stack_t[own]
        sides = (east_of(middle), west_of(middle), north_of(stack_t)[own], south_of(stack_t)[own])
        change = spread(
            middle, sides, count[own], diffusivity, carry * u[own], carry * v[own]
        )
        above = state[2, jnp.maximum(k - 1, 0)]
        below = state[2, jnp.minimum(k + 1, levels - 1)]
        vertical = (above - here) + jnp.where(depth[own] > level + 1.0, below - here, 0.0)
        tracer[k] = jnp.where(
            wet[own], here + (change + (time_step * vertical_mix) * vertical), 0.0
        )
        return 0

    lax.fori_loop(0, levels, body, 0)


def fill_ends(x, west, east):
    lane = lane_of((x.shape[0], LANES))
    tiles = [x[:, i : i + LANES] for i in range(0, x.shape[1], LANES)]
    if west is not None:
        tiles[0] = jnp.where(lane == 0, west, tiles[0])
    if east is not None:
        tiles[-1] = jnp.where(lane == LANES - 1, east, tiles[-1])
    return jnp.concatenate(tiles, axis=1)


def roll_to(x, source, target, k):
    return turn(x, target - source - TILE * k, 1)


def over_groups(x):
    for step in (TILE, 2 * TILE, 4 * TILE, 8 * TILE):
        x = x + pltpu.roll(x, step, 1)
    return x


def krylov(
    sent_even, sent_odd, got_odd, got_even, flow_u, flow_v, kmt, guess,
    rows_even, rows_odd, turning, edges, basis, moments,
):
    levels = (rows_even.shape[0] - 2) // 2
    rows_here, breadth = kmt.shape
    tall = rows_here + 2 * TILE
    lat_even = is_even("lat")
    lon_even = is_even("lon")
    lane = lane_of((tall, LANES))
    place = lax.rem(lane, TILE)
    group = lane // TILE
    level = group.astype(F32)
    own = slice(TILE, TILE + rows_here)
    half_turn = time_step * turning[...]

    def strips(slot):
        rows = slice(slot * tall, (slot + 1) * tall)
        to_east, to_west = swap(lon_even, sent_even[rows], sent_odd[rows])
        from_east, from_west = swap(lon_even, got_even[rows], got_odd[rows])
        west = jnp.where(place < HALO, from_west, turn(to_west, 4, 1))
        east = jnp.where(place >= TILE - HALO, from_east, turn(to_east, -4, 1))
        return west, east

    u_sides, v_sides, other = [strips(slot) for slot in range(3)]
    t_sides = strips(3)
    sums = []
    for side in range(2):
        depth = over_groups(jnp.where(group == 0, other[side], 0.0))
        start = over_groups(jnp.where(group == 1, other[side], 0.0))
        wet = depth > level
        count = count_wet(around(depth), level)
        u = jnp.where(wet, u_sides[side], 0.0)
        v = jnp.where(wet, v_sides[side], 0.0)
        new_u, new_v = advance_flow(u, v, wet, count, half_turn)
        here = jnp.where(wet, t_sides[side], 0.0)
        change = spread(here, around(here), count, diffusivity, carry * u, carry * v)
        above = jnp.where(group > 0, turn(here, TILE, 1) - here, 0.0)
        below = jnp.where(depth > level + 1.0, turn(here, -TILE, 1) - here, 0.0)
        new_t = jnp.where(
            wet, here + (change + (time_step * vertical_mix) * (above + below)), 0.0
        )
        edges[side, 0] = new_u[own]
        edges[side, 1] = new_v[own]
        edges[side, 2] = new_t[own]
        sums.append((over_groups(new_u), over_groups(new_v), depth, start))

    def assemble(field, number, seam):
        west = turn(sums[0][number], 2, 1)
        east = turn(sums[1][number], -2, 1)
        halo = jnp.where(lane < LANES // 2, east, west)
        tiles = [field[:, i : i + LANES] for i in range(0, breadth, LANES)]
        if seam:
            tiles[0] = jnp.where(lane == 0, west, tiles[0])
            tiles[-1] = jnp.where(lane == LANES - 1, east, tiles[-1])
        return jnp.concatenate(tiles + [halo], axis=1)

    def tall_field(slot, value):
        north, south = swap(lat_even, rows_even[slot], rows_odd[slot])
        return stacked(south, value, north)

    wide_u = assemble(flow_u[...], 0, True)
    wide_v = assemble(flow_v[...], 1, True)
    wet_levels = assemble(tall_field(2 * levels, kmt[...].astype(F32)), 2, False)
    first = assemble(tall_field(2 * levels + 1, guess[...]), 3, False)

    divergence = 0.5 * (east_of(wide_u) - west_of(wide_u)) + 0.5 * (
        north_of(wide_v) - south_of(wide_v)
    )
    depth = wet_levels * (1.0 / levels)
    ocean = wet_levels > 0.0
    to_east = edge_weight * jnp.minimum(depth, east_of(depth))
    to_north = edge_weight * jnp.minimum(depth, north_of(depth))
    depth_north = north_of(depth)
    to_ne = corner_weight * jnp.minimum(depth, east_of(depth_north))
    to_nw = corner_weight * jnp.minimum(depth, west_of(depth_north))
    to_west = west_of(to_east)
    to_south = south_of(to_north)
    to_sw = south_of(west_of(to_ne))
    to_se = south_of(east_of(to_nw))
    diagonal = storage + (
        (to_east + to_west) + (to_north + to_south) + ((to_ne + to_nw) + (to_se + to_sw))
    )

    def neighbours(x):
        up, down = (north_of(x), south_of(x))
        eastern = to_east * x + to_ne_w * up + to_se_w * down
        western = to_west * x + to_nw_e * up + to_sw_e * down
        return to_north * up + to_south * down + (east_of(eastern) + west_of(western))

    to_ne_w = west_of(to_ne)
    to_se_w = west_of(to_se)
    to_nw_e = east_of(to_nw)
    to_sw_e = east_of(to_sw)
    to_east, to_west = (west_of(to_east), east_of(to_west))

    start = jnp.where(ocean, first, 0.0)
    rhs = jnp.where(ocean, storage * (start - time_step * divergence), 0.0)
    residual = rhs - (diagonal * start - neighbours(start))
    inverse = 1.0 / diagonal
    vectors = [residual * inverse]
    basis[0] = start
    basis[1] = vectors[0]
    for k in range(1, ITERS):
        vectors.append(neighbours(vectors[-1]) * inverse)
        basis[k + 1] = vectors[k]
    last = neighbours(vectors[-1])

    def inner(x):
        return x[own, :breadth]

    weighted = [inner(diagonal * x) for x in vectors] + [inner(last)]
    held = [inner(x) for x in vectors]
    slot = lane_of((1, LANES))
    total = jnp.zeros((1, LANES), F32)
    for m in range(2 * ITERS):
        product = held[m // 2] * weighted[(m + 1) // 2]
        total = jnp.where(slot == m, jnp.sum(product), total)
    moments[...] = total


def finish(shares, basis, edges, kmt, flow, tracer, out, pressure, done, sems):
    levels, rows_here, breadth = tracer.shape
    own = slice(TILE, TILE + rows_here)
    chunks = sems.shape[1]
    size = levels // chunks

    def send(first, last, c):
        part = pl.ds(c * size, size)
        fields = slice(first, last)
        return pltpu.make_async_copy(
            done.at[fields, part], out.at[fields, part], sems.at[first // 2, c]
        )

    def ended(value, field, k):
        return fill_ends(
            value,
            roll_to(edges[0, field], HALO, 0, k),
            roll_to(edges[1, field], 1, LANES - 1, k),
        )

    for c in range(chunks):
        for k in range(c * size, (c + 1) * size):
            done[2, k] = ended(tracer[k], 2, k)
        send(2, 3, c).start()
    sums = jnp.sum(shares[...], axis=0, keepdims=True)
    res = [sums[:, m : m + 1] for m in range(2 * ITERS)]
    dirn = list(res)
    one, zero = (jnp.ones((1, 1), F32), jnp.zeros((1, 1), F32))
    res_in = [one] + [zero] * (ITERS - 1)
    dir_in = list(res_in)
    height_in = [zero] * ITERS
    for k in range(ITERS):
        step = res[k] / (dirn[k] - dirn[k + 1])
        step = jnp.clip(step, 1.0 / HIGHEST, 1.0 / LOWEST)
        height_in = [h + step * d for h, d in zip(height_in, dir_in)]
        if k + 1 < ITERS:
            new = [res[m] - step * (dirn[m] - dirn[m + 1]) for m in range(len(dirn) - 1)]
            ratio = jnp.clip(step * new[k + 1] / res[k], 0.0, HIGHEST / LOWEST)
            dirn = [n + ratio * d for n, d in zip(new, dirn)]
            res = new
            moved = [zero] + dir_in[:-1]
            res_in = [r - step * (d - m) for r, d, m in zip(res_in, dir_in, moved)]
            dir_in = [r + ratio * d for r, d in zip(res_in, dir_in)]
    height = basis[0]
    for k in range(ITERS):
        height = height + height_in[k] * basis[k + 1]
    pressure[...] = gravity * height[own, :breadth]
    pull = 0.5 * time_step * gravity
    slope_east = pull * (east_of(height) - west_of(height))[own, :breadth]
    slope_north = pull * (north_of(height) - south_of(height))[own, :breadth]
    wet_levels = kmt[...]
    for c in range(chunks):
        for k in range(c * size, (c + 1) * size):
            wet = wet_levels > k
            for field, slope in ((0, slope_east), (1, slope_north)):
                done[field, k] = jnp.where(wet, ended(flow[field, k], field, k) - slope, 0.0)
        send(0, 2, c).start()
    for c in range(chunks):
        send(2, 3, c).wait()
        send(0, 2, c).wait()


def pairs(axis):
    peers = lax.axis_size(axis)
    even = [(i, i ^ 1) for i in range(peers)]
    odd = [(i, ((i + 1) ^ 1) - 1) for i in range(1, peers - 1)]
    if axis == "lon":
        odd += [(0, peers - 1), (peers - 1, 0)]
    return even, odd


def exchange(axis, to_even, to_odd):
    even, odd = pairs(axis)
    from_odd = lax.ppermute(to_odd, axis, odd)
    return lax.ppermute(to_even, axis, even), from_odd


def on_device(state, kmt, first_guess):
    _, levels, rows_here, breadth = state.shape
    tall = rows_here + 2 * TILE
    wide = breadth + LANES
    shape = lambda *dims: jax.ShapeDtypeStruct(dims, F32)

    devices = lax.axis_size("lon") * lax.axis_size("lat")
    slots = 2 * levels + 2
    hbm = pl.BlockSpec(memory_space=pltpu.HBM)
    vmem = pl.BlockSpec(memory_space=pltpu.VMEM)
    to_odd, to_even = pl.pallas_call(
        pack_rows,
        in_specs=[hbm] * 3,
        out_specs=[vmem] * 2,
        out_shape=[shape(slots, TILE, breadth)] * 2,
        scratch_shapes=[
            pltpu.VMEM((2, levels, TILE, breadth), F32),
            pltpu.VMEM((2, TILE, breadth), jnp.int32),
            pltpu.SemaphoreType.DMA((10,)),
        ],
        compiler_params=params(VMEM_FIRST),
    )(state, kmt, first_guess)
    rows_even, rows_odd = exchange("lat", to_even, to_odd)

    strips = pl.pallas_call(
        pack_own,
        out_shape=shape(2, 4, rows_here, LANES),
        compiler_params=params(),
        cost_estimate=cost(state.size),
    )(state, kmt, first_guess)
    length = 4 * tall
    sent_odd, sent_even = pl.pallas_call(
        pack_cols,
        out_shape=[shape(length, LANES)] * 2,
        compiler_params=params(),
    )(strips, rows_odd, rows_even)
    got_even, got_odd = exchange("lon", sent_even, sent_odd)

    flow, tracer, flow_u, flow_v, turning = pl.pallas_call(
        advance_inner,
        out_shape=[
            shape(2, levels, rows_here, breadth),
            shape(levels, rows_here, breadth),
            shape(tall, breadth),
            shape(tall, breadth),
            shape(tall, LANES),
        ],
        compiler_params=params(),
        cost_estimate=cost(state.size),
    )(state, kmt, rows_odd, rows_even)

    edges, basis, moments = pl.pallas_call(
        krylov,
        out_shape=[
            shape(2, 3, rows_here, LANES),
            shape(ITERS + 1, tall, wide),
            shape(1, LANES),
        ],
        compiler_params=params(),
    )(
        sent_even, sent_odd, got_odd, got_even, flow_u, flow_v, kmt, first_guess,
        rows_even, rows_odd, turning,
    )

    shares = jnp.broadcast_to(moments[None], (devices, 1, LANES))
    shares = lax.all_to_all(shares, ("lon", "lat"), 0, 0)
    return pl.pallas_call(
        finish,
        in_specs=[vmem] * 6,
        out_specs=[hbm, vmem],
        out_shape=[shape(3, levels, rows_here, breadth), shape(rows_here, breadth)],
        scratch_shapes=[
            pltpu.VMEM((3, levels, rows_here, breadth), F32),
            pltpu.SemaphoreType.DMA((2, 4)),
        ],
        compiler_params=params(),
    )(shares.reshape(devices, LANES), basis, edges, kmt, flow, tracer)


def solution(mesh):
    placed = (P(None, None, "lat", "lon"), P("lat", "lon"), P("lat", "lon"))
    return jax.shard_map(
        on_device,
        mesh=mesh,
        in_specs=placed,
        out_specs=(P(None, None, "lat", "lon"), P("lat", "lon")),
        check_vma=False,
    )
```

```python
import jax
import jax.numpy as jnp
from jax import lax
from jax.experimental import pallas as pl
from jax.experimental.pallas import tpu as pltpu
from jax.sharding import PartitionSpec as P

ITERS = 4
F32 = jnp.float32

viscosity = 0.12
diffusivity = 0.1
advection_scale = 0.5
vertical_mix = 0.2
coriolis_scale = 0.6
time_step = 0.5
storage = 0.5
gravity = 1.5
edge_weight = 2.0 / 3.0
corner_weight = 1.0 / 6.0

TILE = 8
LANES = 128
LEVELS = LANES // TILE
HALO = 6

U_ROWS = 0
V_ROWS = U_ROWS + LEVELS // 4
T_ROWS = V_ROWS + LEVELS // 4
KMT, GUESS, SUM_U, SUM_V, STRIPS = range(T_ROWS + LEVELS // 8, T_ROWS + LEVELS // 8 + 5)
SLOTS = STRIPS + 3

LOWEST = storage / (storage + 4 * edge_weight + 4 * corner_weight)
HIGHEST = 2.0 - LOWEST
VMEM_LIMIT = 16 * 1024 * 1024
VMEM_FIRST = 64520000


def params(limit=VMEM_LIMIT):
    return pltpu.CompilerParams(vmem_limit_bytes=limit)


def cost(size):
    return pl.CostEstimate(flops=60 * size, bytes_accessed=8 * size, transcendentals=0)


def turn(x, shift, axis):
    return pltpu.roll(x, shift % x.shape[axis], axis)


def east_of(x):
    return turn(x, -1, 1)


def west_of(x):
    return turn(x, 1, 1)


def north_of(x):
    return turn(x, -1, 0)


def south_of(x):
    return turn(x, 1, 0)


def lane_of(shape):
    return lax.broadcasted_iota(jnp.int32, shape, len(shape) - 1)


def is_even(axis):
    return lax.rem(lax.axis_index(axis), 2) == 0


def swap(first, a, b):
    return jnp.where(first, a, b), jnp.where(first, b, a)


def stacked(south, own, north):
    return jnp.concatenate([south, own, north], axis=0)


def place(group, k, west, east, acc):
    to_west, to_east = acc
    to_west = jnp.where(group == k, pltpu.roll(west, 2 + TILE * k, 1), to_west)
    to_east = jnp.where(
        group == k, pltpu.roll(east, lax.rem(HALO + TILE * k, LANES), 1), to_east
    )
    return to_west, to_east


def pack_own(state, kmt, guess, strips):
    levels, rows_here, breadth = state.shape[1:]
    group = lane_of((rows_here, LANES)) // TILE
    ends = slice(0, LANES), slice(breadth - LANES, breadth)
    blank = (jnp.zeros((rows_here, LANES), F32),) * 2
    for field in range(3):

        def body(k, acc, field=field):
            west, east = [state[field, k, :, cols] for cols in ends]
            return place(group, k, west, east, acc)

        acc = lax.fori_loop(0, levels, body, blank, unroll=4)
        strips[0, field], strips[1, field] = acc
    acc = blank
    for number, own in enumerate((kmt[...].astype(F32), guess[...])):
        west, east = [own[:, cols] for cols in ends]
        acc = place(group, jnp.int32(number), west, east, acc)
    strips[0, 3], strips[1, 3] = acc


def pack_cols(strips, rows_odd, rows_even, msg_odd, msg_even):
    tall = strips.shape[2] + 2 * TILE
    lat_even = is_even("lat")
    lon_even = is_even("lon")

    def put(number, field, south, north):
        base = number * tall
        to_west, to_east = (
            stacked(
                south[:, i * LANES : (i + 1) * LANES],
                strips[i, field],
                north[:, i * LANES : (i + 1) * LANES],
            )
            for i in range(2)
        )
        a, b = swap(lon_even, to_east, to_west)
        msg_even[base : base + tall] = a
        msg_odd[base : base + tall] = b

    halos = []
    for slot in range(STRIPS, SLOTS):
        north, south = swap(lat_even, rows_even[slot], rows_odd[slot])
        halos.append((south, north))
    put(0, 0, *halos[0])
    put(1, 1, *halos[1])
    put(2, 3, *halos[2])
    put(3, 2, turn(halos[0][0], -1, 0), turn(halos[0][1], 1, 0))


def rotation_at(row, rows_here):
    total_rows = rows_here * lax.axis_size("lat")
    row = (row + lax.axis_index("lat") * rows_here).astype(F32)
    angle = jnp.pi / 180.0 * (-80.0 + 160.0 * (row + 0.5) / total_rows)
    return coriolis_scale * jnp.sin(angle)


def around(x):
    return east_of(x), west_of(x), north_of(x), south_of(x)


def count_wet(sides, level):
    total = None
    for side in sides:
        term = jnp.where(side > level, 1.0, 0.0)
        total = term if total is None else total + term
    return total


def spread(x, sides, count, coefficient, zonal, merid):
    east, west, north, south = sides
    laplace = east + west + north + south - count * x
    return (
        (time_step * coefficient) * laplace
        - zonal * (east - west)
        - merid * (north - south)
    )


carry = 0.5 * time_step * advection_scale


def advance_flow(u, v, wet, count, half_turn):
    zonal, merid = (carry * u, carry * v)
    new_u = u + (spread(u, around(u), count, viscosity, zonal, merid) + half_turn * v)
    new_v = v + (spread(v, around(v), count, viscosity, zonal, merid) - half_turn * u)
    return jnp.where(wet, new_u, 0.0), jnp.where(wet, new_v, 0.0)


def pack_rows(state, kmt, guess, msg_odd, msg_even, ends, wet_ends, guess_ends, sems):
    levels, rows_here, breadth = state.shape[1:]
    even = is_even("lat")
    copies = []
    for number, rows in enumerate((slice(0, TILE), slice(rows_here - TILE, rows_here))):
        held = slice(number * TILE, (number + 1) * TILE)
        for source, target in (
            (state.at[:, :, rows, :], ends.at[:, :, held, :]),
            (kmt.at[rows, :], wet_ends.at[held, :]),
            (guess.at[rows, :], guess_ends.at[held, :]),
        ):
            copies.append(pltpu.make_async_copy(source, target, sems.at[len(copies)]))
            copies[-1].start()
    row = lax.broadcasted_iota(jnp.int32, (2 * TILE, LANES), 0)
    rotation = rotation_at(jnp.where(row < TILE, row, row + rows_here - 2 * TILE), rows_here)
    half_turn = time_step * rotation[:, :1]
    group = lane_of((2 * TILE, LANES)) // TILE
    row = lax.broadcasted_iota(jnp.int32, (2 * TILE, breadth), 0)
    borrowed = (row == TILE - 1) | (row == TILE)
    for item in copies:
        item.wait()

    depth = wet_ends[...].astype(F32)
    beside = around(depth)
    cut = slice(0, LANES), slice(breadth - LANES, breadth)

    def body(k, carried):
        sum_u, sum_v, strips_u, strips_v = carried
        level = k.astype(F32)
        wet = depth > level
        raw_u, raw_v, raw_t = [ends[field, k] for field in range(3)]
        u = jnp.where(wet, raw_u, 0.0)
        v = jnp.where(wet, raw_v, 0.0)
        new_u, new_v = advance_flow(u, v, wet, count_wet(beside, level), half_turn)
        moved = jnp.concatenate([turn(raw_t[:TILE], -1, 0), turn(raw_t[TILE:], 1, 0)], axis=0)
        lent = jnp.where(borrowed, moved, raw_u)
        strips_u = place(group, k, lent[:, cut[0]], lent[:, cut[1]], strips_u)
        strips_v = place(group, k, raw_v[:, cut[0]], raw_v[:, cut[1]], strips_v)
        return sum_u + new_u, sum_v + new_v, strips_u, strips_v

    empty = jnp.zeros((2 * TILE, breadth), F32)
    blank = (jnp.zeros((2 * TILE, LANES), F32),) * 2
    sum_u, sum_v, strips_u, strips_v = lax.fori_loop(
        0, levels, body, (empty, empty, blank, blank), unroll=2
    )
    starts = guess_ends[...]
    others = blank
    for number, value in enumerate((depth, starts)):
        others = place(group, jnp.int32(number), value[:, cut[0]], value[:, cut[1]], others)

    def put(slot, low, high):
        a, b = swap(even, high, low)
        msg_even[slot] = a
        msg_odd[slot] = b

    whole = [depth, starts, sum_u, sum_v]
    whole += [jnp.concatenate(pair, axis=1) for pair in (strips_u, strips_v, others)]
    for slot, value in enumerate(whole, KMT):
        put(slot, value[:TILE], value[TILE:])
    row = lax.broadcasted_iota(jnp.int32, (TILE, breadth), 0)
    for field, first, width in ((0, U_ROWS, 2), (1, V_ROWS, 2), (2, T_ROWS, 1)):
        each = TILE // width
        for tile in range(levels // each):
            low = high = jnp.zeros((TILE, breadth), F32)
            for q in range(each):
                value = ends[field, tile * each + q]
                here = row // width == q
                low = jnp.where(here, turn(value[:TILE], width * q, 0), low)
                high = jnp.where(here, turn(value[TILE:], width * (q + 1), 0), high)
            put(first + tile, low, high)


def halo_rows(rows_even, rows_odd, first, width, k):
    each = TILE // width
    tile = first + k // each
    north, south = swap(is_even("lat"), rows_even[tile], rows_odd[tile])
    at = lax.rem(k, each) * width
    south = pltpu.roll(south, lax.rem(2 * TILE - width - at, TILE), 0)
    north = pltpu.roll(north, lax.rem(TILE - at, TILE), 0)
    return south, north


def advance_inner(state, kmt, rows_odd, rows_even, flow, tracer, flow_u, flow_v, turning):
    levels, rows_here, breadth = state.shape[1:]
    tall = rows_here + 2 * TILE
    lat_even = is_even("lat")

    def halos(slot):
        north, south = swap(lat_even, rows_even[slot], rows_odd[slot])
        return south, north

    south, north = halos(KMT)
    depth = stacked(south, kmt[...].astype(F32), north)
    beside = around(depth)
    row = lax.broadcasted_iota(jnp.int32, (tall, LANES), 0)
    rotation = rotation_at(row - TILE, rows_here)
    turning[...] = rotation
    half_turn = time_step * rotation[:, :1]
    own = slice(TILE, TILE + rows_here)
    flow_u[...] = jnp.zeros_like(flow_u)
    flow_v[...] = jnp.zeros_like(flow_v)

    def body(k, _):
        level = k.astype(F32)
        wet = depth > level
        count = count_wet(beside, level)
        u_south, u_north = halo_rows(rows_even, rows_odd, U_ROWS, 2, k)
        v_south, v_north = halo_rows(rows_even, rows_odd, V_ROWS, 2, k)
        t_south, t_north = halo_rows(rows_even, rows_odd, T_ROWS, 1, k)
        u = jnp.where(wet, stacked(u_south, state[0, k], u_north), 0.0)
        v = jnp.where(wet, stacked(v_south, state[1, k], v_north), 0.0)
        new_u, new_v = advance_flow(u, v, wet, count, half_turn)
        flow_u[...] += new_u
        flow_v[...] += new_v
        flow[0, k] = new_u[own]
        flow[1, k] = new_v[own]
        here = state[2, k]
        stack_t = jnp.where(wet, stacked(t_south, here, t_north), 0.0)
        middle = stack_t[own]
        sides = (east_of(middle), west_of(middle), north_of(stack_t)[own], south_of(stack_t)[own])
        change = spread(
            middle, sides, count[own], diffusivity, carry * u[own], carry * v[own]
        )
        above = state[2, jnp.maximum(k - 1, 0)]
        below = state[2, jnp.minimum(k + 1, levels - 1)]
        vertical = (above - here) + jnp.where(depth[own] > level + 1.0, below - here, 0.0)
        tracer[k] = jnp.where(
            wet[own], here + (change + (time_step * vertical_mix) * vertical), 0.0
        )
        return 0

    lax.fori_loop(0, levels, body, 0)
    row = lax.broadcasted_iota(jnp.int32, (tall, breadth), 0)
    outer = (row < TILE - 1) | (row > TILE + rows_here)
    inner = jnp.zeros((rows_here, breadth), F32)
    for slot, flow_sum in ((SUM_U, flow_u), (SUM_V, flow_v)):
        south, north = halos(slot)
        flow_sum[...] = jnp.where(outer, stacked(south, inner, north), flow_sum[...])


def fill_ends(x, west, east):
    lane = lane_of((x.shape[0], LANES))
    tiles = [x[:, i : i + LANES] for i in range(0, x.shape[1], LANES)]
    if west is not None:
        tiles[0] = jnp.where(lane == 0, west, tiles[0])
    if east is not None:
        tiles[-1] = jnp.where(lane == LANES - 1, east, tiles[-1])
    return jnp.concatenate(tiles, axis=1)


def roll_to(x, source, target, k):
    return turn(x, target - source - TILE * k, 1)


def over_groups(x):
    for step in (TILE, 2 * TILE, 4 * TILE, 8 * TILE):
        x = x + pltpu.roll(x, step, 1)
    return x


def krylov(
    sent_even, sent_odd, got_odd, got_even, flow_u, flow_v, kmt, guess,
    rows_even, rows_odd, turning, edges, basis, moments,
):
    levels = LEVELS
    rows_here, breadth = kmt.shape
    tall = rows_here + 2 * TILE
    lat_even = is_even("lat")
    lon_even = is_even("lon")
    lane = lane_of((tall, LANES))
    place = lax.rem(lane, TILE)
    group = lane // TILE
    level = group.astype(F32)
    own = slice(TILE, TILE + rows_here)
    half_turn = time_step * turning[...]

    def strips(slot):
        rows = slice(slot * tall, (slot + 1) * tall)
        to_east, to_west = swap(lon_even, sent_even[rows], sent_odd[rows])
        from_east, from_west = swap(lon_even, got_even[rows], got_odd[rows])
        west = jnp.where(place < HALO, from_west, turn(to_west, 4, 1))
        east = jnp.where(place >= TILE - HALO, from_east, turn(to_east, -4, 1))
        return west, east

    u_sides, v_sides, other = [strips(slot) for slot in range(3)]
    t_sides = strips(3)
    sums = []
    for side in range(2):
        depth = over_groups(jnp.where(group == 0, other[side], 0.0))
        start = over_groups(jnp.where(group == 1, other[side], 0.0))
        wet = depth > level
        count = count_wet(around(depth), level)
        u = jnp.where(wet, u_sides[side], 0.0)
        v = jnp.where(wet, v_sides[side], 0.0)
        new_u, new_v = advance_flow(u, v, wet, count, half_turn)
        here = jnp.where(wet, t_sides[side], 0.0)
        change = spread(here, around(here), count, diffusivity, carry * u, carry * v)
        above = jnp.where(group > 0, turn(here, TILE, 1) - here, 0.0)
        below = jnp.where(depth > level + 1.0, turn(here, -TILE, 1) - here, 0.0)
        new_t = jnp.where(
            wet, here + (change + (time_step * vertical_mix) * (above + below)), 0.0
        )
        edges[side, 0] = new_u[own]
        edges[side, 1] = new_v[own]
        edges[side, 2] = new_t[own]
        sums.append((over_groups(new_u), over_groups(new_v), depth, start))

    def assemble(field, number, seam):
        west = turn(sums[0][number], 2, 1)
        east = turn(sums[1][number], -2, 1)
        halo = jnp.where(lane < LANES // 2, east, west)
        tiles = [field[:, i : i + LANES] for i in range(0, breadth, LANES)]
        if seam:
            tiles[0] = jnp.where(lane == 0, west, tiles[0])
            tiles[-1] = jnp.where(lane == LANES - 1, east, tiles[-1])
        return jnp.concatenate(tiles + [halo], axis=1)

    def tall_field(slot, value):
        north, south = swap(lat_even, rows_even[slot], rows_odd[slot])
        return stacked(south, value, north)

    wide_u = assemble(flow_u[...], 0, True)
    wide_v = assemble(flow_v[...], 1, True)
    wet_levels = assemble(tall_field(KMT, kmt[...].astype(F32)), 2, False)
    first = assemble(tall_field(GUESS, guess[...]), 3, False)

    divergence = 0.5 * (east_of(wide_u) - west_of(wide_u)) + 0.5 * (
        north_of(wide_v) - south_of(wide_v)
    )
    depth = wet_levels * (1.0 / levels)
    ocean = wet_levels > 0.0
    to_east = edge_weight * jnp.minimum(depth, east_of(depth))
    to_north = edge_weight * jnp.minimum(depth, north_of(depth))
    depth_north = north_of(depth)
    to_ne = corner_weight * jnp.minimum(depth, east_of(depth_north))
    to_nw = corner_weight * jnp.minimum(depth, west_of(depth_north))
    to_west = west_of(to_east)
    to_south = south_of(to_north)
    to_sw = south_of(west_of(to_ne))
    to_se = south_of(east_of(to_nw))
    diagonal = storage + (
        (to_east + to_west) + (to_north + to_south) + ((to_ne + to_nw) + (to_se + to_sw))
    )

    def neighbours(x):
        up, down = (north_of(x), south_of(x))
        eastern = to_east * x + to_ne_w * up + to_se_w * down
        western = to_west * x + to_nw_e * up + to_sw_e * down
        return to_north * up + to_south * down + (east_of(eastern) + west_of(western))

    to_ne_w = west_of(to_ne)
    to_se_w = west_of(to_se)
    to_nw_e = east_of(to_nw)
    to_sw_e = east_of(to_sw)
    to_east, to_west = (west_of(to_east), east_of(to_west))

    start = jnp.where(ocean, first, 0.0)
    rhs = jnp.where(ocean, storage * (start - time_step * divergence), 0.0)
    residual = rhs - (diagonal * start - neighbours(start))
    inverse = 1.0 / diagonal
    vectors = [residual * inverse]
    basis[0] = start
    basis[1] = vectors[0]
    for k in range(1, ITERS):
        vectors.append(neighbours(vectors[-1]) * inverse)
        basis[k + 1] = vectors[k]
    last = neighbours(vectors[-1])

    def inner(x):
        return x[own, :breadth]

    weighted = [inner(diagonal * x) for x in vectors] + [inner(last)]
    held = [inner(x) for x in vectors]
    slot = lane_of((1, LANES))
    total = jnp.zeros((1, LANES), F32)
    for m in range(2 * ITERS):
        product = held[m // 2] * weighted[(m + 1) // 2]
        total = jnp.where(slot == m, jnp.sum(product), total)
    moments[...] = total


def finish(shares, basis, edges, kmt, flow, tracer, out, pressure, done, sems):
    levels, rows_here, breadth = tracer.shape
    own = slice(TILE, TILE + rows_here)
    chunks = sems.shape[1]
    size = levels // chunks

    def send(first, last, c):
        part = pl.ds(c * size, size)
        fields = slice(first, last)
        return pltpu.make_async_copy(
            done.at[fields, part], out.at[fields, part], sems.at[first // 2, c]
        )

    def ended(value, field, k):
        return fill_ends(
            value,
            roll_to(edges[0, field], HALO, 0, k),
            roll_to(edges[1, field], 1, LANES - 1, k),
        )

    for c in range(chunks):
        for k in range(c * size, (c + 1) * size):
            done[2, k] = ended(tracer[k], 2, k)
        send(2, 3, c).start()
    sums = jnp.sum(shares[...], axis=0, keepdims=True)
    res = [sums[:, m : m + 1] for m in range(2 * ITERS)]
    dirn = list(res)
    one, zero = (jnp.ones((1, 1), F32), jnp.zeros((1, 1), F32))
    res_in = [one] + [zero] * (ITERS - 1)
    dir_in = list(res_in)
    height_in = [zero] * ITERS
    for k in range(ITERS):
        step = res[k] / (dirn[k] - dirn[k + 1])
        step = jnp.clip(step, 1.0 / HIGHEST, 1.0 / LOWEST)
        height_in = [h + step * d for h, d in zip(height_in, dir_in)]
        if k + 1 < ITERS:
            new = [res[m] - step * (dirn[m] - dirn[m + 1]) for m in range(len(dirn) - 1)]
            ratio = jnp.clip(step * new[k + 1] / res[k], 0.0, HIGHEST / LOWEST)
            dirn = [n + ratio * d for n, d in zip(new, dirn)]
            res = new
            moved = [zero] + dir_in[:-1]
            res_in = [r - step * (d - m) for r, d, m in zip(res_in, dir_in, moved)]
            dir_in = [r + ratio * d for r, d in zip(res_in, dir_in)]
    height = basis[0]
    for k in range(ITERS):
        height = height + height_in[k] * basis[k + 1]
    pressure[...] = gravity * height[own, :breadth]
    pull = 0.5 * time_step * gravity
    slope_east = pull * (east_of(height) - west_of(height))[own, :breadth]
    slope_north = pull * (north_of(height) - south_of(height))[own, :breadth]
    wet_levels = kmt[...]
    for c in range(chunks):
        for k in range(c * size, (c + 1) * size):
            wet = wet_levels > k
            for field, slope in ((0, slope_east), (1, slope_north)):
                done[field, k] = jnp.where(wet, ended(flow[field, k], field, k) - slope, 0.0)
        send(0, 2, c).start()
    for c in range(chunks):
        send(2, 3, c).wait()
        send(0, 2, c).wait()


def pairs(axis):
    peers = lax.axis_size(axis)
    even = [(i, i ^ 1) for i in range(peers)]
    odd = [(i, ((i + 1) ^ 1) - 1) for i in range(1, peers - 1)]
    if axis == "lon":
        odd += [(0, peers - 1), (peers - 1, 0)]
    return even, odd


def exchange(axis, to_even, to_odd):
    even, odd = pairs(axis)
    from_odd = lax.ppermute(to_odd, axis, odd)
    return lax.ppermute(to_even, axis, even), from_odd


def on_device(state, kmt, first_guess):
    _, levels, rows_here, breadth = state.shape
    tall = rows_here + 2 * TILE
    wide = breadth + LANES
    shape = lambda *dims: jax.ShapeDtypeStruct(dims, F32)

    devices = lax.axis_size("lon") * lax.axis_size("lat")
    hbm = pl.BlockSpec(memory_space=pltpu.HBM)
    vmem = pl.BlockSpec(memory_space=pltpu.VMEM)
    to_odd, to_even = pl.pallas_call(
        pack_rows,
        in_specs=[hbm] * 3,
        out_specs=[vmem] * 2,
        out_shape=[shape(SLOTS, TILE, breadth)] * 2,
        scratch_shapes=[
            pltpu.VMEM((3, levels, 2 * TILE, breadth), F32),
            pltpu.VMEM((2 * TILE, breadth), jnp.int32),
            pltpu.VMEM((2 * TILE, breadth), F32),
            pltpu.SemaphoreType.DMA((6,)),
        ],
        compiler_params=params(VMEM_FIRST),
    )(state, kmt, first_guess)
    rows_even, rows_odd = exchange("lat", to_even, to_odd)

    strips = pl.pallas_call(
        pack_own,
        out_shape=shape(2, 4, rows_here, LANES),
        compiler_params=params(),
        cost_estimate=cost(state.size),
    )(state, kmt, first_guess)
    length = 4 * tall
    sent_odd, sent_even = pl.pallas_call(
        pack_cols,
        out_shape=[shape(length, LANES)] * 2,
        compiler_params=params(),
    )(strips, rows_odd, rows_even)
    got_even, got_odd = exchange("lon", sent_even, sent_odd)

    flow, tracer, flow_u, flow_v, turning = pl.pallas_call(
        advance_inner,
        out_shape=[
            shape(2, levels, rows_here, breadth),
            shape(levels, rows_here, breadth),
            shape(tall, breadth),
            shape(tall, breadth),
            shape(tall, LANES),
        ],
        compiler_params=params(),
        cost_estimate=cost(state.size),
    )(state, kmt, rows_odd, rows_even)

    edges, basis, moments = pl.pallas_call(
        krylov,
        out_shape=[
            shape(2, 3, rows_here, LANES),
            shape(ITERS + 1, tall, wide),
            shape(1, LANES),
        ],
        compiler_params=params(),
    )(
        sent_even, sent_odd, got_odd, got_even, flow_u, flow_v, kmt, first_guess,
        rows_even, rows_odd, turning,
    )

    shares = jnp.broadcast_to(moments[None], (devices, 1, LANES))
    shares = lax.all_to_all(shares, ("lon", "lat"), 0, 0)
    return pl.pallas_call(
        finish,
        in_specs=[vmem] * 6,
        out_specs=[hbm, vmem],
        out_shape=[shape(3, levels, rows_here, breadth), shape(rows_here, breadth)],
        scratch_shapes=[
            pltpu.VMEM((3, levels, rows_here, breadth), F32),
            pltpu.SemaphoreType.DMA((2, 4)),
        ],
        compiler_params=params(),
    )(shares.reshape(devices, LANES), basis, edges, kmt, flow, tracer)


def solution(mesh):
    placed = (P(None, None, "lat", "lon"), P("lat", "lon"), P("lat", "lon"))
    return jax.shard_map(
        on_device,
        mesh=mesh,
        in_specs=placed,
        out_specs=(P(None, None, "lat", "lon"), P("lat", "lon")),
        check_vma=False,
    )
```

```python
import jax
import jax.numpy as jnp
from jax import lax
from jax.experimental import pallas as pl
from jax.experimental.pallas import tpu as pltpu
from jax.sharding import PartitionSpec as P

ITERS = 4
F32 = jnp.float32

viscosity = 0.12
diffusivity = 0.1
advection_scale = 0.5
vertical_mix = 0.2
coriolis_scale = 0.6
time_step = 0.5
storage = 0.5
gravity = 1.5
edge_weight = 2.0 / 3.0
corner_weight = 1.0 / 6.0

TILE = 8
LANES = 128
LEVELS = LANES // TILE
HALO = 6

U_ROWS = 0
V_ROWS = U_ROWS + LEVELS // 4
T_ROWS = V_ROWS + LEVELS // 4
KMT, GUESS, SUM_U, SUM_V, STRIPS = range(T_ROWS + LEVELS // 8, T_ROWS + LEVELS // 8 + 5)
SLOTS = STRIPS + 3

LOWEST = storage / (storage + 4 * edge_weight + 4 * corner_weight)
HIGHEST = 2.0 - LOWEST
VMEM_LIMIT = 16 * 1024 * 1024
VMEM_FIRST = 64520000


def params(limit=VMEM_LIMIT):
    return pltpu.CompilerParams(vmem_limit_bytes=limit)


def cost(size):
    return pl.CostEstimate(flops=60 * size, bytes_accessed=8 * size, transcendentals=0)


def turn(x, shift, axis):
    return pltpu.roll(x, shift % x.shape[axis], axis)


def east_of(x):
    return turn(x, -1, 1)


def west_of(x):
    return turn(x, 1, 1)


def north_of(x):
    return turn(x, -1, 0)


def south_of(x):
    return turn(x, 1, 0)


def lane_of(shape):
    return lax.broadcasted_iota(jnp.int32, shape, len(shape) - 1)


def is_even(axis):
    return lax.rem(lax.axis_index(axis), 2) == 0


def swap(first, a, b):
    return jnp.where(first, a, b), jnp.where(first, b, a)


def stacked(south, own, north):
    return jnp.concatenate([south, own, north], axis=0)


def place(group, k, west, east, acc):
    to_west, to_east = acc
    to_west = jnp.where(group == k, pltpu.roll(west, 2 + TILE * k, 1), to_west)
    to_east = jnp.where(
        group == k, pltpu.roll(east, lax.rem(HALO + TILE * k, LANES), 1), to_east
    )
    return to_west, to_east


def pack_own(state, kmt, guess, strips):
    levels, rows_here, breadth = state.shape[1:]
    group = lane_of((rows_here, LANES)) // TILE
    ends = slice(0, LANES), slice(breadth - LANES, breadth)
    blank = (jnp.zeros((rows_here, LANES), F32),) * 2
    for field in range(3):

        def body(k, acc, field=field):
            west, east = [state[field, k, :, cols] for cols in ends]
            return place(group, k, west, east, acc)

        acc = lax.fori_loop(0, levels, body, blank, unroll=4)
        strips[0, field], strips[1, field] = acc
    acc = blank
    for number, own in enumerate((kmt[...].astype(F32), guess[...])):
        west, east = [own[:, cols] for cols in ends]
        acc = place(group, jnp.int32(number), west, east, acc)
    strips[0, 3], strips[1, 3] = acc


def pack_cols(strips, rows_odd, rows_even, msg_odd, msg_even):
    tall = strips.shape[2] + 2 * TILE
    lat_even = is_even("lat")
    lon_even = is_even("lon")

    def put(number, field, south, north):
        base = number * tall
        to_west, to_east = (
            stacked(
                south[:, i * LANES : (i + 1) * LANES],
                strips[i, field],
                north[:, i * LANES : (i + 1) * LANES],
            )
            for i in range(2)
        )
        a, b = swap(lon_even, to_east, to_west)
        msg_even[base : base + tall] = a
        msg_odd[base : base + tall] = b

    halos = []
    for slot in range(STRIPS, SLOTS):
        north, south = swap(lat_even, rows_even[slot], rows_odd[slot])
        halos.append((south, north))
    put(0, 0, *halos[0])
    put(1, 1, *halos[1])
    put(2, 3, *halos[2])
    put(3, 2, turn(halos[0][0], -1, 0), turn(halos[0][1], 1, 0))


def rotation_at(row, rows_here):
    total_rows = rows_here * lax.axis_size("lat")
    row = (row + lax.axis_index("lat") * rows_here).astype(F32)
    angle = jnp.pi / 180.0 * (-80.0 + 160.0 * (row + 0.5) / total_rows)
    return coriolis_scale * jnp.sin(angle)


def around(x):
    return east_of(x), west_of(x), north_of(x), south_of(x)


def count_wet(sides, level):
    total = None
    for side in sides:
        term = jnp.where(side > level, 1.0, 0.0)
        total = term if total is None else total + term
    return total


def spread(x, sides, count, coefficient, zonal, merid):
    east, west, north, south = sides
    laplace = east + west + north + south - count * x
    return (
        (time_step * coefficient) * laplace
        - zonal * (east - west)
        - merid * (north - south)
    )


carry = 0.5 * time_step * advection_scale


def advance_flow(u, v, wet, count, half_turn):
    zonal, merid = (carry * u, carry * v)
    new_u = u + (spread(u, around(u), count, viscosity, zonal, merid) + half_turn * v)
    new_v = v + (spread(v, around(v), count, viscosity, zonal, merid) - half_turn * u)
    return jnp.where(wet, new_u, 0.0), jnp.where(wet, new_v, 0.0)


def pack_rows(state, kmt, guess, msg_odd, msg_even, ends, wet_ends, guess_ends, sems):
    levels, rows_here, breadth = state.shape[1:]
    even = is_even("lat")
    copies = []
    for number, rows in enumerate((slice(0, TILE), slice(rows_here - TILE, rows_here))):
        held = slice(number * TILE, (number + 1) * TILE)
        for source, target in (
            (state.at[:, :, rows, :], ends.at[:, :, held, :]),
            (kmt.at[rows, :], wet_ends.at[held, :]),
            (guess.at[rows, :], guess_ends.at[held, :]),
        ):
            copies.append(pltpu.make_async_copy(source, target, sems.at[len(copies)]))
            copies[-1].start()
    row = lax.broadcasted_iota(jnp.int32, (2 * TILE, LANES), 0)
    rotation = rotation_at(jnp.where(row < TILE, row, row + rows_here - 2 * TILE), rows_here)
    half_turn = time_step * rotation[:, :1]
    group = lane_of((2 * TILE, LANES)) // TILE
    row = lax.broadcasted_iota(jnp.int32, (2 * TILE, breadth), 0)
    borrowed = (row == TILE - 1) | (row == TILE)
    for item in copies:
        item.wait()

    depth = wet_ends[...].astype(F32)
    beside = around(depth)
    cut = slice(0, LANES), slice(breadth - LANES, breadth)

    def body(k, carried):
        sum_u, sum_v, strips_u, strips_v = carried
        level = k.astype(F32)
        wet = depth > level
        raw_u, raw_v, raw_t = [ends[field, k] for field in range(3)]
        u = jnp.where(wet, raw_u, 0.0)
        v = jnp.where(wet, raw_v, 0.0)
        new_u, new_v = advance_flow(u, v, wet, count_wet(beside, level), half_turn)
        moved = jnp.concatenate([turn(raw_t[:TILE], -1, 0), turn(raw_t[TILE:], 1, 0)], axis=0)
        lent = jnp.where(borrowed, moved, raw_u)
        strips_u = place(group, k, lent[:, cut[0]], lent[:, cut[1]], strips_u)
        strips_v = place(group, k, raw_v[:, cut[0]], raw_v[:, cut[1]], strips_v)
        return sum_u + new_u, sum_v + new_v, strips_u, strips_v

    empty = jnp.zeros((2 * TILE, breadth), F32)
    blank = (jnp.zeros((2 * TILE, LANES), F32),) * 2
    sum_u, sum_v, strips_u, strips_v = lax.fori_loop(
        0, levels, body, (empty, empty, blank, blank), unroll=4
    )
    starts = guess_ends[...]
    others = blank
    for number, value in enumerate((depth, starts)):
        others = place(group, jnp.int32(number), value[:, cut[0]], value[:, cut[1]], others)

    def put(slot, low, high):
        a, b = swap(even, high, low)
        msg_even[slot] = a
        msg_odd[slot] = b

    whole = [depth, starts, sum_u, sum_v]
    whole += [jnp.concatenate(pair, axis=1) for pair in (strips_u, strips_v, others)]
    for slot, value in enumerate(whole, KMT):
        put(slot, value[:TILE], value[TILE:])
    row = lax.broadcasted_iota(jnp.int32, (TILE, breadth), 0)
    for field, first, width in ((0, U_ROWS, 2), (1, V_ROWS, 2), (2, T_ROWS, 1)):
        each = TILE // width
        for tile in range(levels // each):
            low = high = jnp.zeros((TILE, breadth), F32)
            for q in range(each):
                value = ends[field, tile * each + q]
                here = row // width == q
                low = jnp.where(here, turn(value[:TILE], width * q, 0), low)
                high = jnp.where(here, turn(value[TILE:], width * (q + 1), 0), high)
            put(first + tile, low, high)


def halo_rows(rows_even, rows_odd, first, width, k):
    each = TILE // width
    tile = first + k // each
    north, south = swap(is_even("lat"), rows_even[tile], rows_odd[tile])
    at = lax.rem(k, each) * width
    south = pltpu.roll(south, lax.rem(2 * TILE - width - at, TILE), 0)
    north = pltpu.roll(north, lax.rem(TILE - at, TILE), 0)
    return south, north


def advance_inner(state, kmt, rows_odd, rows_even, flow, tracer, flow_u, flow_v, turning):
    levels, rows_here, breadth = state.shape[1:]
    tall = rows_here + 2 * TILE
    lat_even = is_even("lat")

    def halos(slot):
        north, south = swap(lat_even, rows_even[slot], rows_odd[slot])
        return south, north

    south, north = halos(KMT)
    depth = stacked(south, kmt[...].astype(F32), north)
    beside = around(depth)
    row = lax.broadcasted_iota(jnp.int32, (tall, LANES), 0)
    rotation = rotation_at(row - TILE, rows_here)
    turning[...] = rotation
    half_turn = time_step * rotation[:, :1]
    own = slice(TILE, TILE + rows_here)
    flow_u[...] = jnp.zeros_like(flow_u)
    flow_v[...] = jnp.zeros_like(flow_v)

    def body(k, _):
        level = k.astype(F32)
        wet = depth > level
        count = count_wet(beside, level)
        u_south, u_north = halo_rows(rows_even, rows_odd, U_ROWS, 2, k)
        v_south, v_north = halo_rows(rows_even, rows_odd, V_ROWS, 2, k)
        t_south, t_north = halo_rows(rows_even, rows_odd, T_ROWS, 1, k)
        u = jnp.where(wet, stacked(u_south, state[0, k], u_north), 0.0)
        v = jnp.where(wet, stacked(v_south, state[1, k], v_north), 0.0)
        new_u, new_v = advance_flow(u, v, wet, count, half_turn)
        flow_u[...] += new_u
        flow_v[...] += new_v
        flow[0, k] = new_u[own]
        flow[1, k] = new_v[own]
        here = state[2, k]
        stack_t = jnp.where(wet, stacked(t_south, here, t_north), 0.0)
        middle = stack_t[own]
        sides = (east_of(middle), west_of(middle), north_of(stack_t)[own], south_of(stack_t)[own])
        change = spread(
            middle, sides, count[own], diffusivity, carry * u[own], carry * v[own]
        )
        above = state[2, jnp.maximum(k - 1, 0)]
        below = state[2, jnp.minimum(k + 1, levels - 1)]
        vertical = (above - here) + jnp.where(depth[own] > level + 1.0, below - here, 0.0)
        tracer[k] = jnp.where(
            wet[own], here + (change + (time_step * vertical_mix) * vertical), 0.0
        )
        return 0

    lax.fori_loop(0, levels, body, 0)
    row = lax.broadcasted_iota(jnp.int32, (tall, breadth), 0)
    outer = (row < TILE - 1) | (row > TILE + rows_here)
    inner = jnp.zeros((rows_here, breadth), F32)
    for slot, flow_sum in ((SUM_U, flow_u), (SUM_V, flow_v)):
        south, north = halos(slot)
        flow_sum[...] = jnp.where(outer, stacked(south, inner, north), flow_sum[...])


def fill_ends(x, west, east):
    lane = lane_of((x.shape[0], LANES))
    tiles = [x[:, i : i + LANES] for i in range(0, x.shape[1], LANES)]
    if west is not None:
        tiles[0] = jnp.where(lane == 0, west, tiles[0])
    if east is not None:
        tiles[-1] = jnp.where(lane == LANES - 1, east, tiles[-1])
    return jnp.concatenate(tiles, axis=1)


def roll_to(x, source, target, k):
    return turn(x, target - source - TILE * k, 1)


def over_groups(x):
    for step in (TILE, 2 * TILE, 4 * TILE, 8 * TILE):
        x = x + pltpu.roll(x, step, 1)
    return x


def krylov(
    sent_even, sent_odd, got_odd, got_even, flow_u, flow_v, kmt, guess,
    rows_even, rows_odd, turning, edges, basis, moments,
):
    levels = LEVELS
    rows_here, breadth = kmt.shape
    tall = rows_here + 2 * TILE
    lat_even = is_even("lat")
    lon_even = is_even("lon")
    lane = lane_of((tall, LANES))
    place = lax.rem(lane, TILE)
    group = lane // TILE
    level = group.astype(F32)
    own = slice(TILE, TILE + rows_here)
    half_turn = time_step * turning[...]

    def strips(slot):
        rows = slice(slot * tall, (slot + 1) * tall)
        to_east, to_west = swap(lon_even, sent_even[rows], sent_odd[rows])
        from_east, from_west = swap(lon_even, got_even[rows], got_odd[rows])
        west = jnp.where(place < HALO, from_west, turn(to_west, 4, 1))
        east = jnp.where(place >= TILE - HALO, from_east, turn(to_east, -4, 1))
        return west, east

    u_sides, v_sides, other = [strips(slot) for slot in range(3)]
    t_sides = strips(3)
    sums = []
    for side in range(2):
        depth = over_groups(jnp.where(group == 0, other[side], 0.0))
        start = over_groups(jnp.where(group == 1, other[side], 0.0))
        wet = depth > level
        count = count_wet(around(depth), level)
        u = jnp.where(wet, u_sides[side], 0.0)
        v = jnp.where(wet, v_sides[side], 0.0)
        new_u, new_v = advance_flow(u, v, wet, count, half_turn)
        here = jnp.where(wet, t_sides[side], 0.0)
        change = spread(here, around(here), count, diffusivity, carry * u, carry * v)
        above = jnp.where(group > 0, turn(here, TILE, 1) - here, 0.0)
        below = jnp.where(depth > level + 1.0, turn(here, -TILE, 1) - here, 0.0)
        new_t = jnp.where(
            wet, here + (change + (time_step * vertical_mix) * (above + below)), 0.0
        )
        edges[side, 0] = new_u[own]
        edges[side, 1] = new_v[own]
        edges[side, 2] = new_t[own]
        sums.append((over_groups(new_u), over_groups(new_v), depth, start))

    def assemble(field, number, seam):
        west = turn(sums[0][number], 2, 1)
        east = turn(sums[1][number], -2, 1)
        halo = jnp.where(lane < LANES // 2, east, west)
        tiles = [field[:, i : i + LANES] for i in range(0, breadth, LANES)]
        if seam:
            tiles[0] = jnp.where(lane == 0, west, tiles[0])
            tiles[-1] = jnp.where(lane == LANES - 1, east, tiles[-1])
        return jnp.concatenate(tiles + [halo], axis=1)

    def tall_field(slot, value):
        north, south = swap(lat_even, rows_even[slot], rows_odd[slot])
        return stacked(south, value, north)

    wide_u = assemble(flow_u[...], 0, True)
    wide_v = assemble(flow_v[...], 1, True)
    wet_levels = assemble(tall_field(KMT, kmt[...].astype(F32)), 2, False)
    first = assemble(tall_field(GUESS, guess[...]), 3, False)

    divergence = 0.5 * (east_of(wide_u) - west_of(wide_u)) + 0.5 * (
        north_of(wide_v) - south_of(wide_v)
    )
    depth = wet_levels * (1.0 / levels)
    ocean = wet_levels > 0.0
    to_east = edge_weight * jnp.minimum(depth, east_of(depth))
    to_north = edge_weight * jnp.minimum(depth, north_of(depth))
    depth_north = north_of(depth)
    to_ne = corner_weight * jnp.minimum(depth, east_of(depth_north))
    to_nw = corner_weight * jnp.minimum(depth, west_of(depth_north))
    to_west = west_of(to_east)
    to_south = south_of(to_north)
    to_sw = south_of(west_of(to_ne))
    to_se = south_of(east_of(to_nw))
    diagonal = storage + (
        (to_east + to_west) + (to_north + to_south) + ((to_ne + to_nw) + (to_se + to_sw))
    )

    def neighbours(x):
        up, down = (north_of(x), south_of(x))
        eastern = to_east * x + to_ne_w * up + to_se_w * down
        western = to_west * x + to_nw_e * up + to_sw_e * down
        return to_north * up + to_south * down + (east_of(eastern) + west_of(western))

    to_ne_w = west_of(to_ne)
    to_se_w = west_of(to_se)
    to_nw_e = east_of(to_nw)
    to_sw_e = east_of(to_sw)
    to_east, to_west = (west_of(to_east), east_of(to_west))

    start = jnp.where(ocean, first, 0.0)
    rhs = jnp.where(ocean, storage * (start - time_step * divergence), 0.0)
    residual = rhs - (diagonal * start - neighbours(start))
    inverse = 1.0 / diagonal
    vectors = [residual * inverse]
    basis[0] = start
    basis[1] = vectors[0]
    for k in range(1, ITERS):
        vectors.append(neighbours(vectors[-1]) * inverse)
        basis[k + 1] = vectors[k]
    last = neighbours(vectors[-1])

    def inner(x):
        return x[own, :breadth]

    weighted = [inner(diagonal * x) for x in vectors] + [inner(last)]
    held = [inner(x) for x in vectors]
    slot = lane_of((TILE, LANES))
    total = jnp.zeros((TILE, LANES), F32)
    for m in range(2 * ITERS):
        product = held[m // 2] * weighted[(m + 1) // 2]
        folded = None
        for i in range(0, rows_here, TILE):
            for j in range(0, breadth, LANES):
                part = product[i : i + TILE, j : j + LANES]
                folded = part if folded is None else folded + part
        total = jnp.where(slot == m, jnp.sum(folded, axis=1, keepdims=True), total)
    moments[...] = jnp.sum(total, axis=0, keepdims=True)


def finish(shares, basis, edges, kmt, flow, tracer, out, pressure, done, held, sems, held_sem):
    levels, rows_here, breadth = tracer.shape
    own = slice(TILE, TILE + rows_here)
    chunks = sems.shape[1]
    size = levels // chunks

    def send(first, last, c):
        part = pl.ds(c * size, size)
        fields = slice(first, last)
        return pltpu.make_async_copy(
            done.at[fields, part], out.at[fields, part], sems.at[first // 2, c]
        )

    def ended(value, field, k):
        return fill_ends(
            value,
            roll_to(edges[0, field], HALO, 0, k),
            roll_to(edges[1, field], 1, LANES - 1, k),
        )

    for c in range(chunks):
        for k in range(c * size, (c + 1) * size):
            done[2, k] = ended(tracer[k], 2, k)
        send(2, 3, c).start()
    totals = jnp.sum(shares[...].reshape(-1, TILE, LANES), axis=0)
    for step in (1, 2, 4):
        totals = totals + turn(totals, step, 0)
    lane = lane_of((TILE, LANES))

    def everywhere(m):
        one = jnp.sum(jnp.where(lane == m, totals, 0.0), axis=1, keepdims=True)
        return jnp.broadcast_to(one, (TILE, LANES))

    res = [everywhere(m) for m in range(2 * ITERS)]
    dirn = list(res)
    one, zero = (jnp.ones((TILE, LANES), F32), jnp.zeros((TILE, LANES), F32))
    res_in = [one] + [zero] * (ITERS - 1)
    dir_in = list(res_in)
    height_in = [zero] * ITERS
    for k in range(ITERS):
        step = res[k] / (dirn[k] - dirn[k + 1])
        step = jnp.clip(step, 1.0 / HIGHEST, 1.0 / LOWEST)
        height_in = [h + step * d for h, d in zip(height_in, dir_in)]
        if k + 1 < ITERS:
            new = [res[m] - step * (dirn[m] - dirn[m + 1]) for m in range(len(dirn) - 1)]
            ratio = jnp.clip((step * (1.0 / res[k])) * new[k + 1], 0.0, HIGHEST / LOWEST)
            dirn = [n + ratio * d for n, d in zip(new, dirn)]
            res = new
            moved = [zero] + dir_in[:-1]
            res_in = [r - step * (d - m) for r, d, m in zip(res_in, dir_in, moved)]
            dir_in = [r + ratio * d for r, d in zip(res_in, dir_in)]

    def tile_of(i, j):
        cut = slice(i, i + TILE), slice(j, j + LANES)
        value = basis[0, *cut]
        for k in range(ITERS):
            value = value + height_in[k] * basis[k + 1, *cut]
        return value

    tall, wide = basis.shape[1:]
    height = jnp.concatenate(
        [
            jnp.concatenate([tile_of(i, j) for j in range(0, wide, LANES)], axis=1)
            for i in range(0, tall, TILE)
        ],
        axis=0,
    )
    held[...] = gravity * height[own, :breadth]
    pressure_out = pltpu.make_async_copy(held, pressure, held_sem.at[0])
    pressure_out.start()
    pull = 0.5 * time_step * gravity
    slope_east = pull * (east_of(height) - west_of(height))[own, :breadth]
    slope_north = pull * (north_of(height) - south_of(height))[own, :breadth]
    wet_levels = kmt[...]
    for c in range(chunks):
        for k in range(c * size, (c + 1) * size):
            wet = wet_levels > k
            for field, slope in ((0, slope_east), (1, slope_north)):
                done[field, k] = jnp.where(wet, ended(flow[field, k], field, k) - slope, 0.0)
        send(0, 2, c).start()
    pressure_out.wait()
    for c in range(chunks):
        send(2, 3, c).wait()
        send(0, 2, c).wait()


def pairs(axis):
    peers = lax.axis_size(axis)
    even = [(i, i ^ 1) for i in range(peers)]
    odd = [(i, ((i + 1) ^ 1) - 1) for i in range(1, peers - 1)]
    if axis == "lon":
        odd += [(0, peers - 1), (peers - 1, 0)]
    return even, odd


def exchange(axis, to_even, to_odd):
    even, odd = pairs(axis)
    from_odd = lax.ppermute(to_odd, axis, odd)
    return lax.ppermute(to_even, axis, even), from_odd


def on_device(state, kmt, first_guess):
    _, levels, rows_here, breadth = state.shape
    tall = rows_here + 2 * TILE
    wide = breadth + LANES
    shape = lambda *dims: jax.ShapeDtypeStruct(dims, F32)

    devices = lax.axis_size("lon") * lax.axis_size("lat")
    hbm = pl.BlockSpec(memory_space=pltpu.HBM)
    vmem = pl.BlockSpec(memory_space=pltpu.VMEM)
    to_odd, to_even = pl.pallas_call(
        pack_rows,
        in_specs=[hbm] * 3,
        out_specs=[vmem] * 2,
        out_shape=[pltpu.VMEM((SLOTS, TILE, breadth), F32)] * 2,
        scratch_shapes=[
            pltpu.VMEM((3, levels, 2 * TILE, breadth), F32),
            pltpu.VMEM((2 * TILE, breadth), jnp.int32),
            pltpu.VMEM((2 * TILE, breadth), F32),
            pltpu.SemaphoreType.DMA((6,)),
        ],
        compiler_params=params(VMEM_FIRST),
    )(state, kmt, first_guess)
    rows_even, rows_odd = exchange("lat", to_even, to_odd)

    strips = pl.pallas_call(
        pack_own,
        out_shape=shape(2, 4, rows_here, LANES),
        compiler_params=params(),
        cost_estimate=cost(state.size),
    )(state, kmt, first_guess)
    length = 4 * tall
    sent_odd, sent_even = pl.pallas_call(
        pack_cols,
        out_shape=[shape(length, LANES)] * 2,
        compiler_params=params(),
    )(strips, rows_odd, rows_even)
    got_even, got_odd = exchange("lon", sent_even, sent_odd)

    flow, tracer, flow_u, flow_v, turning = pl.pallas_call(
        advance_inner,
        out_shape=[
            shape(2, levels, rows_here, breadth),
            shape(levels, rows_here, breadth),
            shape(tall, breadth),
            shape(tall, breadth),
            shape(tall, LANES),
        ],
        compiler_params=params(),
        cost_estimate=cost(state.size),
    )(state, kmt, rows_odd, rows_even)

    edges, basis, moments = pl.pallas_call(
        krylov,
        out_shape=[
            shape(2, 3, rows_here, LANES),
            shape(ITERS + 1, tall, wide),
            shape(1, LANES),
        ],
        compiler_params=params(),
    )(
        sent_even, sent_odd, got_odd, got_even, flow_u, flow_v, kmt, first_guess,
        rows_even, rows_odd, turning,
    )

    shares = jnp.broadcast_to(moments[None], (devices, 1, LANES))
    shares = lax.all_to_all(shares, ("lon", "lat"), 0, 0)
    return pl.pallas_call(
        finish,
        in_specs=[vmem] * 6,
        out_specs=[hbm, hbm],
        out_shape=[shape(3, levels, rows_here, breadth), shape(rows_here, breadth)],
        scratch_shapes=[
            pltpu.VMEM((3, levels, rows_here, breadth), F32),
            pltpu.VMEM((rows_here, breadth), F32),
            pltpu.SemaphoreType.DMA((2, 4)),
            pltpu.SemaphoreType.DMA((1,)),
        ],
        compiler_params=params(),
    )(shares.reshape(devices, LANES), basis, edges, kmt, flow, tracer)


def solution(mesh):
    placed = (P(None, None, "lat", "lon"), P("lat", "lon"), P("lat", "lon"))
    return jax.shard_map(
        on_device,
        mesh=mesh,
        in_specs=placed,
        out_specs=(P(None, None, "lat", "lon"), P("lat", "lon")),
        check_vma=False,
    )
```

```python
import jax
import jax.numpy as jnp
from jax import lax
from jax.experimental import pallas as pl
from jax.experimental.pallas import tpu as pltpu
from jax.sharding import PartitionSpec as P

ITERS = 4
F32 = jnp.float32

viscosity = 0.12
diffusivity = 0.1
advection_scale = 0.5
vertical_mix = 0.2
coriolis_scale = 0.6
time_step = 0.5
storage = 0.5
gravity = 1.5
edge_weight = 2.0 / 3.0
corner_weight = 1.0 / 6.0

TILE = 8
LANES = 128
LEVELS = LANES // TILE
HALO = 6

U_ROWS = 0
V_ROWS = U_ROWS + LEVELS // 4
T_ROWS = V_ROWS + LEVELS // 4
KMT, GUESS, SUMS, STRIPS = range(T_ROWS + LEVELS // 8, T_ROWS + LEVELS // 8 + 4)
SLOTS = STRIPS + 3

LOWEST = storage / (storage + 4 * edge_weight + 4 * corner_weight)
HIGHEST = 2.0 - LOWEST
VMEM_LIMIT = 16 * 1024 * 1024
VMEM_FIRST = 64520000


def params(limit=VMEM_LIMIT):
    return pltpu.CompilerParams(vmem_limit_bytes=limit)


def cost(size):
    return pl.CostEstimate(flops=60 * size, bytes_accessed=8 * size, transcendentals=0)


def turn(x, shift, axis):
    return pltpu.roll(x, shift % x.shape[axis], axis)


def east_of(x):
    return turn(x, -1, 1)


def west_of(x):
    return turn(x, 1, 1)


def north_of(x):
    return turn(x, -1, 0)


def south_of(x):
    return turn(x, 1, 0)


def lane_of(shape):
    return lax.broadcasted_iota(jnp.int32, shape, len(shape) - 1)


def is_even(axis):
    return lax.rem(lax.axis_index(axis), 2) == 0


def swap(first, a, b):
    return jnp.where(first, a, b), jnp.where(first, b, a)


def stacked(south, own, north):
    return jnp.concatenate([south, own, north], axis=0)


def place(group, k, west, east, acc):
    to_west, to_east = acc
    to_west = jnp.where(group == k, pltpu.roll(west, 2 + TILE * k, 1), to_west)
    to_east = jnp.where(
        group == k, pltpu.roll(east, lax.rem(HALO + TILE * k, LANES), 1), to_east
    )
    return to_west, to_east


def pack_own(state, kmt, guess, strips):
    levels, rows_here, breadth = state.shape[1:]
    group = lane_of((rows_here, LANES)) // TILE
    ends = slice(0, LANES), slice(breadth - LANES, breadth)
    blank = (jnp.zeros((rows_here, LANES), F32),) * 2
    for field in range(3):

        def body(k, acc, field=field):
            west, east = [state[field, k, :, cols] for cols in ends]
            return place(group, k, west, east, acc)

        acc = lax.fori_loop(0, levels, body, blank, unroll=4)
        strips[0, field], strips[1, field] = acc
    slot = lax.rem(lane_of((rows_here, LANES)), TILE)
    strips[0, 0] = jnp.where(slot == 1, turn(strips[0, 2], -1, 1), strips[0, 0])
    strips[1, 0] = jnp.where(slot == HALO, turn(strips[1, 2], 1, 1), strips[1, 0])
    acc = blank
    for number, own in enumerate((kmt[...].astype(F32), guess[...])):
        west, east = [own[:, cols] for cols in ends]
        acc = place(group, jnp.int32(number), west, east, acc)
    strips[0, 3], strips[1, 3] = acc


def pack_cols(strips, rows_odd, rows_even, msg_odd, msg_even, own_tracer):
    tall = strips.shape[2] + 2 * TILE
    lat_even = is_even("lat")
    lon_even = is_even("lon")

    def tall_strips(field, south, north):
        return [
            stacked(
                south[:, i * LANES : (i + 1) * LANES],
                strips[i, field],
                north[:, i * LANES : (i + 1) * LANES],
            )
            for i in range(2)
        ]

    def put(number, field, south, north):
        base = number * tall
        to_west, to_east = tall_strips(field, south, north)
        a, b = swap(lon_even, to_east, to_west)
        msg_even[base : base + tall] = a
        msg_odd[base : base + tall] = b

    halos = []
    for slot in range(STRIPS, SLOTS):
        north, south = swap(lat_even, rows_even[slot], rows_odd[slot])
        halos.append((south, north))
    put(0, 0, *halos[0])
    put(1, 1, *halos[1])
    put(2, 3, *halos[2])
    own_tracer[0], own_tracer[1] = tall_strips(
        2, turn(halos[0][0], -1, 0), turn(halos[0][1], 1, 0)
    )


def rotation_at(row, rows_here):
    total_rows = rows_here * lax.axis_size("lat")
    row = (row + lax.axis_index("lat") * rows_here).astype(F32)
    angle = jnp.pi / 180.0 * (-80.0 + 160.0 * (row + 0.5) / total_rows)
    return coriolis_scale * jnp.sin(angle)


def around(x):
    return east_of(x), west_of(x), north_of(x), south_of(x)


def count_wet(sides, level):
    total = None
    for side in sides:
        term = jnp.where(side > level, 1.0, 0.0)
        total = term if total is None else total + term
    return total


def spread(x, sides, count, coefficient, zonal, merid):
    east, west, north, south = sides
    laplace = east + west + north + south - count * x
    return (
        (time_step * coefficient) * laplace
        - zonal * (east - west)
        - merid * (north - south)
    )


carry = 0.5 * time_step * advection_scale


def advance_flow(u, v, wet, count, half_turn):
    zonal, merid = (carry * u, carry * v)
    new_u = u + (spread(u, around(u), count, viscosity, zonal, merid) + half_turn * v)
    new_v = v + (spread(v, around(v), count, viscosity, zonal, merid) - half_turn * u)
    return jnp.where(wet, new_u, 0.0), jnp.where(wet, new_v, 0.0)


def is_sum_u(row, southern):
    first = TILE - 5 if southern else 1
    return (row >= first) & (row < first + 4)


def pack_rows(state, kmt, guess, msg_odd, msg_even, ends, wet_ends, guess_ends, sems):
    levels, rows_here, breadth = state.shape[1:]
    even = is_even("lat")
    parts = [slice(k, k + levels // 4) for k in range(0, levels, levels // 4)]
    copies = []
    for part in [None] + parts:
        copies.append([])
        for number, rows in enumerate((slice(0, TILE), slice(rows_here - TILE, rows_here))):
            held = slice(number * TILE, (number + 1) * TILE)
            if part is not None:
                pairs_of_refs = [(state.at[:, part, rows, :], ends.at[:, part, held, :])]
            else:
                pairs_of_refs = [
                    (kmt.at[rows, :], wet_ends.at[held, :]),
                    (guess.at[rows, :], guess_ends.at[held, :]),
                ]
            for source, target in pairs_of_refs:
                item = pltpu.make_async_copy(source, target, sems.at[sum(map(len, copies))])
                item.start()
                copies[-1].append(item)
    row = lax.broadcasted_iota(jnp.int32, (2 * TILE, LANES), 0)
    rotation = rotation_at(jnp.where(row < TILE, row, row + rows_here - 2 * TILE), rows_here)
    half_turn = time_step * rotation[:, :1]
    group = lane_of((2 * TILE, LANES)) // TILE
    row = lax.broadcasted_iota(jnp.int32, (2 * TILE, breadth), 0)
    borrowed = (row == TILE - 1) | (row == TILE)
    for item in copies[0]:
        item.wait()

    depth = wet_ends[...].astype(F32)
    beside = around(depth)
    cut = slice(0, LANES), slice(breadth - LANES, breadth)

    def body(k, carried):
        sum_u, sum_v, strips_u, strips_v = carried
        level = k.astype(F32)
        wet = depth > level
        raw_u, raw_v, raw_t = [ends[field, k] for field in range(3)]
        u = jnp.where(wet, raw_u, 0.0)
        v = jnp.where(wet, raw_v, 0.0)
        new_u, new_v = advance_flow(u, v, wet, count_wet(beside, level), half_turn)
        moved = jnp.concatenate([turn(raw_t[:TILE], -1, 0), turn(raw_t[TILE:], 1, 0)], axis=0)
        lent = jnp.where(borrowed, moved, raw_u)
        strips_u = place(group, k, lent[:, cut[0]], lent[:, cut[1]], strips_u)
        strips_v = place(group, k, raw_v[:, cut[0]], raw_v[:, cut[1]], strips_v)
        return sum_u + new_u, sum_v + new_v, strips_u, strips_v

    empty = jnp.zeros((2 * TILE, breadth), F32)
    blank = (jnp.zeros((2 * TILE, LANES), F32),) * 2
    carried = (empty, empty, blank, blank)
    for part, items in zip(parts, copies[1:]):
        for item in items:
            item.wait()
        carried = lax.fori_loop(part.start, part.stop, body, carried, unroll=4)
    sum_u, sum_v, strips_u, strips_v = carried
    starts = guess_ends[...]
    others = blank
    for number, value in enumerate((depth, starts)):
        others = place(group, jnp.int32(number), value[:, cut[0]], value[:, cut[1]], others)

    def put(slot, low, high):
        a, b = swap(even, high, low)
        msg_even[slot] = a
        msg_odd[slot] = b

    row = lax.rem(lax.broadcasted_iota(jnp.int32, (2 * TILE, breadth), 0), TILE)
    first = jnp.concatenate(
        [is_sum_u(row[:TILE], False), is_sum_u(row[TILE:], True)], axis=0
    )
    moved = jnp.concatenate([turn(sum_v[:TILE], 4, 0), turn(sum_v[TILE:], 4, 0)], axis=0)
    whole = [depth, starts, jnp.where(first, sum_u, moved)]
    whole += [jnp.concatenate(pair, axis=1) for pair in (strips_u, strips_v, others)]
    for slot, value in enumerate(whole, KMT):
        put(slot, value[:TILE], value[TILE:])
    row = lax.broadcasted_iota(jnp.int32, (TILE, breadth), 0)
    for field, first, width in ((0, U_ROWS, 2), (1, V_ROWS, 2), (2, T_ROWS, 1)):
        each = TILE // width
        for tile in range(levels // each):
            low = high = jnp.zeros((TILE, breadth), F32)
            for q in range(each):
                value = ends[field, tile * each + q]
                here = row // width == q
                low = jnp.where(here, turn(value[:TILE], width * q, 0), low)
                high = jnp.where(here, turn(value[TILE:], width * (q + 1), 0), high)
            put(first + tile, low, high)


def halo_rows(rows_even, rows_odd, first, width, k):
    each = TILE // width
    tile = first + k // each
    north, south = swap(is_even("lat"), rows_even[tile], rows_odd[tile])
    at = lax.rem(k, each) * width
    south = pltpu.roll(south, lax.rem(2 * TILE - width - at, TILE), 0)
    north = pltpu.roll(north, lax.rem(TILE - at, TILE), 0)
    return south, north


def advance_inner(state, kmt, rows_odd, rows_even, flow, tracer, flow_u, flow_v, turning):
    levels, rows_here, breadth = state.shape[1:]
    tall = rows_here + 2 * TILE
    lat_even = is_even("lat")

    def halos(slot):
        north, south = swap(lat_even, rows_even[slot], rows_odd[slot])
        return south, north

    south, north = halos(KMT)
    depth = stacked(south, kmt[...].astype(F32), north)
    beside = around(depth)
    row = lax.broadcasted_iota(jnp.int32, (tall, LANES), 0)
    rotation = rotation_at(row - TILE, rows_here)
    turning[...] = rotation
    half_turn = time_step * rotation[:, :1]
    own = slice(TILE, TILE + rows_here)
    flow_u[...] = jnp.zeros_like(flow_u)
    flow_v[...] = jnp.zeros_like(flow_v)

    def body(k, _):
        level = k.astype(F32)
        wet = depth > level
        count = count_wet(beside, level)
        u_south, u_north = halo_rows(rows_even, rows_odd, U_ROWS, 2, k)
        v_south, v_north = halo_rows(rows_even, rows_odd, V_ROWS, 2, k)
        t_south, t_north = halo_rows(rows_even, rows_odd, T_ROWS, 1, k)
        u = jnp.where(wet, stacked(u_south, state[0, k], u_north), 0.0)
        v = jnp.where(wet, stacked(v_south, state[1, k], v_north), 0.0)
        new_u, new_v = advance_flow(u, v, wet, count, half_turn)
        flow_u[...] += new_u
        flow_v[...] += new_v
        flow[0, k] = new_u[own]
        flow[1, k] = new_v[own]
        here = state[2, k]
        stack_t = jnp.where(wet, stacked(t_south, here, t_north), 0.0)
        middle = stack_t[own]
        sides = (east_of(middle), west_of(middle), north_of(stack_t)[own], south_of(stack_t)[own])
        change = spread(
            middle, sides, count[own], diffusivity, carry * u[own], carry * v[own]
        )
        above = state[2, jnp.maximum(k - 1, 0)]
        below = state[2, jnp.minimum(k + 1, levels - 1)]
        vertical = (above - here) + jnp.where(depth[own] > level + 1.0, below - here, 0.0)
        tracer[k] = jnp.where(
            wet[own], here + (change + (time_step * vertical_mix) * vertical), 0.0
        )
        return 0

    lax.fori_loop(0, levels, body, 0)
    row = lax.broadcasted_iota(jnp.int32, (tall, breadth), 0)
    outer = (row < TILE - 1) | (row > TILE + rows_here)
    inner = jnp.zeros((rows_here, breadth), F32)
    sums = halos(SUMS)
    for shift, flow_sum in ((0, flow_u), (-4, flow_v)):
        south, north = [turn(x, shift, 0) for x in sums]
        flow_sum[...] = jnp.where(outer, stacked(south, inner, north), flow_sum[...])


def fill_ends(x, west, east):
    lane = lane_of((x.shape[0], LANES))
    tiles = [x[:, i : i + LANES] for i in range(0, x.shape[1], LANES)]
    if west is not None:
        tiles[0] = jnp.where(lane == 0, west, tiles[0])
    if east is not None:
        tiles[-1] = jnp.where(lane == LANES - 1, east, tiles[-1])
    return jnp.concatenate(tiles, axis=1)


def roll_to(x, source, target, k):
    return turn(x, target - source - TILE * k, 1)


def over_groups(x):
    for step in (TILE, 2 * TILE, 4 * TILE, 8 * TILE):
        x = x + pltpu.roll(x, step, 1)
    return x


def krylov(
    sent_even, sent_odd, got_odd, got_even, flow_u, flow_v, kmt, guess,
    rows_even, rows_odd, turning, own_tracer, edges, basis, moments,
):
    levels = LEVELS
    rows_here, breadth = kmt.shape
    tall = rows_here + 2 * TILE
    lat_even = is_even("lat")
    lon_even = is_even("lon")
    lane = lane_of((tall, LANES))
    place = lax.rem(lane, TILE)
    group = lane // TILE
    level = group.astype(F32)
    own = slice(TILE, TILE + rows_here)
    half_turn = time_step * turning[...]

    def received(slot):
        rows = slice(slot * tall, (slot + 1) * tall)
        from_east, from_west = swap(lon_even, got_even[rows], got_odd[rows])
        return from_west, from_east

    def strips(slot):
        rows = slice(slot * tall, (slot + 1) * tall)
        to_east, to_west = swap(lon_even, sent_even[rows], sent_odd[rows])
        from_west, from_east = received(slot)
        west = jnp.where(place < HALO, from_west, turn(to_west, 4, 1))
        east = jnp.where(place >= TILE - HALO, from_east, turn(to_east, -4, 1))
        return west, east

    u_sides, v_sides, other = [strips(slot) for slot in range(3)]
    from_west, from_east = received(0)
    t_sides = (
        jnp.where(place == HALO - 1, turn(from_west, -1, 1), turn(own_tracer[0], 4, 1)),
        jnp.where(place == TILE - HALO, turn(from_east, 1, 1), turn(own_tracer[1], -4, 1)),
    )
    sums = []
    for side in range(2):
        depth = over_groups(jnp.where(group == 0, other[side], 0.0))
        wet = depth > level
        count = count_wet(around(depth), level)
        u = jnp.where(wet, u_sides[side], 0.0)
        v = jnp.where(wet, v_sides[side], 0.0)
        new_u, new_v = advance_flow(u, v, wet, count, half_turn)
        here = jnp.where(wet, t_sides[side], 0.0)
        change = spread(here, around(here), count, diffusivity, carry * u, carry * v)
        above = jnp.where(group > 0, turn(here, TILE, 1) - here, 0.0)
        below = jnp.where(depth > level + 1.0, turn(here, -TILE, 1) - here, 0.0)
        new_t = jnp.where(
            wet, here + (change + (time_step * vertical_mix) * (above + below)), 0.0
        )
        edges[side, 0] = new_u[own]
        edges[side, 1] = new_v[own]
        edges[side, 2] = new_t[own]
        sums.append((over_groups(new_u), over_groups(new_v), depth, turn(other[side], -TILE, 1)))

    def assemble(field, number, seam):
        west = turn(sums[0][number], -HALO, 1)
        east = turn(sums[1][number], -2, 1)
        halo = jnp.where(lane < LANES // 2, east, west)
        tiles = [field[:, i : i + LANES] for i in range(0, breadth, LANES)]
        if seam:
            tiles[0] = jnp.where(lane == 0, west, tiles[0])
            tiles[-1] = jnp.where(lane == LANES - 1, east, tiles[-1])
        return jnp.concatenate(tiles + [halo], axis=1)

    def tall_field(slot, value):
        north, south = swap(lat_even, rows_even[slot], rows_odd[slot])
        return stacked(south, value, north)

    wide_u = assemble(flow_u[...], 0, True)
    wide_v = assemble(flow_v[...], 1, True)
    wet_levels = assemble(tall_field(KMT, kmt[...].astype(F32)), 2, False)
    first = assemble(tall_field(GUESS, guess[...]), 3, False)

    divergence = 0.5 * (east_of(wide_u) - west_of(wide_u)) + 0.5 * (
        north_of(wide_v) - south_of(wide_v)
    )
    depth = wet_levels * (1.0 / levels)
    ocean = wet_levels > 0.0
    to_east = edge_weight * jnp.minimum(depth, east_of(depth))
    to_north = edge_weight * jnp.minimum(depth, north_of(depth))
    depth_north = north_of(depth)
    to_ne = corner_weight * jnp.minimum(depth, east_of(depth_north))
    to_nw = corner_weight * jnp.minimum(depth, west_of(depth_north))
    to_west = west_of(to_east)
    to_south = south_of(to_north)
    to_sw = south_of(west_of(to_ne))
    to_se = south_of(east_of(to_nw))
    diagonal = storage + (
        (to_east + to_west) + (to_north + to_south) + ((to_ne + to_nw) + (to_se + to_sw))
    )

    def neighbours(x):
        up, down = (north_of(x), south_of(x))
        eastern = to_east * x + to_ne_w * up + to_se_w * down
        western = to_west * x + to_nw_e * up + to_sw_e * down
        return to_north * up + to_south * down + (east_of(eastern) + west_of(western))

    to_ne_w = west_of(to_ne)
    to_se_w = west_of(to_se)
    to_nw_e = east_of(to_nw)
    to_sw_e = east_of(to_sw)
    to_east, to_west = (west_of(to_east), east_of(to_west))

    start = jnp.where(ocean, first, 0.0)
    rhs = jnp.where(ocean, storage * (start - time_step * divergence), 0.0)
    residual = rhs - (diagonal * start - neighbours(start))
    inverse = 1.0 / diagonal
    vectors = [residual * inverse]
    basis[0] = start
    basis[1] = vectors[0]
    for k in range(1, ITERS):
        vectors.append(neighbours(vectors[-1]) * inverse)
        basis[k + 1] = vectors[k]
    last = neighbours(vectors[-1])

    def inner(x):
        return x[own, :breadth]

    weighted = [inner(diagonal * x) for x in vectors] + [inner(last)]
    held = [inner(x) for x in vectors]
    slot = lane_of((TILE, LANES))
    total = jnp.zeros((TILE, LANES), F32)
    for m in range(2 * ITERS):
        product = held[m // 2] * weighted[(m + 1) // 2]
        folded = None
        for i in range(0, rows_here, TILE):
            for j in range(0, breadth, LANES):
                part = product[i : i + TILE, j : j + LANES]
                folded = part if folded is None else folded + part
        total = jnp.where(slot == m, jnp.sum(folded, axis=1, keepdims=True), total)
    moments[...] = jnp.sum(total, axis=0, keepdims=True)


def finish(shares, basis, edges, kmt, flow, tracer, out, pressure, done, held, sems, held_sem):
    levels, rows_here, breadth = tracer.shape
    own = slice(TILE, TILE + rows_here)
    chunks = sems.shape[1]
    size = levels // chunks

    def send(first, last, c):
        part = pl.ds(c * size, size)
        fields = slice(first, last)
        return pltpu.make_async_copy(
            done.at[fields, part], out.at[fields, part], sems.at[first // 2, c]
        )

    def ended(value, field, k):
        return fill_ends(
            value,
            roll_to(edges[0, field], HALO, 0, k),
            roll_to(edges[1, field], 1, LANES - 1, k),
        )

    for c in range(chunks):
        for k in range(c * size, (c + 1) * size):
            done[2, k] = ended(tracer[k], 2, k)
        send(2, 3, c).start()
    totals = jnp.sum(shares[...].reshape(-1, TILE, LANES), axis=0)
    for step in (1, 2, 4):
        totals = totals + turn(totals, step, 0)
    lane = lane_of((TILE, LANES))

    def everywhere(m):
        one = jnp.sum(jnp.where(lane == m, totals, 0.0), axis=1, keepdims=True)
        return jnp.broadcast_to(one, (TILE, LANES))

    res = [everywhere(m) for m in range(2 * ITERS)]
    dirn = list(res)
    one, zero = (jnp.ones((TILE, LANES), F32), jnp.zeros((TILE, LANES), F32))
    res_in = [one] + [zero] * (ITERS - 1)
    dir_in = list(res_in)
    height_in = [zero] * ITERS
    for k in range(ITERS):
        step = res[k] / (dirn[k] - dirn[k + 1])
        step = jnp.clip(step, 1.0 / HIGHEST, 1.0 / LOWEST)
        height_in = [h + step * d for h, d in zip(height_in, dir_in)]
        if k + 1 < ITERS:
            new = [res[m] - step * (dirn[m] - dirn[m + 1]) for m in range(len(dirn) - 1)]
            ratio = jnp.clip((step * (1.0 / res[k])) * new[k + 1], 0.0, HIGHEST / LOWEST)
            dirn = [n + ratio * d for n, d in zip(new, dirn)]
            res = new
            moved = [zero] + dir_in[:-1]
            res_in = [r - step * (d - m) for r, d, m in zip(res_in, dir_in, moved)]
            dir_in = [r + ratio * d for r, d in zip(res_in, dir_in)]

    def tile_of(i, j):
        cut = slice(i, i + TILE), slice(j, j + LANES)
        value = basis[0, *cut]
        for k in range(ITERS):
            value = value + height_in[k] * basis[k + 1, *cut]
        return value

    tall, wide = basis.shape[1:]
    height = jnp.concatenate(
        [
            jnp.concatenate([tile_of(i, j) for j in range(0, wide, LANES)], axis=1)
            for i in range(0, tall, TILE)
        ],
        axis=0,
    )
    held[...] = gravity * height[own, :breadth]
    pressure_out = pltpu.make_async_copy(held, pressure, held_sem.at[0])
    pressure_out.start()
    pull = 0.5 * time_step * gravity
    slope_east = pull * (east_of(height) - west_of(height))[own, :breadth]
    slope_north = pull * (north_of(height) - south_of(height))[own, :breadth]
    wet_levels = kmt[...]
    for c in range(chunks):
        for k in range(c * size, (c + 1) * size):
            wet = wet_levels > k
            for field, slope in ((0, slope_east), (1, slope_north)):
                done[field, k] = jnp.where(wet, ended(flow[field, k], field, k) - slope, 0.0)
        send(0, 2, c).start()
    pressure_out.wait()
    for c in range(chunks):
        send(2, 3, c).wait()
        send(0, 2, c).wait()


def pairs(axis):
    peers = lax.axis_size(axis)
    even = [(i, i ^ 1) for i in range(peers)]
    odd = [(i, ((i + 1) ^ 1) - 1) for i in range(1, peers - 1)]
    if axis == "lon":
        odd += [(0, peers - 1), (peers - 1, 0)]
    return even, odd


def exchange(axis, to_even, to_odd):
    even, odd = pairs(axis)
    from_odd = lax.ppermute(to_odd, axis, odd)
    return lax.ppermute(to_even, axis, even), from_odd


def on_device(state, kmt, first_guess):
    _, levels, rows_here, breadth = state.shape
    tall = rows_here + 2 * TILE
    wide = breadth + LANES
    shape = lambda *dims: jax.ShapeDtypeStruct(dims, F32)

    devices = lax.axis_size("lon") * lax.axis_size("lat")
    hbm = pl.BlockSpec(memory_space=pltpu.HBM)
    vmem = pl.BlockSpec(memory_space=pltpu.VMEM)
    to_odd, to_even = pl.pallas_call(
        pack_rows,
        in_specs=[hbm] * 3,
        out_specs=[vmem] * 2,
        out_shape=[pltpu.VMEM((SLOTS, TILE, breadth), F32)] * 2,
        scratch_shapes=[
            pltpu.VMEM((3, levels, 2 * TILE, breadth), F32),
            pltpu.VMEM((2 * TILE, breadth), jnp.int32),
            pltpu.VMEM((2 * TILE, breadth), F32),
            pltpu.SemaphoreType.DMA((12,)),
        ],
        compiler_params=params(VMEM_FIRST),
    )(state, kmt, first_guess)
    rows_even, rows_odd = exchange("lat", to_even, to_odd)

    strips = pl.pallas_call(
        pack_own,
        out_shape=shape(2, 4, rows_here, LANES),
        compiler_params=params(),
        cost_estimate=cost(state.size),
    )(state, kmt, first_guess)
    length = 3 * tall
    sent_odd, sent_even, own_tracer = pl.pallas_call(
        pack_cols,
        out_shape=[shape(length, LANES)] * 2 + [shape(2, tall, LANES)],
        compiler_params=params(),
    )(strips, rows_odd, rows_even)
    got_even, got_odd = exchange("lon", sent_even, sent_odd)

    flow, tracer, flow_u, flow_v, turning = pl.pallas_call(
        advance_inner,
        out_shape=[
            shape(2, levels, rows_here, breadth),
            shape(levels, rows_here, breadth),
            shape(tall, breadth),
            shape(tall, breadth),
            shape(tall, LANES),
        ],
        compiler_params=params(),
        cost_estimate=cost(state.size),
    )(state, kmt, rows_odd, rows_even)

    edges, basis, moments = pl.pallas_call(
        krylov,
        out_shape=[
            shape(2, 3, rows_here, LANES),
            shape(ITERS + 1, tall, wide),
            shape(1, LANES),
        ],
        compiler_params=params(),
    )(
        sent_even, sent_odd, got_odd, got_even, flow_u, flow_v, kmt, first_guess,
        rows_even, rows_odd, turning, own_tracer,
    )

    shares = jnp.broadcast_to(moments[None], (devices, 1, LANES))
    shares = lax.all_to_all(shares, ("lon", "lat"), 0, 0)
    return pl.pallas_call(
        finish,
        in_specs=[vmem] * 6,
        out_specs=[hbm, hbm],
        out_shape=[shape(3, levels, rows_here, breadth), shape(rows_here, breadth)],
        scratch_shapes=[
            pltpu.VMEM((3, levels, rows_here, breadth), F32),
            pltpu.VMEM((rows_here, breadth), F32),
            pltpu.SemaphoreType.DMA((2, 4)),
            pltpu.SemaphoreType.DMA((1,)),
        ],
        compiler_params=params(),
    )(shares.reshape(devices, LANES), basis, edges, kmt, flow, tracer)


def solution(mesh):
    placed = (P(None, None, "lat", "lon"), P("lat", "lon"), P("lat", "lon"))
    return jax.shard_map(
        on_device,
        mesh=mesh,
        in_specs=placed,
        out_specs=(P(None, None, "lat", "lon"), P("lat", "lon")),
        check_vma=False,
    )
```

```python
import jax
import jax.numpy as jnp
from jax import lax
from jax.experimental import pallas as pl
from jax.experimental.pallas import tpu as pltpu
from jax.sharding import PartitionSpec as P

ITERS = 4
F32 = jnp.float32

viscosity = 0.12
diffusivity = 0.1
advection_scale = 0.5
vertical_mix = 0.2
coriolis_scale = 0.6
time_step = 0.5
storage = 0.5
gravity = 1.5
edge_weight = 2.0 / 3.0
corner_weight = 1.0 / 6.0

TILE = 8
LANES = 128
LEVELS = LANES // TILE
HALO = 6

U_ROWS = 0
V_ROWS = U_ROWS + LEVELS // TILE
T_ROWS = V_ROWS + LEVELS // TILE
KMT, GUESS, SUMS, STRIPS = range(T_ROWS + LEVELS // TILE, T_ROWS + LEVELS // TILE + 4)
SLOTS = STRIPS + 3

LOWEST = storage / (storage + 4 * edge_weight + 4 * corner_weight)
HIGHEST = 2.0 - LOWEST
VMEM_LIMIT = 16 * 1024 * 1024
VMEM_FIRST = 64520000


def params(limit=VMEM_LIMIT):
    return pltpu.CompilerParams(vmem_limit_bytes=limit)


def cost(size):
    return pl.CostEstimate(flops=60 * size, bytes_accessed=8 * size, transcendentals=0)


def turn(x, shift, axis):
    return pltpu.roll(x, shift % x.shape[axis], axis)


def east_of(x):
    return turn(x, -1, 1)


def west_of(x):
    return turn(x, 1, 1)


def north_of(x):
    return turn(x, -1, 0)


def south_of(x):
    return turn(x, 1, 0)


def lane_of(shape):
    return lax.broadcasted_iota(jnp.int32, shape, len(shape) - 1)


def is_even(axis):
    return lax.rem(lax.axis_index(axis), 2) == 0


def swap(first, a, b):
    return jnp.where(first, a, b), jnp.where(first, b, a)


def stacked(south, own, north):
    return jnp.concatenate([south, own, north], axis=0)


def place(group, k, west, east, acc):
    to_west, to_east = acc
    to_west = jnp.where(group == k, pltpu.roll(west, 2 + TILE * k, 1), to_west)
    to_east = jnp.where(
        group == k, pltpu.roll(east, lax.rem(HALO + TILE * k, LANES), 1), to_east
    )
    return to_west, to_east


def over_groups(x):
    for step in (TILE, 2 * TILE, 4 * TILE, 8 * TILE):
        x = x + pltpu.roll(x, step, 1)
    return x


def pack_others(group, wet, guess, cut):
    blank = (jnp.zeros_like(wet[:, cut[0]]),) * 2
    wet = place(group, jnp.int32(0), wet[:, cut[0]], wet[:, cut[1]], blank)
    wet = tuple(over_groups(x) for x in wet)
    return place(group, jnp.int32(1), guess[:, cut[0]], guess[:, cut[1]], wet)


def pack_own(state, kmt, guess, strips):
    levels, rows_here, breadth = state.shape[1:]
    group = lane_of((rows_here, LANES)) // TILE
    ends = slice(0, LANES), slice(breadth - LANES, breadth)
    blank = (jnp.zeros((rows_here, LANES), F32),) * 2
    for field in range(3):

        def body(k, acc, field=field):
            west, east = [state[field, k, :, cols] for cols in ends]
            return place(group, k, west, east, acc)

        acc = lax.fori_loop(0, levels, body, blank, unroll=4)
        strips[0, field], strips[1, field] = acc
    slot = lax.rem(lane_of((rows_here, LANES)), TILE)
    strips[0, 0] = jnp.where(slot == 1, turn(strips[0, 2], -1, 1), strips[0, 0])
    strips[1, 0] = jnp.where(slot == HALO, turn(strips[1, 2], 1, 1), strips[1, 0])
    strips[0, 3], strips[1, 3] = pack_others(group, kmt[...].astype(F32), guess[...], ends)


def pack_cols(strips, rows_odd, rows_even, msg_odd, msg_even, own_tracer):
    tall = strips.shape[2] + 2 * TILE
    lat_even = is_even("lat")
    lon_even = is_even("lon")

    def tall_strips(field, south, north):
        return [
            stacked(
                south[:, i * LANES : (i + 1) * LANES],
                strips[i, field],
                north[:, i * LANES : (i + 1) * LANES],
            )
            for i in range(2)
        ]

    def put(number, field, south, north):
        base = number * tall
        to_west, to_east = tall_strips(field, south, north)
        a, b = swap(lon_even, to_east, to_west)
        msg_even[base : base + tall] = a
        msg_odd[base : base + tall] = b

    halos = []
    for slot in range(STRIPS, SLOTS):
        north, south = swap(lat_even, rows_even[slot], rows_odd[slot])
        halos.append((south, north))
    put(0, 0, *halos[0])
    put(1, 1, *halos[1])
    put(2, 3, *halos[2])
    own_tracer[0], own_tracer[1] = tall_strips(
        2, turn(halos[0][0], -1, 0), turn(halos[0][1], 1, 0)
    )


def rotation_at(row, rows_here):
    total_rows = rows_here * lax.axis_size("lat")
    row = (row + lax.axis_index("lat") * rows_here).astype(F32)
    angle = jnp.pi / 180.0 * (-80.0 + 160.0 * (row + 0.5) / total_rows)
    return coriolis_scale * jnp.sin(angle)


def around(x):
    return east_of(x), west_of(x), north_of(x), south_of(x)


def count_wet(sides, level):
    total = None
    for side in sides:
        term = jnp.where(side > level, 1.0, 0.0)
        total = term if total is None else total + term
    return total


def spread(x, sides, count, coefficient, zonal, merid):
    east, west, north, south = sides
    laplace = east + west + north + south - count * x
    return (
        (time_step * coefficient) * laplace
        - zonal * (east - west)
        - merid * (north - south)
    )


carry = 0.5 * time_step * advection_scale


def advance_flow(u, v, wet, count, half_turn, around=around):
    zonal, merid = (carry * u, carry * v)
    new_u = u + (spread(u, around(u), count, viscosity, zonal, merid) + half_turn * v)
    new_v = v + (spread(v, around(v), count, viscosity, zonal, merid) - half_turn * u)
    return jnp.where(wet, new_u, 0.0), jnp.where(wet, new_v, 0.0)


def is_sum_u(row, southern):
    first = TILE - 5 if southern else 1
    return (row >= first) & (row < first + 4)


def pack_rows(state, kmt, guess, msg_odd, msg_even, ends, wet_ends, guess_ends, sems):
    levels, rows_here, breadth = state.shape[1:]
    even = is_even("lat")
    parts = [slice(k, k + levels // 4) for k in range(0, levels, levels // 4)]
    copies = []
    for part in [None] + parts:
        copies.append([])
        for number, rows in enumerate((slice(0, TILE), slice(rows_here - TILE, rows_here))):
            held = slice(number * TILE, (number + 1) * TILE)
            if part is not None:
                pairs_of_refs = [(state.at[:, part, rows, :], ends.at[:, part, held, :])]
            else:
                pairs_of_refs = [
                    (kmt.at[rows, :], wet_ends.at[held, :]),
                    (guess.at[rows, :], guess_ends.at[held, :]),
                ]
            for source, target in pairs_of_refs:
                item = pltpu.make_async_copy(source, target, sems.at[sum(map(len, copies))])
                item.start()
                copies[-1].append(item)
    row = lax.broadcasted_iota(jnp.int32, (2 * TILE, LANES), 0)
    rotation = rotation_at(jnp.where(row < TILE, row, row + rows_here - 2 * TILE), rows_here)
    half_turn = time_step * rotation[:, :1]
    group = lane_of((2 * TILE, LANES)) // TILE
    row = lax.broadcasted_iota(jnp.int32, (2 * TILE, breadth), 0)
    borrowed = (row == TILE - 1) | (row == TILE)
    for item in copies[0]:
        item.wait()

    top = row == 2 * TILE - 1

    def within(x):
        east, west, north, south = around(x)
        return east, west, jnp.where(top, 0.0, north), jnp.where(row == 0, 0.0, south)

    depth = wet_ends[...].astype(F32)
    beside = within(depth)
    cut = slice(0, LANES), slice(breadth - LANES, breadth)
    starts = guess_ends[...]
    others = pack_others(group, depth, starts, cut)

    def body(k, carried):
        sum_u, sum_v, strips_u, strips_v = carried
        level = k.astype(F32)
        wet = depth > level
        raw_u, raw_v, raw_t = [ends[field, k] for field in range(3)]
        u = jnp.where(wet, raw_u, 0.0)
        v = jnp.where(wet, raw_v, 0.0)
        new_u, new_v = advance_flow(
            u, v, wet, count_wet(beside, level), half_turn, within
        )
        moved = jnp.concatenate([turn(raw_t[:TILE], -1, 0), turn(raw_t[TILE:], 1, 0)], axis=0)
        lent = jnp.where(borrowed, moved, raw_u)
        strips_u = place(group, k, lent[:, cut[0]], lent[:, cut[1]], strips_u)
        strips_v = place(group, k, raw_v[:, cut[0]], raw_v[:, cut[1]], strips_v)
        return sum_u + new_u, sum_v + new_v, strips_u, strips_v

    empty = jnp.zeros((2 * TILE, breadth), F32)
    blank = (jnp.zeros((2 * TILE, LANES), F32),) * 2
    carried = (empty, empty, blank, blank)
    for part, items in zip(parts, copies[1:]):
        for item in items:
            item.wait()
        carried = lax.fori_loop(part.start, part.stop, body, carried, unroll=4)
    sum_u, sum_v, strips_u, strips_v = carried

    def put(slot, low, high):
        a, b = swap(even, high, low)
        msg_even[slot] = a
        msg_odd[slot] = b

    row = lax.rem(lax.broadcasted_iota(jnp.int32, (2 * TILE, breadth), 0), TILE)
    first = jnp.concatenate(
        [is_sum_u(row[:TILE], False), is_sum_u(row[TILE:], True)], axis=0
    )
    moved = jnp.concatenate([turn(sum_v[:TILE], 4, 0), turn(sum_v[TILE:], 4, 0)], axis=0)
    spare = starts[:TILE], starts[TILE:]
    for shift, at, total in ((-2, TILE - 2, sum_u), (-1, TILE - 1, sum_v)):
        spare = (
            jnp.where(row[:TILE] == at, turn(total[:TILE], shift, 0), spare[0]),
            jnp.where(
                row[TILE:] == at - TILE + 2, turn(total[TILE:], shift + 3, 0), spare[1]
            ),
        )
    starts = jnp.concatenate(spare, axis=0)
    whole = [depth, starts, jnp.where(first, sum_u, moved)]
    whole += [jnp.concatenate(pair, axis=1) for pair in (strips_u, strips_v, others)]
    for slot, value in enumerate(whole, KMT):
        put(slot, value[:TILE], value[TILE:])
    row = lax.broadcasted_iota(jnp.int32, (TILE, breadth), 0)
    for field, first in ((0, U_ROWS), (1, V_ROWS), (2, T_ROWS)):
        for tile in range(levels // TILE):
            low = high = jnp.zeros((TILE, breadth), F32)
            for q in range(TILE):
                value = ends[field, tile * TILE + q]
                here = row == q
                low = jnp.where(here, turn(value[:TILE], q, 0), low)
                high = jnp.where(here, turn(value[TILE:], q + 1, 0), high)
            put(first + tile, low, high)


def halo_rows(rows_even, rows_odd, first, k):
    tile = first + k // TILE
    north, south = swap(is_even("lat"), rows_even[tile], rows_odd[tile])
    at = lax.rem(k, TILE)
    south = pltpu.roll(south, lax.rem(2 * TILE - 1 - at, TILE), 0)
    north = pltpu.roll(north, lax.rem(TILE - at, TILE), 0)
    return south, north


def advance_inner(state, kmt, rows_odd, rows_even, flow, tracer, flow_u, flow_v, turning):
    levels, rows_here, breadth = state.shape[1:]
    tall = rows_here + 2 * TILE
    lat_even = is_even("lat")

    def halos(slot):
        north, south = swap(lat_even, rows_even[slot], rows_odd[slot])
        return south, north

    south, north = halos(KMT)
    depth = stacked(south, kmt[...].astype(F32), north)
    beside = around(depth)
    row = lax.broadcasted_iota(jnp.int32, (tall, LANES), 0)
    rotation = rotation_at(row - TILE, rows_here)
    turning[...] = rotation
    half_turn = time_step * rotation[:, :1]
    own = slice(TILE, TILE + rows_here)
    flow_u[...] = jnp.zeros_like(flow_u)
    flow_v[...] = jnp.zeros_like(flow_v)

    def body(k, _):
        level = k.astype(F32)
        wet = depth > level
        count = count_wet(beside, level)
        u_south, u_north = halo_rows(rows_even, rows_odd, U_ROWS, k)
        v_south, v_north = halo_rows(rows_even, rows_odd, V_ROWS, k)
        t_south, t_north = halo_rows(rows_even, rows_odd, T_ROWS, k)
        u = jnp.where(wet, stacked(u_south, state[0, k], u_north), 0.0)
        v = jnp.where(wet, stacked(v_south, state[1, k], v_north), 0.0)
        new_u, new_v = advance_flow(u, v, wet, count, half_turn)
        flow_u[own] += new_u[own]
        flow_v[own] += new_v[own]
        for tile, inner, shift, sign in (
            (slice(0, TILE), slice(TILE, 2 * TILE), -1, 1.0),
            (slice(tall - TILE, tall), slice(tall - 2 * TILE, tall - TILE), 1, -1.0),
        ):
            open_to = turn(jnp.where(wet[inner], 1.0, 0.0), shift, 0)
            across = sign * carry * v[tile]
            for value, flow_sum in ((u, flow_u), (v, flow_v)):
                other = turn(value[inner], shift, 0)
                term = (time_step * viscosity) * (other - open_to * value[tile]) - across * other
                flow_sum[tile] += jnp.where(wet[tile], term, 0.0)
        flow[0, k] = new_u[own]
        flow[1, k] = new_v[own]
        here = state[2, k]
        stack_t = jnp.where(wet, stacked(t_south, here, t_north), 0.0)
        middle = stack_t[own]
        sides = (east_of(middle), west_of(middle), north_of(stack_t)[own], south_of(stack_t)[own])
        change = spread(
            middle, sides, count[own], diffusivity, carry * u[own], carry * v[own]
        )
        above = state[2, jnp.maximum(k - 1, 0)]
        below = state[2, jnp.minimum(k + 1, levels - 1)]
        vertical = (above - here) + jnp.where(depth[own] > level + 1.0, below - here, 0.0)
        tracer[k] = jnp.where(
            wet[own], here + (change + (time_step * vertical_mix) * vertical), 0.0
        )
        return 0

    lax.fori_loop(0, levels, body, 0)
    row = lax.broadcasted_iota(jnp.int32, (tall, breadth), 0)
    outer = (row < TILE - 1) | (row > TILE + rows_here)
    edge = (row == TILE - 1) | (row == TILE + rows_here)
    inner = jnp.zeros((rows_here, breadth), F32)
    sums, spare = halos(SUMS), halos(GUESS)
    for number, flow_sum in enumerate((flow_u, flow_v)):
        further = stacked(turn(sums[0], -4 * number, 0), inner, turn(sums[1], -4 * number, 0))
        next_row = stacked(
            turn(spare[0], -1 - number, 0), inner, turn(spare[1], 2 - number, 0)
        )
        total = flow_sum[...]
        total = jnp.where(edge, total + next_row, total)
        flow_sum[...] = jnp.where(outer, further, total)


def fill_ends(x, west, east):
    lane = lane_of((x.shape[0], LANES))
    tiles = [x[:, i : i + LANES] for i in range(0, x.shape[1], LANES)]
    if west is not None:
        tiles[0] = jnp.where(lane == 0, west, tiles[0])
    if east is not None:
        tiles[-1] = jnp.where(lane == LANES - 1, east, tiles[-1])
    return jnp.concatenate(tiles, axis=1)


def roll_to(x, source, target, k):
    return turn(x, target - source - TILE * k, 1)


def krylov(
    sent_even, sent_odd, got_odd, got_even, flow_u, flow_v, kmt, guess,
    rows_even, rows_odd, turning, own_tracer, edges, basis, moments,
):
    levels = LEVELS
    rows_here, breadth = kmt.shape
    tall = rows_here + 2 * TILE
    lat_even = is_even("lat")
    lon_even = is_even("lon")
    lane = lane_of((tall, LANES))
    place = lax.rem(lane, TILE)
    group = lane // TILE
    level = group.astype(F32)
    own = slice(TILE, TILE + rows_here)
    half_turn = time_step * turning[...]

    def received(slot):
        rows = slice(slot * tall, (slot + 1) * tall)
        from_east, from_west = swap(lon_even, got_even[rows], got_odd[rows])
        return from_west, from_east

    def strips(slot):
        rows = slice(slot * tall, (slot + 1) * tall)
        to_east, to_west = swap(lon_even, sent_even[rows], sent_odd[rows])
        from_west, from_east = received(slot)
        west = jnp.where(place < HALO, from_west, turn(to_west, 4, 1))
        east = jnp.where(place >= TILE - HALO, from_east, turn(to_east, -4, 1))
        return west, east

    u_sides, v_sides, other = [strips(slot) for slot in range(3)]
    from_west, from_east = received(0)
    t_sides = (
        jnp.where(place == HALO - 1, turn(from_west, -1, 1), turn(own_tracer[0], 4, 1)),
        jnp.where(place == TILE - HALO, turn(from_east, 1, 1), turn(own_tracer[1], -4, 1)),
    )
    sums = []
    for side in range(2):
        depth = jnp.where(group == 1, turn(other[side], TILE, 1), other[side])
        wet = depth > level
        count = count_wet(around(depth), level)
        u = jnp.where(wet, u_sides[side], 0.0)
        v = jnp.where(wet, v_sides[side], 0.0)
        new_u, new_v = advance_flow(u, v, wet, count, half_turn)
        here = jnp.where(wet, t_sides[side], 0.0)
        change = spread(here, around(here), count, diffusivity, carry * u, carry * v)
        above = jnp.where(group > 0, turn(here, TILE, 1) - here, 0.0)
        below = jnp.where(depth > level + 1.0, turn(here, -TILE, 1) - here, 0.0)
        new_t = jnp.where(
            wet, here + (change + (time_step * vertical_mix) * (above + below)), 0.0
        )
        edges[side, 0] = new_u[own]
        edges[side, 1] = new_v[own]
        edges[side, 2] = new_t[own]
        sums.append((new_u, new_v))

    def fold(x, step):
        return x + turn(x, step, 1)

    (u_west, v_west), (u_east, v_east) = [
        [fold(x, LANES // 2) for x in side] for side in sums
    ]
    half = lane < LANES // 2
    west = fold(jnp.where(half, u_west, v_west), LANES // 4)
    east = fold(jnp.where(half, u_east, v_east), -LANES // 4)
    quarter = lax.rem(lane // (LANES // 4), 2) == 1
    folded = fold(fold(jnp.where(quarter, west, east), 2 * TILE), TILE)

    def assemble(field, west, west_at, east, east_at, seam):
        west = turn(west, -HALO - west_at, 1)
        east = turn(east, -2 - east_at, 1)
        halo = jnp.where(lane < LANES // 2, east, west)
        tiles = [field[:, i : i + LANES] for i in range(0, breadth, LANES)]
        if seam:
            tiles[0] = jnp.where(lane == 0, west, tiles[0])
            tiles[-1] = jnp.where(lane == LANES - 1, east, tiles[-1])
        return jnp.concatenate(tiles + [halo], axis=1)

    def tall_field(slot, value):
        north, south = swap(lat_even, rows_even[slot], rows_odd[slot])
        return stacked(south, value, north)

    last = LANES // 4 - TILE
    wide_u = assemble(flow_u[...], folded, LANES // 4 + last, folded, last, True)
    wide_v = assemble(flow_v[...], folded, 3 * LANES // 4 + last, folded, LANES // 2 + last, True)
    wet_levels = assemble(
        tall_field(KMT, kmt[...].astype(F32)), other[0], 0, other[1], 0, False
    )
    first = assemble(tall_field(GUESS, guess[...]), other[0], TILE, other[1], TILE, False)

    divergence = 0.5 * (east_of(wide_u) - west_of(wide_u)) + 0.5 * (
        north_of(wide_v) - south_of(wide_v)
    )
    depth = wet_levels * (1.0 / levels)
    ocean = wet_levels > 0.0
    to_east = edge_weight * jnp.minimum(depth, east_of(depth))
    to_north = edge_weight * jnp.minimum(depth, north_of(depth))
    depth_north = north_of(depth)
    to_ne = corner_weight * jnp.minimum(depth, east_of(depth_north))
    to_nw = corner_weight * jnp.minimum(depth, west_of(depth_north))
    to_west = west_of(to_east)
    to_south = south_of(to_north)
    to_sw = south_of(west_of(to_ne))
    to_se = south_of(east_of(to_nw))
    diagonal = storage + (
        (to_east + to_west) + (to_north + to_south) + ((to_ne + to_nw) + (to_se + to_sw))
    )

    def neighbours(x):
        up, down = (north_of(x), south_of(x))
        eastern = to_east * x + to_ne_w * up + to_se_w * down
        western = to_west * x + to_nw_e * up + to_sw_e * down
        return to_north * up + to_south * down + (east_of(eastern) + west_of(western))

    to_ne_w = west_of(to_ne)
    to_se_w = west_of(to_se)
    to_nw_e = east_of(to_nw)
    to_sw_e = east_of(to_sw)
    to_east, to_west = (west_of(to_east), east_of(to_west))

    start = jnp.where(ocean, first, 0.0)
    rhs = jnp.where(ocean, storage * (start - time_step * divergence), 0.0)
    residual = rhs - (diagonal * start - neighbours(start))
    inverse = 1.0 / diagonal
    vectors = [residual * inverse]
    basis[0] = start
    basis[1] = vectors[0]
    for k in range(1, ITERS):
        vectors.append(neighbours(vectors[-1]) * inverse)
        basis[k + 1] = vectors[k]
    last = neighbours(vectors[-1])

    def inner(x):
        return x[own, :breadth]

    weighted = [inner(diagonal * x) for x in vectors] + [inner(last)]
    held = [inner(x) for x in vectors]
    slot = lane_of((TILE, LANES))
    total = jnp.zeros((TILE, LANES), F32)
    for m in range(2 * ITERS):
        product = held[m // 2] * weighted[(m + 1) // 2]
        folded = None
        for i in range(0, rows_here, TILE):
            for j in range(0, breadth, LANES):
                part = product[i : i + TILE, j : j + LANES]
                folded = part if folded is None else folded + part
        total = jnp.where(slot == m, jnp.sum(folded, axis=1, keepdims=True), total)
    moments[...] = jnp.sum(total, axis=0, keepdims=True)


def finish(shares, basis, edges, kmt, flow, tracer, out, pressure, done, held, sems, held_sem):
    levels, rows_here, breadth = tracer.shape
    own = slice(TILE, TILE + rows_here)
    chunks = sems.shape[1]
    size = levels // chunks

    def send(first, last, c):
        part = pl.ds(c * size, size)
        fields = slice(first, last)
        return pltpu.make_async_copy(
            done.at[fields, part], out.at[fields, part], sems.at[first // 2, c]
        )

    def ended(value, field, k):
        return fill_ends(
            value,
            roll_to(edges[0, field], HALO, 0, k),
            roll_to(edges[1, field], 1, LANES - 1, k),
        )

    totals = jnp.sum(shares[...].reshape(-1, TILE, LANES), axis=0)
    for step in (1, 2, 4):
        totals = totals + turn(totals, step, 0)
    lane = lane_of((TILE, LANES))

    def everywhere(m):
        one = jnp.sum(jnp.where(lane == m, totals, 0.0), axis=1, keepdims=True)
        return jnp.broadcast_to(one, (TILE, LANES))

    res = [everywhere(m) for m in range(2 * ITERS)]
    dirn = list(res)
    one, zero = (jnp.ones((TILE, LANES), F32), jnp.zeros((TILE, LANES), F32))
    res_in = [one] + [zero] * (ITERS - 1)
    dir_in = list(res_in)
    height_in = [zero] * ITERS
    for k in range(ITERS):
        step = res[k] / (dirn[k] - dirn[k + 1])
        step = jnp.clip(step, 1.0 / HIGHEST, 1.0 / LOWEST)
        height_in = [h + step * d for h, d in zip(height_in, dir_in)]
        if k + 1 < ITERS:
            new = [res[m] - step * (dirn[m] - dirn[m + 1]) for m in range(len(dirn) - 1)]
            ratio = jnp.clip((step * (1.0 / res[k])) * new[k + 1], 0.0, HIGHEST / LOWEST)
            dirn = [n + ratio * d for n, d in zip(new, dirn)]
            res = new
            moved = [zero] + dir_in[:-1]
            res_in = [r - step * (d - m) for r, d, m in zip(res_in, dir_in, moved)]
            dir_in = [r + ratio * d for r, d in zip(res_in, dir_in)]

    for k in range(levels):
        done[2, k] = ended(tracer[k], 2, k)
    for c in range(chunks):
        send(2, 3, c).start()

    def tile_of(i, j):
        cut = slice(i, i + TILE), slice(j, j + LANES)
        value = basis[0, *cut]
        for k in range(ITERS):
            value = value + height_in[k] * basis[k + 1, *cut]
        return value

    tall, wide = basis.shape[1:]
    height = jnp.concatenate(
        [
            jnp.concatenate([tile_of(i, j) for j in range(0, wide, LANES)], axis=1)
            for i in range(0, tall, TILE)
        ],
        axis=0,
    )
    held[...] = gravity * height[own, :breadth]
    pressure_out = pltpu.make_async_copy(held, pressure, held_sem.at[0])
    pressure_out.start()
    pull = 0.5 * time_step * gravity
    slope_east = pull * (east_of(height) - west_of(height))[own, :breadth]
    slope_north = pull * (north_of(height) - south_of(height))[own, :breadth]
    wet_levels = kmt[...]
    for c in range(chunks):
        for k in range(c * size, (c + 1) * size):
            wet = wet_levels > k
            for field, slope in ((0, slope_east), (1, slope_north)):
                done[field, k] = jnp.where(wet, ended(flow[field, k], field, k) - slope, 0.0)
        send(0, 2, c).start()
    pressure_out.wait()
    for c in range(chunks):
        send(2, 3, c).wait()
        send(0, 2, c).wait()


def pairs(axis):
    peers = lax.axis_size(axis)
    even = [(i, i ^ 1) for i in range(peers)]
    odd = [(i, ((i + 1) ^ 1) - 1) for i in range(1, peers - 1)]
    if axis == "lon":
        odd += [(0, peers - 1), (peers - 1, 0)]
    return even, odd


def exchange(axis, to_even, to_odd):
    even, odd = pairs(axis)
    from_odd = lax.ppermute(to_odd, axis, odd)
    return lax.ppermute(to_even, axis, even), from_odd


def on_device(state, kmt, first_guess):
    _, levels, rows_here, breadth = state.shape
    tall = rows_here + 2 * TILE
    wide = breadth + LANES
    shape = lambda *dims: jax.ShapeDtypeStruct(dims, F32)

    devices = lax.axis_size("lon") * lax.axis_size("lat")
    hbm = pl.BlockSpec(memory_space=pltpu.HBM)
    vmem = pl.BlockSpec(memory_space=pltpu.VMEM)
    to_odd, to_even = pl.pallas_call(
        pack_rows,
        in_specs=[hbm] * 3,
        out_specs=[vmem] * 2,
        out_shape=[pltpu.VMEM((SLOTS, TILE, breadth), F32)] * 2,
        scratch_shapes=[
            pltpu.VMEM((3, levels, 2 * TILE, breadth), F32),
            pltpu.VMEM((2 * TILE, breadth), jnp.int32),
            pltpu.VMEM((2 * TILE, breadth), F32),
            pltpu.SemaphoreType.DMA((12,)),
        ],
        compiler_params=params(VMEM_FIRST),
    )(state, kmt, first_guess)
    rows_even, rows_odd = exchange("lat", to_even, to_odd)

    strips = pl.pallas_call(
        pack_own,
        out_shape=shape(2, 4, rows_here, LANES),
        compiler_params=params(),
        cost_estimate=cost(state.size),
    )(state, kmt, first_guess)
    length = 3 * tall
    sent_odd, sent_even, own_tracer = pl.pallas_call(
        pack_cols,
        out_shape=[shape(length, LANES)] * 2 + [shape(2, tall, LANES)],
        compiler_params=params(),
    )(strips, rows_odd, rows_even)
    got_even, got_odd = exchange("lon", sent_even, sent_odd)

    flow, tracer, flow_u, flow_v, turning = pl.pallas_call(
        advance_inner,
        out_shape=[
            shape(2, levels, rows_here, breadth),
            shape(levels, rows_here, breadth),
            shape(tall, breadth),
            shape(tall, breadth),
            shape(tall, LANES),
        ],
        compiler_params=params(),
        cost_estimate=cost(state.size),
    )(state, kmt, rows_odd, rows_even)

    edges, basis, moments = pl.pallas_call(
        krylov,
        out_shape=[
            shape(2, 3, rows_here, LANES),
            shape(ITERS + 1, tall, wide),
            shape(1, LANES),
        ],
        compiler_params=params(),
    )(
        sent_even, sent_odd, got_odd, got_even, flow_u, flow_v, kmt, first_guess,
        rows_even, rows_odd, turning, own_tracer,
    )

    shares = jnp.broadcast_to(moments[None], (devices, 1, LANES))
    shares = lax.all_to_all(shares, ("lon", "lat"), 0, 0)
    return pl.pallas_call(
        finish,
        in_specs=[vmem] * 6,
        out_specs=[hbm, hbm],
        out_shape=[shape(3, levels, rows_here, breadth), shape(rows_here, breadth)],
        scratch_shapes=[
            pltpu.VMEM((3, levels, rows_here, breadth), F32),
            pltpu.VMEM((rows_here, breadth), F32),
            pltpu.SemaphoreType.DMA((2, 4)),
            pltpu.SemaphoreType.DMA((1,)),
        ],
        compiler_params=params(),
    )(shares.reshape(devices, LANES), basis, edges, kmt, flow, tracer)


def solution(mesh):
    placed = (P(None, None, "lat", "lon"), P("lat", "lon"), P("lat", "lon"))
    return jax.shard_map(
        on_device,
        mesh=mesh,
        in_specs=placed,
        out_specs=(P(None, None, "lat", "lon"), P("lat", "lon")),
        check_vma=False,
    )
```

```python
import jax
import jax.numpy as jnp
from jax import lax
from jax.experimental import pallas as pl
from jax.experimental.pallas import tpu as pltpu
from jax.sharding import PartitionSpec as P

ITERS = 4
F32 = jnp.float32

viscosity = 0.12
diffusivity = 0.1
advection_scale = 0.5
vertical_mix = 0.2
coriolis_scale = 0.6
time_step = 0.5
storage = 0.5
gravity = 1.5
edge_weight = 2.0 / 3.0
corner_weight = 1.0 / 6.0

TILE = 8
LANES = 128
LEVELS = LANES // TILE
HALO = 6

U_ROWS = 0
V_ROWS = U_ROWS + LEVELS // TILE
T_ROWS = V_ROWS + LEVELS // TILE
KMT, GUESS, SUMS, STRIPS = range(T_ROWS + LEVELS // TILE, T_ROWS + LEVELS // TILE + 4)
SLOTS = STRIPS + 3

LOWEST = storage / (storage + 4 * edge_weight + 4 * corner_weight)
HIGHEST = 2.0 - LOWEST
VMEM_LIMIT = 16 * 1024 * 1024
VMEM_FIRST = 64520000


def params(limit=VMEM_LIMIT):
    return pltpu.CompilerParams(vmem_limit_bytes=limit)


def cost(size):
    return pl.CostEstimate(flops=60 * size, bytes_accessed=8 * size, transcendentals=0)


def turn(x, shift, axis):
    return pltpu.roll(x, shift % x.shape[axis], axis)


def east_of(x):
    return turn(x, -1, 1)


def west_of(x):
    return turn(x, 1, 1)


def north_of(x):
    return turn(x, -1, 0)


def south_of(x):
    return turn(x, 1, 0)


def lane_of(shape):
    return lax.broadcasted_iota(jnp.int32, shape, len(shape) - 1)


def is_even(axis):
    return lax.rem(lax.axis_index(axis), 2) == 0


def swap(first, a, b):
    return jnp.where(first, a, b), jnp.where(first, b, a)


def stacked(south, own, north):
    return jnp.concatenate([south, own, north], axis=0)


def place(group, k, west, east, acc):
    to_west, to_east = acc
    to_west = jnp.where(group == k, pltpu.roll(west, 2 + TILE * k, 1), to_west)
    to_east = jnp.where(
        group == k, pltpu.roll(east, lax.rem(HALO + TILE * k, LANES), 1), to_east
    )
    return to_west, to_east


def over_groups(x):
    for step in (TILE, 2 * TILE, 4 * TILE, 8 * TILE):
        x = x + pltpu.roll(x, step, 1)
    return x


def pack_others(group, wet, guess, cut):
    blank = (jnp.zeros_like(wet[:, cut[0]]),) * 2
    wet = place(group, jnp.int32(0), wet[:, cut[0]], wet[:, cut[1]], blank)
    wet = tuple(over_groups(x) for x in wet)
    return place(group, jnp.int32(1), guess[:, cut[0]], guess[:, cut[1]], wet)


def pack_own(state, kmt, guess, strips):
    levels, rows_here, breadth = state.shape[1:]
    group = lane_of((rows_here, LANES)) // TILE
    ends = slice(0, LANES), slice(breadth - LANES, breadth)
    blank = (jnp.zeros((rows_here, LANES), F32),) * 2
    for field in range(3):

        def body(k, acc, field=field):
            west, east = [state[field, k, :, cols] for cols in ends]
            return place(group, k, west, east, acc)

        acc = lax.fori_loop(0, levels, body, blank, unroll=4)
        strips[0, field], strips[1, field] = acc
    slot = lax.rem(lane_of((rows_here, LANES)), TILE)
    strips[0, 0] = jnp.where(slot == 1, turn(strips[0, 2], -1, 1), strips[0, 0])
    strips[1, 0] = jnp.where(slot == HALO, turn(strips[1, 2], 1, 1), strips[1, 0])
    strips[0, 3], strips[1, 3] = pack_others(group, kmt[...].astype(F32), guess[...], ends)


def pack_cols(strips, rows_odd, rows_even, msg_odd, msg_even, own_tracer):
    tall = strips.shape[2] + 2 * TILE
    lat_even = is_even("lat")
    lon_even = is_even("lon")

    def tall_strips(field, south, north):
        return [
            stacked(
                south[:, i * LANES : (i + 1) * LANES],
                strips[i, field],
                north[:, i * LANES : (i + 1) * LANES],
            )
            for i in range(2)
        ]

    def put(number, field, south, north):
        base = number * tall
        to_west, to_east = tall_strips(field, south, north)
        a, b = swap(lon_even, to_east, to_west)
        msg_even[base : base + tall] = a
        msg_odd[base : base + tall] = b

    halos = []
    for slot in range(STRIPS, SLOTS):
        north, south = swap(lat_even, rows_even[slot], rows_odd[slot])
        halos.append((south, north))
    put(0, 0, *halos[0])
    put(1, 1, *halos[1])
    put(2, 3, *halos[2])
    own_tracer[0], own_tracer[1] = tall_strips(
        2, turn(halos[0][0], -1, 0), turn(halos[0][1], 1, 0)
    )


def rotation_at(row, rows_here):
    total_rows = rows_here * lax.axis_size("lat")
    row = (row + lax.axis_index("lat") * rows_here).astype(F32)
    angle = jnp.pi / 180.0 * (-80.0 + 160.0 * (row + 0.5) / total_rows)
    return coriolis_scale * jnp.sin(angle)


def around(x):
    return east_of(x), west_of(x), north_of(x), south_of(x)


def count_wet(sides, level):
    total = None
    for side in sides:
        term = jnp.where(side > level, 1.0, 0.0)
        total = term if total is None else total + term
    return total


def spread(x, sides, count, coefficient, zonal, merid):
    east, west, north, south = sides
    laplace = east + west + north + south - count * x
    return (
        (time_step * coefficient) * laplace
        - zonal * (east - west)
        - merid * (north - south)
    )


carry = 0.5 * time_step * advection_scale


def advance_flow(u, v, wet, count, half_turn, around=around):
    zonal, merid = (carry * u, carry * v)
    new_u = u + (spread(u, around(u), count, viscosity, zonal, merid) + half_turn * v)
    new_v = v + (spread(v, around(v), count, viscosity, zonal, merid) - half_turn * u)
    return jnp.where(wet, new_u, 0.0), jnp.where(wet, new_v, 0.0)


def is_sum_u(row, southern):
    first = TILE - 5 if southern else 1
    return (row >= first) & (row < first + 4)


def pack_rows(state, kmt, guess, msg_odd, msg_even, ends, wet_ends, guess_ends, sems):
    levels, rows_here, breadth = state.shape[1:]
    even = is_even("lat")
    parts = [slice(k, k + levels // 4) for k in range(0, levels, levels // 4)]
    copies = []
    for part in [None] + parts:
        copies.append([])
        for number, rows in enumerate((slice(0, TILE), slice(rows_here - TILE, rows_here))):
            held = slice(number * TILE, (number + 1) * TILE)
            if part is not None:
                pairs_of_refs = [(state.at[:, part, rows, :], ends.at[:, part, held, :])]
            else:
                pairs_of_refs = [
                    (kmt.at[rows, :], wet_ends.at[held, :]),
                    (guess.at[rows, :], guess_ends.at[held, :]),
                ]
            for source, target in pairs_of_refs:
                item = pltpu.make_async_copy(source, target, sems.at[sum(map(len, copies))])
                item.start()
                copies[-1].append(item)
    row = lax.broadcasted_iota(jnp.int32, (2 * TILE, LANES), 0)
    rotation = rotation_at(jnp.where(row < TILE, row, row + rows_here - 2 * TILE), rows_here)
    half_turn = time_step * rotation[:, :1]
    group = lane_of((2 * TILE, LANES)) // TILE
    row = lax.broadcasted_iota(jnp.int32, (2 * TILE, breadth), 0)
    borrowed = (row == TILE - 1) | (row == TILE)
    for item in copies[0]:
        item.wait()

    top = row == 2 * TILE - 1

    def within(x):
        east, west, north, south = around(x)
        return east, west, jnp.where(top, 0.0, north), jnp.where(row == 0, 0.0, south)

    depth = wet_ends[...].astype(F32)
    beside = within(depth)
    cut = slice(0, LANES), slice(breadth - LANES, breadth)
    starts = guess_ends[...]
    others = pack_others(group, depth, starts, cut)

    def body(k, carried):
        sum_u, sum_v, strips_u, strips_v = carried
        level = k.astype(F32)
        wet = depth > level
        raw_u, raw_v, raw_t = [ends[field, k] for field in range(3)]
        u = jnp.where(wet, raw_u, 0.0)
        v = jnp.where(wet, raw_v, 0.0)
        new_u, new_v = advance_flow(
            u, v, wet, count_wet(beside, level), half_turn, within
        )
        moved = jnp.concatenate([turn(raw_t[:TILE], -1, 0), turn(raw_t[TILE:], 1, 0)], axis=0)
        lent = jnp.where(borrowed, moved, raw_u)
        strips_u = place(group, k, lent[:, cut[0]], lent[:, cut[1]], strips_u)
        strips_v = place(group, k, raw_v[:, cut[0]], raw_v[:, cut[1]], strips_v)
        return sum_u + new_u, sum_v + new_v, strips_u, strips_v

    empty = jnp.zeros((2 * TILE, breadth), F32)
    blank = (jnp.zeros((2 * TILE, LANES), F32),) * 2
    carried = (empty, empty, blank, blank)
    for part, items in zip(parts, copies[1:]):
        for item in items:
            item.wait()
        carried = lax.fori_loop(part.start, part.stop, body, carried, unroll=4)
    sum_u, sum_v, strips_u, strips_v = carried

    def put(slot, low, high):
        a, b = swap(even, high, low)
        msg_even[slot] = a
        msg_odd[slot] = b

    row = lax.rem(lax.broadcasted_iota(jnp.int32, (2 * TILE, breadth), 0), TILE)
    first = jnp.concatenate(
        [is_sum_u(row[:TILE], False), is_sum_u(row[TILE:], True)], axis=0
    )
    moved = jnp.concatenate([turn(sum_v[:TILE], 4, 0), turn(sum_v[TILE:], 4, 0)], axis=0)
    spare = starts[:TILE], starts[TILE:]
    for shift, at, total in ((-2, TILE - 2, sum_u), (-1, TILE - 1, sum_v)):
        spare = (
            jnp.where(row[:TILE] == at, turn(total[:TILE], shift, 0), spare[0]),
            jnp.where(
                row[TILE:] == at - TILE + 2, turn(total[TILE:], shift + 3, 0), spare[1]
            ),
        )
    starts = jnp.concatenate(spare, axis=0)
    whole = [depth, starts, jnp.where(first, sum_u, moved)]
    whole += [jnp.concatenate(pair, axis=1) for pair in (strips_u, strips_v, others)]
    for slot, value in enumerate(whole, KMT):
        put(slot, value[:TILE], value[TILE:])
    row = lax.broadcasted_iota(jnp.int32, (TILE, breadth), 0)
    for field, first in ((0, U_ROWS), (1, V_ROWS), (2, T_ROWS)):
        for tile in range(levels // TILE):
            low = high = jnp.zeros((TILE, breadth), F32)
            for q in range(TILE):
                value = ends[field, tile * TILE + q]
                here = row == q
                low = jnp.where(here, turn(value[:TILE], q, 0), low)
                high = jnp.where(here, turn(value[TILE:], q + 1, 0), high)
            put(first + tile, low, high)


def halo_rows(rows_even, rows_odd, first, k):
    tile = first + k // TILE
    north, south = swap(is_even("lat"), rows_even[tile], rows_odd[tile])
    at = lax.rem(k, TILE)
    south = pltpu.roll(south, lax.rem(2 * TILE - 1 - at, TILE), 0)
    north = pltpu.roll(north, lax.rem(TILE - at, TILE), 0)
    return south, north


def advance_inner(state, kmt, rows_odd, rows_even, flow, tracer, flow_u, flow_v, turning):
    levels, rows_here, breadth = state.shape[1:]
    tall = rows_here + 2 * TILE
    lat_even = is_even("lat")

    def halos(slot):
        north, south = swap(lat_even, rows_even[slot], rows_odd[slot])
        return south, north

    south, north = halos(KMT)
    depth = stacked(south, kmt[...].astype(F32), north)
    beside = around(depth)
    row = lax.broadcasted_iota(jnp.int32, (tall, LANES), 0)
    rotation = rotation_at(row - TILE, rows_here)
    turning[...] = rotation
    half_turn = time_step * rotation[:, :1]
    own = slice(TILE, TILE + rows_here)
    flow_u[...] = jnp.zeros_like(flow_u)
    flow_v[...] = jnp.zeros_like(flow_v)

    def body(k, _):
        level = k.astype(F32)
        wet = depth > level
        count = count_wet(beside, level)
        u_south, u_north = halo_rows(rows_even, rows_odd, U_ROWS, k)
        v_south, v_north = halo_rows(rows_even, rows_odd, V_ROWS, k)
        t_south, t_north = halo_rows(rows_even, rows_odd, T_ROWS, k)
        u = jnp.where(wet, stacked(u_south, state[0, k], u_north), 0.0)
        v = jnp.where(wet, stacked(v_south, state[1, k], v_north), 0.0)
        new_u, new_v = advance_flow(u, v, wet, count, half_turn)
        flow_u[own] += new_u[own]
        flow_v[own] += new_v[own]
        for tile, inner, shift, sign in (
            (slice(0, TILE), slice(TILE, 2 * TILE), -1, 1.0),
            (slice(tall - TILE, tall), slice(tall - 2 * TILE, tall - TILE), 1, -1.0),
        ):
            open_to = turn(jnp.where(wet[inner], 1.0, 0.0), shift, 0)
            across = sign * carry * v[tile]
            for value, flow_sum in ((u, flow_u), (v, flow_v)):
                other = turn(value[inner], shift, 0)
                term = (time_step * viscosity) * (other - open_to * value[tile]) - across * other
                flow_sum[tile] += jnp.where(wet[tile], term, 0.0)
        flow[0, k] = new_u[own]
        flow[1, k] = new_v[own]
        here = state[2, k]
        stack_t = jnp.where(wet, stacked(t_south, here, t_north), 0.0)
        middle = stack_t[own]
        sides = (east_of(middle), west_of(middle), north_of(stack_t)[own], south_of(stack_t)[own])
        change = spread(
            middle, sides, count[own], diffusivity, carry * u[own], carry * v[own]
        )
        above = state[2, jnp.maximum(k - 1, 0)]
        below = state[2, jnp.minimum(k + 1, levels - 1)]
        vertical = (above - here) + jnp.where(depth[own] > level + 1.0, below - here, 0.0)
        tracer[k] = jnp.where(
            wet[own], here + (change + (time_step * vertical_mix) * vertical), 0.0
        )
        return 0

    lax.fori_loop(0, levels, body, 0)
    row = lax.broadcasted_iota(jnp.int32, (tall, breadth), 0)
    outer = (row < TILE - 1) | (row > TILE + rows_here)
    edge = (row == TILE - 1) | (row == TILE + rows_here)
    inner = jnp.zeros((rows_here, breadth), F32)
    sums, spare = halos(SUMS), halos(GUESS)
    for number, flow_sum in enumerate((flow_u, flow_v)):
        further = stacked(turn(sums[0], -4 * number, 0), inner, turn(sums[1], -4 * number, 0))
        next_row = stacked(
            turn(spare[0], -1 - number, 0), inner, turn(spare[1], 2 - number, 0)
        )
        total = flow_sum[...]
        total = jnp.where(edge, total + next_row, total)
        flow_sum[...] = jnp.where(outer, further, total)


def fill_ends(x, west, east):
    lane = lane_of((x.shape[0], LANES))
    tiles = [x[:, i : i + LANES] for i in range(0, x.shape[1], LANES)]
    if west is not None:
        tiles[0] = jnp.where(lane == 0, west, tiles[0])
    if east is not None:
        tiles[-1] = jnp.where(lane == LANES - 1, east, tiles[-1])
    return jnp.concatenate(tiles, axis=1)


def roll_to(x, source, target, k):
    return turn(x, target - source - TILE * k, 1)


def krylov(
    sent_even, sent_odd, got_odd, got_even, flow_u, flow_v, kmt, guess,
    rows_even, rows_odd, turning, own_tracer, edges, basis, moments,
):
    levels = LEVELS
    rows_here, breadth = kmt.shape
    tall = rows_here + 2 * TILE
    lat_even = is_even("lat")
    lon_even = is_even("lon")
    lane = lane_of((tall, LANES))
    place = lax.rem(lane, TILE)
    group = lane // TILE
    level = group.astype(F32)
    own = slice(TILE, TILE + rows_here)
    half_turn = time_step * turning[...]

    def received(slot):
        rows = slice(slot * tall, (slot + 1) * tall)
        from_east, from_west = swap(lon_even, got_even[rows], got_odd[rows])
        return from_west, from_east

    def strips(slot):
        rows = slice(slot * tall, (slot + 1) * tall)
        to_east, to_west = swap(lon_even, sent_even[rows], sent_odd[rows])
        from_west, from_east = received(slot)
        west = jnp.where(place < HALO, from_west, turn(to_west, 4, 1))
        east = jnp.where(place >= TILE - HALO, from_east, turn(to_east, -4, 1))
        return west, east

    u_sides, v_sides, other = [strips(slot) for slot in range(3)]
    from_west, from_east = received(0)
    t_sides = (
        jnp.where(place == HALO - 1, turn(from_west, -1, 1), turn(own_tracer[0], 4, 1)),
        jnp.where(place == TILE - HALO, turn(from_east, 1, 1), turn(own_tracer[1], -4, 1)),
    )
    sums = []
    for side in range(2):
        depth = jnp.where(group == 1, turn(other[side], TILE, 1), other[side])
        wet = depth > level
        count = count_wet(around(depth), level)
        u = jnp.where(wet, u_sides[side], 0.0)
        v = jnp.where(wet, v_sides[side], 0.0)
        new_u, new_v = advance_flow(u, v, wet, count, half_turn)
        here = jnp.where(wet, t_sides[side], 0.0)
        change = spread(here, around(here), count, diffusivity, carry * u, carry * v)
        above = jnp.where(group > 0, turn(here, TILE, 1) - here, 0.0)
        below = jnp.where(depth > level + 1.0, turn(here, -TILE, 1) - here, 0.0)
        new_t = jnp.where(
            wet, here + (change + (time_step * vertical_mix) * (above + below)), 0.0
        )
        edges[side, 0] = new_u[own]
        edges[side, 1] = new_v[own]
        edges[side, 2] = new_t[own]
        sums.append((new_u, new_v))

    def fold(x, step):
        return x + turn(x, step, 1)

    (u_west, v_west), (u_east, v_east) = [
        [fold(x, LANES // 2) for x in side] for side in sums
    ]
    half = lane < LANES // 2
    west = fold(jnp.where(half, u_west, v_west), LANES // 4)
    east = fold(jnp.where(half, u_east, v_east), -LANES // 4)
    quarter = lax.rem(lane // (LANES // 4), 2) == 1
    folded = fold(fold(jnp.where(quarter, west, east), 2 * TILE), TILE)

    def assemble(field, west, west_at, east, east_at, seam):
        west = turn(west, -HALO - west_at, 1)
        east = turn(east, -2 - east_at, 1)
        halo = jnp.where(lane < LANES // 2, east, west)
        tiles = [field[:, i : i + LANES] for i in range(0, breadth, LANES)]
        if seam:
            tiles[0] = jnp.where(lane == 0, west, tiles[0])
            tiles[-1] = jnp.where(lane == LANES - 1, east, tiles[-1])
        return jnp.concatenate(tiles + [halo], axis=1)

    def tall_field(slot, value):
        north, south = swap(lat_even, rows_even[slot], rows_odd[slot])
        return stacked(south, value, north)

    last = LANES // 4 - TILE
    wide_u = assemble(flow_u[...], folded, LANES // 4 + last, folded, last, True)
    wide_v = assemble(flow_v[...], folded, 3 * LANES // 4 + last, folded, LANES // 2 + last, True)
    wet_levels = assemble(
        tall_field(KMT, kmt[...].astype(F32)), other[0], 0, other[1], 0, False
    )
    first = assemble(tall_field(GUESS, guess[...]), other[0], TILE, other[1], TILE, False)

    divergence = 0.5 * (east_of(wide_u) - west_of(wide_u)) + 0.5 * (
        north_of(wide_v) - south_of(wide_v)
    )
    depth = wet_levels * (1.0 / levels)
    ocean = wet_levels > 0.0
    to_east = edge_weight * jnp.minimum(depth, east_of(depth))
    to_north = edge_weight * jnp.minimum(depth, north_of(depth))
    depth_north = north_of(depth)
    to_ne = corner_weight * jnp.minimum(depth, east_of(depth_north))
    to_nw = corner_weight * jnp.minimum(depth, west_of(depth_north))
    to_west = west_of(to_east)
    to_south = south_of(to_north)
    to_sw = south_of(west_of(to_ne))
    to_se = south_of(east_of(to_nw))
    diagonal = storage + (
        (to_east + to_west) + (to_north + to_south) + ((to_ne + to_nw) + (to_se + to_sw))
    )

    def neighbours(x):
        up, down = (north_of(x), south_of(x))
        eastern = to_east * x + to_ne_w * up + to_se_w * down
        western = to_west * x + to_nw_e * up + to_sw_e * down
        return to_north * up + to_south * down + (east_of(eastern) + west_of(western))

    to_ne_w = west_of(to_ne)
    to_se_w = west_of(to_se)
    to_nw_e = east_of(to_nw)
    to_sw_e = east_of(to_sw)
    to_east, to_west = (west_of(to_east), east_of(to_west))

    start = jnp.where(ocean, first, 0.0)
    rhs = jnp.where(ocean, storage * (start - time_step * divergence), 0.0)
    residual = rhs - (diagonal * start - neighbours(start))
    inverse = 1.0 / diagonal
    vectors = [residual * inverse]
    basis[0] = start
    basis[1] = vectors[0]
    for k in range(1, ITERS):
        vectors.append(neighbours(vectors[-1]) * inverse)
        basis[k + 1] = vectors[k]
    last = neighbours(vectors[-1])

    def inner(x):
        return x[own, :breadth]

    weighted = [inner(diagonal * x) for x in vectors] + [inner(last)]
    held = [inner(x) for x in vectors]
    slot = lane_of((TILE, LANES))
    total = jnp.zeros((TILE, LANES), F32)
    for m in range(2 * ITERS):
        product = held[m // 2] * weighted[(m + 1) // 2]
        folded = None
        for i in range(0, rows_here, TILE):
            for j in range(0, breadth, LANES):
                part = product[i : i + TILE, j : j + LANES]
                folded = part if folded is None else folded + part
        total = jnp.where(slot == m, jnp.sum(folded, axis=1, keepdims=True), total)
    moments[...] = jnp.sum(total, axis=0, keepdims=True)


def over(a, b):
    return a / jnp.where(b > 1e-37, b, 1.0)


def finish(shares, basis, edges, kmt, flow, tracer, out, pressure, done, held, sems, held_sem):
    levels, rows_here, breadth = tracer.shape
    own = slice(TILE, TILE + rows_here)
    chunks = sems.shape[1]
    size = levels // chunks

    def send(first, last, c):
        part = pl.ds(c * size, size)
        fields = slice(first, last)
        return pltpu.make_async_copy(
            done.at[fields, part], out.at[fields, part], sems.at[first // 2, c]
        )

    def ended(value, field, k):
        return fill_ends(
            value,
            roll_to(edges[0, field], HALO, 0, k),
            roll_to(edges[1, field], 1, LANES - 1, k),
        )

    totals = jnp.sum(shares[...].reshape(-1, TILE, LANES), axis=0)
    for step in (1, 2, 4):
        totals = totals + turn(totals, step, 0)
    lane = lane_of((TILE, LANES))

    def everywhere(m):
        one = jnp.sum(jnp.where(lane == m, totals, 0.0), axis=1, keepdims=True)
        return jnp.broadcast_to(one, (TILE, LANES))

    res = [everywhere(m) for m in range(2 * ITERS)]
    dirn = list(res)
    one, zero = (jnp.ones((TILE, LANES), F32), jnp.zeros((TILE, LANES), F32))
    res_in = [one] + [zero] * (ITERS - 1)
    dir_in = list(res_in)
    height_in = [zero] * ITERS
    for k in range(ITERS):
        step = over(res[k], dirn[k] - dirn[k + 1])
        step = jnp.clip(step, 1.0 / HIGHEST, 1.0 / LOWEST)
        height_in = [h + step * d for h, d in zip(height_in, dir_in)]
        if k + 1 < ITERS:
            new = [res[m] - step * (dirn[m] - dirn[m + 1]) for m in range(len(dirn) - 1)]
            ratio = jnp.clip(over(step, res[k]) * new[k + 1], 0.0, HIGHEST / LOWEST)
            dirn = [n + ratio * d for n, d in zip(new, dirn)]
            res = new
            moved = [zero] + dir_in[:-1]
            res_in = [r - step * (d - m) for r, d, m in zip(res_in, dir_in, moved)]
            dir_in = [r + ratio * d for r, d in zip(res_in, dir_in)]

    for k in range(levels):
        done[2, k] = ended(tracer[k], 2, k)
    for c in range(chunks):
        send(2, 3, c).start()

    def tile_of(i, j):
        cut = slice(i, i + TILE), slice(j, j + LANES)
        value = basis[0, *cut]
        for k in range(ITERS):
            value = value + height_in[k] * basis[k + 1, *cut]
        return value

    tall, wide = basis.shape[1:]
    height = jnp.concatenate(
        [
            jnp.concatenate([tile_of(i, j) for j in range(0, wide, LANES)], axis=1)
            for i in range(0, tall, TILE)
        ],
        axis=0,
    )
    held[...] = gravity * height[own, :breadth]
    pressure_out = pltpu.make_async_copy(held, pressure, held_sem.at[0])
    pressure_out.start()
    pull = 0.5 * time_step * gravity
    slope_east = pull * (east_of(height) - west_of(height))[own, :breadth]
    slope_north = pull * (north_of(height) - south_of(height))[own, :breadth]
    wet_levels = kmt[...]
    for c in range(chunks):
        for k in range(c * size, (c + 1) * size):
            wet = wet_levels > k
            for field, slope in ((0, slope_east), (1, slope_north)):
                done[field, k] = jnp.where(wet, ended(flow[field, k], field, k) - slope, 0.0)
        send(0, 2, c).start()
    pressure_out.wait()
    for c in range(chunks):
        send(2, 3, c).wait()
        send(0, 2, c).wait()


def pairs(axis):
    peers = lax.axis_size(axis)
    even = [(i, i ^ 1) for i in range(peers)]
    odd = [(i, ((i + 1) ^ 1) - 1) for i in range(1, peers - 1)]
    if axis == "lon":
        odd += [(0, peers - 1), (peers - 1, 0)]
    return even, odd


def exchange(axis, to_even, to_odd):
    even, odd = pairs(axis)
    from_odd = lax.ppermute(to_odd, axis, odd)
    return lax.ppermute(to_even, axis, even), from_odd


def on_device(state, kmt, first_guess):
    _, levels, rows_here, breadth = state.shape
    tall = rows_here + 2 * TILE
    wide = breadth + LANES
    shape = lambda *dims: jax.ShapeDtypeStruct(dims, F32)

    devices = lax.axis_size("lon") * lax.axis_size("lat")
    hbm = pl.BlockSpec(memory_space=pltpu.HBM)
    vmem = pl.BlockSpec(memory_space=pltpu.VMEM)
    to_odd, to_even = pl.pallas_call(
        pack_rows,
        in_specs=[hbm] * 3,
        out_specs=[vmem] * 2,
        out_shape=[pltpu.VMEM((SLOTS, TILE, breadth), F32)] * 2,
        scratch_shapes=[
            pltpu.VMEM((3, levels, 2 * TILE, breadth), F32),
            pltpu.VMEM((2 * TILE, breadth), jnp.int32),
            pltpu.VMEM((2 * TILE, breadth), F32),
            pltpu.SemaphoreType.DMA((12,)),
        ],
        compiler_params=params(VMEM_FIRST),
    )(state, kmt, first_guess)
    rows_even, rows_odd = exchange("lat", to_even, to_odd)

    strips = pl.pallas_call(
        pack_own,
        out_shape=shape(2, 4, rows_here, LANES),
        compiler_params=params(),
        cost_estimate=cost(state.size),
    )(state, kmt, first_guess)
    length = 3 * tall
    sent_odd, sent_even, own_tracer = pl.pallas_call(
        pack_cols,
        out_shape=[shape(length, LANES)] * 2 + [shape(2, tall, LANES)],
        compiler_params=params(),
    )(strips, rows_odd, rows_even)
    got_even, got_odd = exchange("lon", sent_even, sent_odd)

    flow, tracer, flow_u, flow_v, turning = pl.pallas_call(
        advance_inner,
        out_shape=[
            shape(2, levels, rows_here, breadth),
            shape(levels, rows_here, breadth),
            shape(tall, breadth),
            shape(tall, breadth),
            shape(tall, LANES),
        ],
        compiler_params=params(),
        cost_estimate=cost(state.size),
    )(state, kmt, rows_odd, rows_even)

    edges, basis, moments = pl.pallas_call(
        krylov,
        out_shape=[
            shape(2, 3, rows_here, LANES),
            shape(ITERS + 1, tall, wide),
            shape(1, LANES),
        ],
        compiler_params=params(),
    )(
        sent_even, sent_odd, got_odd, got_even, flow_u, flow_v, kmt, first_guess,
        rows_even, rows_odd, turning, own_tracer,
    )

    shares = jnp.broadcast_to(moments[None], (devices, 1, LANES))
    shares = lax.all_to_all(shares, ("lon", "lat"), 0, 0)
    return pl.pallas_call(
        finish,
        in_specs=[vmem] * 6,
        out_specs=[hbm, hbm],
        out_shape=[shape(3, levels, rows_here, breadth), shape(rows_here, breadth)],
        scratch_shapes=[
            pltpu.VMEM((3, levels, rows_here, breadth), F32),
            pltpu.VMEM((rows_here, breadth), F32),
            pltpu.SemaphoreType.DMA((2, 4)),
            pltpu.SemaphoreType.DMA((1,)),
        ],
        compiler_params=params(),
    )(shares.reshape(devices, LANES), basis, edges, kmt, flow, tracer)


def solution(mesh):
    placed = (P(None, None, "lat", "lon"), P("lat", "lon"), P("lat", "lon"))
    return jax.shard_map(
        on_device,
        mesh=mesh,
        in_specs=placed,
        out_specs=(P(None, None, "lat", "lon"), P("lat", "lon")),
        check_vma=False,
    )
```

```python
import jax
import jax.numpy as jnp
from jax import lax
from jax.experimental import pallas as pl
from jax.experimental.pallas import tpu as pltpu
from jax.sharding import PartitionSpec as P

ITERS = 4
F32 = jnp.float32

viscosity = 0.12
diffusivity = 0.1
advection_scale = 0.5
vertical_mix = 0.2
coriolis_scale = 0.6
time_step = 0.5
storage = 0.5
gravity = 1.5
edge_weight = 2.0 / 3.0
corner_weight = 1.0 / 6.0

TILE = 8
LANES = 128
LEVELS = LANES // TILE
HALO = 6

U_ROWS = 0
V_ROWS = U_ROWS + LEVELS // TILE
T_ROWS = V_ROWS + LEVELS // TILE
KMT, GUESS, SUMS, STRIPS = range(T_ROWS + LEVELS // TILE, T_ROWS + LEVELS // TILE + 4)
SLOTS = STRIPS + 3

LOWEST = storage / (storage + 4 * edge_weight + 4 * corner_weight)
HIGHEST = 2.0 - LOWEST
VMEM_LIMIT = 16 * 1024 * 1024
VMEM_FIRST = 64520000
VMEM_OWN = 60000000


def params(limit=VMEM_LIMIT):
    return pltpu.CompilerParams(vmem_limit_bytes=limit)


def cost(size):
    return pl.CostEstimate(flops=60 * size, bytes_accessed=8 * size, transcendentals=0)


def turn(x, shift, axis):
    return pltpu.roll(x, shift % x.shape[axis], axis)


def east_of(x):
    return turn(x, -1, 1)


def west_of(x):
    return turn(x, 1, 1)


def north_of(x):
    return turn(x, -1, 0)


def south_of(x):
    return turn(x, 1, 0)


def lane_of(shape):
    return lax.broadcasted_iota(jnp.int32, shape, len(shape) - 1)


def is_even(axis):
    return lax.rem(lax.axis_index(axis), 2) == 0


def swap(first, a, b):
    return jnp.where(first, a, b), jnp.where(first, b, a)


def stacked(south, own, north):
    return jnp.concatenate([south, own, north], axis=0)


def place(group, k, west, east, acc):
    to_west, to_east = acc
    to_west = jnp.where(group == k, pltpu.roll(west, 2 + TILE * k, 1), to_west)
    to_east = jnp.where(
        group == k, pltpu.roll(east, lax.rem(HALO + TILE * k, LANES), 1), to_east
    )
    return to_west, to_east


def over_groups(x):
    for step in (TILE, 2 * TILE, 4 * TILE, 8 * TILE):
        x = x + pltpu.roll(x, step, 1)
    return x


def pack_others(group, wet, guess, cut):
    blank = (jnp.zeros_like(wet[:, cut[0]]),) * 2
    wet = place(group, jnp.int32(0), wet[:, cut[0]], wet[:, cut[1]], blank)
    wet = tuple(over_groups(x) for x in wet)
    return place(group, jnp.int32(1), guess[:, cut[0]], guess[:, cut[1]], wet)


def pack_own(state_hbm, kmt, guess, state, strips, sems):
    levels, rows_here, breadth = state.shape[1:]
    copies = [
        pltpu.make_async_copy(state_hbm.at[field], state.at[field], sems.at[field])
        for field in range(3)
    ]
    for item in copies:
        item.start()
    group = lane_of((rows_here, LANES)) // TILE
    ends = slice(0, LANES), slice(breadth - LANES, breadth)
    blank = (jnp.zeros((rows_here, LANES), F32),) * 2
    for field in range(3):
        copies[field].wait()

        def body(k, acc, field=field):
            west, east = [state[field, k, :, cols] for cols in ends]
            return place(group, k, west, east, acc)

        acc = lax.fori_loop(0, levels, body, blank, unroll=4)
        strips[0, field], strips[1, field] = acc
    slot = lax.rem(lane_of((rows_here, LANES)), TILE)
    strips[0, 0] = jnp.where(slot == 1, turn(strips[0, 2], -1, 1), strips[0, 0])
    strips[1, 0] = jnp.where(slot == HALO, turn(strips[1, 2], 1, 1), strips[1, 0])
    strips[0, 3], strips[1, 3] = pack_others(group, kmt[...].astype(F32), guess[...], ends)


def pack_cols(strips, rows_odd, rows_even, msg_odd, msg_even, own_tracer):
    tall = strips.shape[2] + 2 * TILE
    lat_even = is_even("lat")
    lon_even = is_even("lon")

    def tall_strips(field, south, north):
        return [
            stacked(
                south[:, i * LANES : (i + 1) * LANES],
                strips[i, field],
                north[:, i * LANES : (i + 1) * LANES],
            )
            for i in range(2)
        ]

    def put(number, field, south, north):
        base = number * tall
        to_west, to_east = tall_strips(field, south, north)
        a, b = swap(lon_even, to_east, to_west)
        msg_even[base : base + tall] = a
        msg_odd[base : base + tall] = b

    halos = []
    for slot in range(STRIPS, SLOTS):
        north, south = swap(lat_even, rows_even[slot], rows_odd[slot])
        halos.append((south, north))
    put(0, 0, *halos[0])
    put(1, 1, *halos[1])
    put(2, 3, *halos[2])
    own_tracer[0], own_tracer[1] = tall_strips(
        2, turn(halos[0][0], -1, 0), turn(halos[0][1], 1, 0)
    )


def rotation_at(row, rows_here):
    total_rows = rows_here * lax.axis_size("lat")
    row = (row + lax.axis_index("lat") * rows_here).astype(F32)
    angle = jnp.pi / 180.0 * (-80.0 + 160.0 * (row + 0.5) / total_rows)
    return coriolis_scale * jnp.sin(angle)


def around(x):
    return east_of(x), west_of(x), north_of(x), south_of(x)


def count_wet(sides, level):
    total = None
    for side in sides:
        term = jnp.where(side > level, 1.0, 0.0)
        total = term if total is None else total + term
    return total


def spread(x, sides, count, coefficient, zonal, merid):
    east, west, north, south = sides
    laplace = east + west + north + south - count * x
    return (
        (time_step * coefficient) * laplace
        - zonal * (east - west)
        - merid * (north - south)
    )


carry = 0.5 * time_step * advection_scale


def advance_flow(u, v, wet, count, half_turn, around=around):
    zonal, merid = (carry * u, carry * v)
    new_u = u + (spread(u, around(u), count, viscosity, zonal, merid) + half_turn * v)
    new_v = v + (spread(v, around(v), count, viscosity, zonal, merid) - half_turn * u)
    return jnp.where(wet, new_u, 0.0), jnp.where(wet, new_v, 0.0)


def is_sum_u(row, southern):
    first = TILE - 5 if southern else 1
    return (row >= first) & (row < first + 4)


def pack_rows(state, kmt, guess, msg_odd, msg_even, ends, wet_ends, guess_ends, sems):
    levels, rows_here, breadth = state.shape[1:]
    even = is_even("lat")
    parts = [slice(k, k + levels // 4) for k in range(0, levels, levels // 4)]
    copies = []
    for part in [None] + parts:
        copies.append([])
        for number, rows in enumerate((slice(0, TILE), slice(rows_here - TILE, rows_here))):
            held = slice(number * TILE, (number + 1) * TILE)
            if part is not None:
                pairs_of_refs = [(state.at[:, part, rows, :], ends.at[:, part, held, :])]
            else:
                pairs_of_refs = [
                    (kmt.at[rows, :], wet_ends.at[held, :]),
                    (guess.at[rows, :], guess_ends.at[held, :]),
                ]
            for source, target in pairs_of_refs:
                item = pltpu.make_async_copy(source, target, sems.at[sum(map(len, copies))])
                item.start()
                copies[-1].append(item)
    row = lax.broadcasted_iota(jnp.int32, (2 * TILE, LANES), 0)
    rotation = rotation_at(jnp.where(row < TILE, row, row + rows_here - 2 * TILE), rows_here)
    half_turn = time_step * rotation[:, :1]
    group = lane_of((2 * TILE, LANES)) // TILE
    row = lax.broadcasted_iota(jnp.int32, (2 * TILE, breadth), 0)
    borrowed = (row == TILE - 1) | (row == TILE)
    for item in copies[0]:
        item.wait()

    top = row == 2 * TILE - 1

    def within(x):
        east, west, north, south = around(x)
        return east, west, jnp.where(top, 0.0, north), jnp.where(row == 0, 0.0, south)

    depth = wet_ends[...].astype(F32)
    beside = within(depth)
    cut = slice(0, LANES), slice(breadth - LANES, breadth)
    starts = guess_ends[...]
    others = pack_others(group, depth, starts, cut)

    def body(k, carried):
        sum_u, sum_v, strips_u, strips_v = carried
        level = k.astype(F32)
        wet = depth > level
        raw_u, raw_v, raw_t = [ends[field, k] for field in range(3)]
        u = jnp.where(wet, raw_u, 0.0)
        v = jnp.where(wet, raw_v, 0.0)
        new_u, new_v = advance_flow(
            u, v, wet, count_wet(beside, level), half_turn, within
        )
        moved = jnp.concatenate([turn(raw_t[:TILE], -1, 0), turn(raw_t[TILE:], 1, 0)], axis=0)
        lent = jnp.where(borrowed, moved, raw_u)
        strips_u = place(group, k, lent[:, cut[0]], lent[:, cut[1]], strips_u)
        strips_v = place(group, k, raw_v[:, cut[0]], raw_v[:, cut[1]], strips_v)
        return sum_u + new_u, sum_v + new_v, strips_u, strips_v

    empty = jnp.zeros((2 * TILE, breadth), F32)
    blank = (jnp.zeros((2 * TILE, LANES), F32),) * 2
    carried = (empty, empty, blank, blank)
    for part, items in zip(parts, copies[1:]):
        for item in items:
            item.wait()
        carried = lax.fori_loop(part.start, part.stop, body, carried, unroll=4)
    sum_u, sum_v, strips_u, strips_v = carried

    def put(slot, low, high):
        a, b = swap(even, high, low)
        msg_even[slot] = a
        msg_odd[slot] = b

    row = lax.rem(lax.broadcasted_iota(jnp.int32, (2 * TILE, breadth), 0), TILE)
    first = jnp.concatenate(
        [is_sum_u(row[:TILE], False), is_sum_u(row[TILE:], True)], axis=0
    )
    moved = jnp.concatenate([turn(sum_v[:TILE], 4, 0), turn(sum_v[TILE:], 4, 0)], axis=0)
    spare = starts[:TILE], starts[TILE:]
    for shift, at, total in ((-2, TILE - 2, sum_u), (-1, TILE - 1, sum_v)):
        spare = (
            jnp.where(row[:TILE] == at, turn(total[:TILE], shift, 0), spare[0]),
            jnp.where(
                row[TILE:] == at - TILE + 2, turn(total[TILE:], shift + 3, 0), spare[1]
            ),
        )
    starts = jnp.concatenate(spare, axis=0)
    whole = [depth, starts, jnp.where(first, sum_u, moved)]
    whole += [jnp.concatenate(pair, axis=1) for pair in (strips_u, strips_v, others)]
    for slot, value in enumerate(whole, KMT):
        put(slot, value[:TILE], value[TILE:])
    row = lax.broadcasted_iota(jnp.int32, (TILE, breadth), 0)
    for field, first in ((0, U_ROWS), (1, V_ROWS), (2, T_ROWS)):
        for tile in range(levels // TILE):
            low = high = jnp.zeros((TILE, breadth), F32)
            for q in range(TILE):
                value = ends[field, tile * TILE + q]
                here = row == q
                low = jnp.where(here, turn(value[:TILE], q, 0), low)
                high = jnp.where(here, turn(value[TILE:], q + 1, 0), high)
            put(first + tile, low, high)


def halo_rows(rows_even, rows_odd, first, k):
    tile = first + k // TILE
    north, south = swap(is_even("lat"), rows_even[tile], rows_odd[tile])
    at = lax.rem(k, TILE)
    south = pltpu.roll(south, lax.rem(2 * TILE - 1 - at, TILE), 0)
    north = pltpu.roll(north, lax.rem(TILE - at, TILE), 0)
    return south, north


def advance_inner(state, kmt, rows_odd, rows_even, flow, tracer, flow_u, flow_v, turning):
    levels, rows_here, breadth = state.shape[1:]
    tall = rows_here + 2 * TILE
    lat_even = is_even("lat")

    def halos(slot):
        north, south = swap(lat_even, rows_even[slot], rows_odd[slot])
        return south, north

    south, north = halos(KMT)
    depth = stacked(south, kmt[...].astype(F32), north)
    beside = around(depth)
    row = lax.broadcasted_iota(jnp.int32, (tall, LANES), 0)
    rotation = rotation_at(row - TILE, rows_here)
    turning[...] = rotation
    half_turn = time_step * rotation[:, :1]
    own = slice(TILE, TILE + rows_here)
    flow_u[...] = jnp.zeros_like(flow_u)
    flow_v[...] = jnp.zeros_like(flow_v)

    def body(k, _):
        level = k.astype(F32)
        wet = depth > level
        count = count_wet(beside, level)
        u_south, u_north = halo_rows(rows_even, rows_odd, U_ROWS, k)
        v_south, v_north = halo_rows(rows_even, rows_odd, V_ROWS, k)
        t_south, t_north = halo_rows(rows_even, rows_odd, T_ROWS, k)
        u = jnp.where(wet, stacked(u_south, state[0, k], u_north), 0.0)
        v = jnp.where(wet, stacked(v_south, state[1, k], v_north), 0.0)
        new_u, new_v = advance_flow(u, v, wet, count, half_turn)
        flow_u[own] += new_u[own]
        flow_v[own] += new_v[own]
        for tile, inner, shift, sign in (
            (slice(0, TILE), slice(TILE, 2 * TILE), -1, 1.0),
            (slice(tall - TILE, tall), slice(tall - 2 * TILE, tall - TILE), 1, -1.0),
        ):
            open_to = turn(jnp.where(wet[inner], 1.0, 0.0), shift, 0)
            across = sign * carry * v[tile]
            for value, flow_sum in ((u, flow_u), (v, flow_v)):
                other = turn(value[inner], shift, 0)
                term = (time_step * viscosity) * (other - open_to * value[tile]) - across * other
                flow_sum[tile] += jnp.where(wet[tile], term, 0.0)
        flow[0, k] = new_u[own]
        flow[1, k] = new_v[own]
        here = state[2, k]
        stack_t = jnp.where(wet, stacked(t_south, here, t_north), 0.0)
        middle = stack_t[own]
        sides = (east_of(middle), west_of(middle), north_of(stack_t)[own], south_of(stack_t)[own])
        change = spread(
            middle, sides, count[own], diffusivity, carry * u[own], carry * v[own]
        )
        above = state[2, jnp.maximum(k - 1, 0)]
        below = state[2, jnp.minimum(k + 1, levels - 1)]
        vertical = (above - here) + jnp.where(depth[own] > level + 1.0, below - here, 0.0)
        tracer[k] = jnp.where(
            wet[own], here + (change + (time_step * vertical_mix) * vertical), 0.0
        )
        return 0

    lax.fori_loop(0, levels, body, 0)
    row = lax.broadcasted_iota(jnp.int32, (tall, breadth), 0)
    outer = (row < TILE - 1) | (row > TILE + rows_here)
    edge = (row == TILE - 1) | (row == TILE + rows_here)
    inner = jnp.zeros((rows_here, breadth), F32)
    sums, spare = halos(SUMS), halos(GUESS)
    for number, flow_sum in enumerate((flow_u, flow_v)):
        further = stacked(turn(sums[0], -4 * number, 0), inner, turn(sums[1], -4 * number, 0))
        next_row = stacked(
            turn(spare[0], -1 - number, 0), inner, turn(spare[1], 2 - number, 0)
        )
        total = flow_sum[...]
        total = jnp.where(edge, total + next_row, total)
        flow_sum[...] = jnp.where(outer, further, total)


def fill_ends(x, west, east):
    lane = lane_of((x.shape[0], LANES))
    tiles = [x[:, i : i + LANES] for i in range(0, x.shape[1], LANES)]
    if west is not None:
        tiles[0] = jnp.where(lane == 0, west, tiles[0])
    if east is not None:
        tiles[-1] = jnp.where(lane == LANES - 1, east, tiles[-1])
    return jnp.concatenate(tiles, axis=1)


def roll_to(x, source, target, k):
    return turn(x, target - source - TILE * k, 1)


def krylov(
    sent_even, sent_odd, got_odd, got_even, flow_u, flow_v, kmt, guess,
    rows_even, rows_odd, turning, own_tracer, edges, basis, moments,
):
    levels = LEVELS
    rows_here, breadth = kmt.shape
    tall = rows_here + 2 * TILE
    lat_even = is_even("lat")
    lon_even = is_even("lon")
    lane = lane_of((tall, LANES))
    place = lax.rem(lane, TILE)
    group = lane // TILE
    level = group.astype(F32)
    own = slice(TILE, TILE + rows_here)
    half_turn = time_step * turning[...]

    def received(slot):
        rows = slice(slot * tall, (slot + 1) * tall)
        from_east, from_west = swap(lon_even, got_even[rows], got_odd[rows])
        return from_west, from_east

    def strips(slot):
        rows = slice(slot * tall, (slot + 1) * tall)
        to_east, to_west = swap(lon_even, sent_even[rows], sent_odd[rows])
        from_west, from_east = received(slot)
        west = jnp.where(place < HALO, from_west, turn(to_west, 4, 1))
        east = jnp.where(place >= TILE - HALO, from_east, turn(to_east, -4, 1))
        return west, east

    u_sides, v_sides, other = [strips(slot) for slot in range(3)]
    from_west, from_east = received(0)
    t_sides = (
        jnp.where(place == HALO - 1, turn(from_west, -1, 1), turn(own_tracer[0], 4, 1)),
        jnp.where(place == TILE - HALO, turn(from_east, 1, 1), turn(own_tracer[1], -4, 1)),
    )
    sums = []
    for side in range(2):
        depth = jnp.where(group == 1, turn(other[side], TILE, 1), other[side])
        wet = depth > level
        count = count_wet(around(depth), level)
        u = jnp.where(wet, u_sides[side], 0.0)
        v = jnp.where(wet, v_sides[side], 0.0)
        new_u, new_v = advance_flow(u, v, wet, count, half_turn)
        here = jnp.where(wet, t_sides[side], 0.0)
        change = spread(here, around(here), count, diffusivity, carry * u, carry * v)
        above = jnp.where(group > 0, turn(here, TILE, 1) - here, 0.0)
        below = jnp.where(depth > level + 1.0, turn(here, -TILE, 1) - here, 0.0)
        new_t = jnp.where(
            wet, here + (change + (time_step * vertical_mix) * (above + below)), 0.0
        )
        edges[side, 0] = new_u[own]
        edges[side, 1] = new_v[own]
        edges[side, 2] = new_t[own]
        sums.append((new_u, new_v))

    def fold(x, step):
        return x + turn(x, step, 1)

    (u_west, v_west), (u_east, v_east) = [
        [fold(x, LANES // 2) for x in side] for side in sums
    ]
    half = lane < LANES // 2
    west = fold(jnp.where(half, u_west, v_west), LANES // 4)
    east = fold(jnp.where(half, u_east, v_east), -LANES // 4)
    quarter = lax.rem(lane // (LANES // 4), 2) == 1
    folded = fold(fold(jnp.where(quarter, west, east), 2 * TILE), TILE)

    def assemble(field, west, west_at, east, east_at, seam):
        west = turn(west, -HALO - west_at, 1)
        east = turn(east, -2 - east_at, 1)
        halo = jnp.where(lane < LANES // 2, east, west)
        tiles = [field[:, i : i + LANES] for i in range(0, breadth, LANES)]
        if seam:
            tiles[0] = jnp.where(lane == 0, west, tiles[0])
            tiles[-1] = jnp.where(lane == LANES - 1, east, tiles[-1])
        return jnp.concatenate(tiles + [halo], axis=1)

    def tall_field(slot, value):
        north, south = swap(lat_even, rows_even[slot], rows_odd[slot])
        return stacked(south, value, north)

    last = LANES // 4 - TILE
    wide_u = assemble(flow_u[...], folded, LANES // 4 + last, folded, last, True)
    wide_v = assemble(flow_v[...], folded, 3 * LANES // 4 + last, folded, LANES // 2 + last, True)
    wet_levels = assemble(
        tall_field(KMT, kmt[...].astype(F32)), other[0], 0, other[1], 0, False
    )
    first = assemble(tall_field(GUESS, guess[...]), other[0], TILE, other[1], TILE, False)

    divergence = 0.5 * (east_of(wide_u) - west_of(wide_u)) + 0.5 * (
        north_of(wide_v) - south_of(wide_v)
    )
    depth = wet_levels * (1.0 / levels)
    ocean = wet_levels > 0.0
    to_east = edge_weight * jnp.minimum(depth, east_of(depth))
    to_north = edge_weight * jnp.minimum(depth, north_of(depth))
    depth_north = north_of(depth)
    to_ne = corner_weight * jnp.minimum(depth, east_of(depth_north))
    to_nw = corner_weight * jnp.minimum(depth, west_of(depth_north))
    to_west = west_of(to_east)
    to_south = south_of(to_north)
    to_sw = south_of(west_of(to_ne))
    to_se = south_of(east_of(to_nw))
    diagonal = storage + (
        (to_east + to_west) + (to_north + to_south) + ((to_ne + to_nw) + (to_se + to_sw))
    )

    def neighbours(x):
        up, down = (north_of(x), south_of(x))
        eastern = to_east * x + to_ne_w * up + to_se_w * down
        western = to_west * x + to_nw_e * up + to_sw_e * down
        return to_north * up + to_south * down + (east_of(eastern) + west_of(western))

    to_ne_w = west_of(to_ne)
    to_se_w = west_of(to_se)
    to_nw_e = east_of(to_nw)
    to_sw_e = east_of(to_sw)
    to_east, to_west = (west_of(to_east), east_of(to_west))

    start = jnp.where(ocean, first, 0.0)
    rhs = jnp.where(ocean, storage * (start - time_step * divergence), 0.0)
    residual = rhs - (diagonal * start - neighbours(start))
    inverse = 1.0 / diagonal
    vectors = [residual * inverse]
    basis[0] = start
    basis[1] = vectors[0]
    for k in range(1, ITERS):
        vectors.append(neighbours(vectors[-1]) * inverse)
        basis[k + 1] = vectors[k]
    last = neighbours(vectors[-1])

    def inner(x):
        return x[own, :breadth]

    weighted = [inner(diagonal * x) for x in vectors] + [inner(last)]
    held = [inner(x) for x in vectors]
    slot = lane_of((TILE, LANES))
    total = jnp.zeros((TILE, LANES), F32)
    for m in range(2 * ITERS):
        product = held[m // 2] * weighted[(m + 1) // 2]
        folded = None
        for i in range(0, rows_here, TILE):
            for j in range(0, breadth, LANES):
                part = product[i : i + TILE, j : j + LANES]
                folded = part if folded is None else folded + part
        total = jnp.where(slot == m, jnp.sum(folded, axis=1, keepdims=True), total)
    moments[...] = jnp.sum(total, axis=0, keepdims=True)


def over(a, b):
    return a / jnp.where(b > 1e-37, b, 1.0)


def finish(shares, basis, edges, kmt, flow, tracer, out, pressure, done, held, sems, held_sem):
    levels, rows_here, breadth = tracer.shape
    own = slice(TILE, TILE + rows_here)
    chunks = sems.shape[1]
    size = levels // chunks

    def send(first, last, c):
        part = pl.ds(c * size, size)
        fields = slice(first, last)
        return pltpu.make_async_copy(
            done.at[fields, part], out.at[fields, part], sems.at[first // 2, c]
        )

    def ended(value, field, k):
        return fill_ends(
            value,
            roll_to(edges[0, field], HALO, 0, k),
            roll_to(edges[1, field], 1, LANES - 1, k),
        )

    totals = shares[...]
    while totals.shape[0] % (2 * TILE) == 0:
        part = totals.shape[0] // 2
        totals = totals[:part] + totals[part:]
    totals = jnp.sum(totals.reshape(-1, TILE, LANES), axis=0)
    for step in (1, 2, 4):
        totals = totals + turn(totals, step, 0)
    lane = lane_of((TILE, LANES))

    def everywhere(m):
        one = jnp.sum(jnp.where(lane == m, totals, 0.0), axis=1, keepdims=True)
        return jnp.broadcast_to(one, (TILE, LANES))

    res = [everywhere(m) for m in range(2 * ITERS)]
    dirn = list(res)
    one, zero = (jnp.ones((TILE, LANES), F32), jnp.zeros((TILE, LANES), F32))
    res_in = [one] + [zero] * (ITERS - 1)
    dir_in = list(res_in)
    height_in = [zero] * ITERS
    for k in range(ITERS):
        step = over(res[k], dirn[k] - dirn[k + 1])
        step = jnp.clip(step, 1.0 / HIGHEST, 1.0 / LOWEST)
        height_in = [h + step * d for h, d in zip(height_in, dir_in)]
        if k + 1 < ITERS:
            new = [res[m] - step * (dirn[m] - dirn[m + 1]) for m in range(len(dirn) - 1)]
            ratio = jnp.clip((step * over(1.0, res[k])) * new[k + 1], 0.0, HIGHEST / LOWEST)
            dirn = [n + ratio * d for n, d in zip(new, dirn)]
            res = new
            moved = [zero] + dir_in[:-1]
            res_in = [r - step * (d - m) for r, d, m in zip(res_in, dir_in, moved)]
            dir_in = [r + ratio * d for r, d in zip(res_in, dir_in)]

    for k in range(levels):
        done[2, k] = ended(tracer[k], 2, k)
    for c in range(chunks):
        send(2, 3, c).start()

    def tile_of(i, j):
        cut = slice(i, i + TILE), slice(j, j + LANES)
        value = basis[0, *cut]
        for k in range(ITERS):
            value = value + height_in[k] * basis[k + 1, *cut]
        return value

    tall, wide = basis.shape[1:]
    height = jnp.concatenate(
        [
            jnp.concatenate([tile_of(i, j) for j in range(0, wide, LANES)], axis=1)
            for i in range(0, tall, TILE)
        ],
        axis=0,
    )
    held[...] = gravity * height[own, :breadth]
    pressure_out = pltpu.make_async_copy(held, pressure, held_sem.at[0])
    pressure_out.start()
    pull = 0.5 * time_step * gravity
    slope_east = pull * (east_of(height) - west_of(height))[own, :breadth]
    slope_north = pull * (north_of(height) - south_of(height))[own, :breadth]
    wet_levels = kmt[...]
    for c in range(chunks):
        for k in range(c * size, (c + 1) * size):
            wet = wet_levels > k
            for field, slope in ((0, slope_east), (1, slope_north)):
                done[field, k] = jnp.where(wet, ended(flow[field, k], field, k) - slope, 0.0)
        send(0, 2, c).start()
    pressure_out.wait()
    for c in range(chunks):
        send(2, 3, c).wait()
        send(0, 2, c).wait()


def pairs(axis):
    peers = lax.axis_size(axis)
    even = [(i, i ^ 1) for i in range(peers)]
    odd = [(i, ((i + 1) ^ 1) - 1) for i in range(1, peers - 1)]
    if axis == "lon":
        odd += [(0, peers - 1), (peers - 1, 0)]
    return even, odd


def exchange(axis, to_even, to_odd):
    even, odd = pairs(axis)
    from_odd = lax.ppermute(to_odd, axis, odd)
    return lax.ppermute(to_even, axis, even), from_odd


def on_device(state, kmt, first_guess):
    _, levels, rows_here, breadth = state.shape
    tall = rows_here + 2 * TILE
    wide = breadth + LANES
    shape = lambda *dims: jax.ShapeDtypeStruct(dims, F32)

    devices = lax.axis_size("lon") * lax.axis_size("lat")
    hbm = pl.BlockSpec(memory_space=pltpu.HBM)
    vmem = pl.BlockSpec(memory_space=pltpu.VMEM)
    to_odd, to_even = pl.pallas_call(
        pack_rows,
        in_specs=[hbm] * 3,
        out_specs=[vmem] * 2,
        out_shape=[pltpu.VMEM((SLOTS, TILE, breadth), F32)] * 2,
        scratch_shapes=[
            pltpu.VMEM((3, levels, 2 * TILE, breadth), F32),
            pltpu.VMEM((2 * TILE, breadth), jnp.int32),
            pltpu.VMEM((2 * TILE, breadth), F32),
            pltpu.SemaphoreType.DMA((12,)),
        ],
        compiler_params=params(VMEM_FIRST),
    )(state, kmt, first_guess)
    rows_even, rows_odd = exchange("lat", to_even, to_odd)

    held, strips = pl.pallas_call(
        pack_own,
        in_specs=[hbm, vmem, vmem],
        out_shape=[pltpu.VMEM(state.shape, F32), pltpu.VMEM((2, 4, rows_here, LANES), F32)],
        scratch_shapes=[pltpu.SemaphoreType.DMA((3,))],
        compiler_params=params(VMEM_OWN),
        cost_estimate=cost(state.size),
    )(state, kmt, first_guess)
    length = 3 * tall
    sent_odd, sent_even, own_tracer = pl.pallas_call(
        pack_cols,
        out_shape=[shape(length, LANES)] * 2 + [shape(2, tall, LANES)],
        compiler_params=params(),
    )(strips, rows_odd, rows_even)
    got_even, got_odd = exchange("lon", sent_even, sent_odd)

    flow, tracer, flow_u, flow_v, turning = pl.pallas_call(
        advance_inner,
        out_shape=[
            shape(2, levels, rows_here, breadth),
            shape(levels, rows_here, breadth),
            shape(tall, breadth),
            shape(tall, breadth),
            shape(tall, LANES),
        ],
        compiler_params=params(),
        cost_estimate=cost(state.size),
    )(held, kmt, rows_odd, rows_even)

    edges, basis, moments = pl.pallas_call(
        krylov,
        out_shape=[
            shape(2, 3, rows_here, LANES),
            shape(ITERS + 1, tall, wide),
            shape(1, LANES),
        ],
        compiler_params=params(),
    )(
        sent_even, sent_odd, got_odd, got_even, flow_u, flow_v, kmt, first_guess,
        rows_even, rows_odd, turning, own_tracer,
    )

    shares = jnp.broadcast_to(moments[None], (devices, 1, LANES))
    shares = lax.all_to_all(shares, ("lon", "lat"), 0, 0)
    return pl.pallas_call(
        finish,
        in_specs=[vmem] * 6,
        out_specs=[hbm, hbm],
        out_shape=[shape(3, levels, rows_here, breadth), shape(rows_here, breadth)],
        scratch_shapes=[
            pltpu.VMEM((3, levels, rows_here, breadth), F32),
            pltpu.VMEM((rows_here, breadth), F32),
            pltpu.SemaphoreType.DMA((2, 4)),
            pltpu.SemaphoreType.DMA((1,)),
        ],
        compiler_params=params(),
    )(shares.reshape(devices, LANES), basis, edges, kmt, flow, tracer)


def solution(mesh):
    placed = (P(None, None, "lat", "lon"), P("lat", "lon"), P("lat", "lon"))
    return jax.shard_map(
        on_device,
        mesh=mesh,
        in_specs=placed,
        out_specs=(P(None, None, "lat", "lon"), P("lat", "lon")),
        check_vma=False,
    )
```

```python
import jax
import jax.numpy as jnp
from jax import lax
from jax.experimental import pallas as pl
from jax.experimental.pallas import tpu as pltpu
from jax.sharding import PartitionSpec as P

ITERS = 4
F32 = jnp.float32

viscosity = 0.12
diffusivity = 0.1
advection_scale = 0.5
vertical_mix = 0.2
coriolis_scale = 0.6
time_step = 0.5
storage = 0.5
gravity = 1.5
edge_weight = 2.0 / 3.0
corner_weight = 1.0 / 6.0

TILE = 8
LANES = 128
LEVELS = LANES // TILE
HALO = 6

U_ROWS = 0
V_ROWS = U_ROWS + LEVELS // TILE
T_ROWS = V_ROWS + LEVELS // TILE
KMT, GUESS, SUMS, STRIPS = range(T_ROWS + LEVELS // TILE, T_ROWS + LEVELS // TILE + 4)
SLOTS = STRIPS + 3

LOWEST = storage / (storage + 4 * edge_weight + 4 * corner_weight)
HIGHEST = 2.0 - LOWEST
VMEM_LIMIT = 16 * 1024 * 1024
VMEM_FIRST = 64520000
VMEM_OWN = 60000000


def params(limit=VMEM_LIMIT):
    return pltpu.CompilerParams(vmem_limit_bytes=limit)


def cost(size):
    return pl.CostEstimate(flops=60 * size, bytes_accessed=8 * size, transcendentals=0)


def turn(x, shift, axis):
    return pltpu.roll(x, shift % x.shape[axis], axis)


def east_of(x):
    return turn(x, -1, 1)


def west_of(x):
    return turn(x, 1, 1)


def north_of(x):
    return turn(x, -1, 0)


def south_of(x):
    return turn(x, 1, 0)


def lane_of(shape):
    return lax.broadcasted_iota(jnp.int32, shape, len(shape) - 1)


def is_even(axis):
    return lax.rem(lax.axis_index(axis), 2) == 0


def swap(first, a, b):
    return jnp.where(first, a, b), jnp.where(first, b, a)


def stacked(south, own, north):
    return jnp.concatenate([south, own, north], axis=0)


def place(group, k, west, east, acc):
    to_west, to_east = acc
    to_west = jnp.where(group == k, pltpu.roll(west, 2 + TILE * k, 1), to_west)
    to_east = jnp.where(
        group == k, pltpu.roll(east, lax.rem(HALO + TILE * k, LANES), 1), to_east
    )
    return to_west, to_east


def over_groups(x):
    for step in (TILE, 2 * TILE, 4 * TILE, 8 * TILE):
        x = x + pltpu.roll(x, step, 1)
    return x


def pack_others(group, wet, guess, cut):
    blank = (jnp.zeros_like(wet[:, cut[0]]),) * 2
    wet = place(group, jnp.int32(0), wet[:, cut[0]], wet[:, cut[1]], blank)
    wet = tuple(over_groups(x) for x in wet)
    return place(group, jnp.int32(1), guess[:, cut[0]], guess[:, cut[1]], wet)


def pack_own(state_hbm, kmt, guess, state, strips, sems):
    levels, rows_here, breadth = state.shape[1:]
    copies = [
        pltpu.make_async_copy(state_hbm.at[field], state.at[field], sems.at[field])
        for field in range(3)
    ]
    for item in copies:
        item.start()
    group = lane_of((rows_here, LANES)) // TILE
    ends = slice(0, LANES), slice(breadth - LANES, breadth)
    blank = (jnp.zeros((rows_here, LANES), F32),) * 2
    strips[0, 3], strips[1, 3] = pack_others(group, kmt[...].astype(F32), guess[...], ends)
    for field in range(3):
        copies[field].wait()

        def body(k, acc, field=field):
            west, east = [state[field, k, :, cols] for cols in ends]
            return place(group, k, west, east, acc)

        acc = lax.fori_loop(0, levels, body, blank, unroll=4)
        strips[0, field], strips[1, field] = acc
    slot = lax.rem(lane_of((rows_here, LANES)), TILE)
    strips[0, 0] = jnp.where(slot == 1, turn(strips[0, 2], -1, 1), strips[0, 0])
    strips[1, 0] = jnp.where(slot == HALO, turn(strips[1, 2], 1, 1), strips[1, 0])


def pack_cols(strips, rows_odd, rows_even, msg_odd, msg_even, own_tracer):
    tall = strips.shape[2] + 2 * TILE
    lat_even = is_even("lat")
    lon_even = is_even("lon")

    def tall_strips(field, south, north):
        return [
            stacked(
                south[:, i * LANES : (i + 1) * LANES],
                strips[i, field],
                north[:, i * LANES : (i + 1) * LANES],
            )
            for i in range(2)
        ]

    def put(number, field, south, north):
        base = number * tall
        to_west, to_east = tall_strips(field, south, north)
        a, b = swap(lon_even, to_east, to_west)
        msg_even[base : base + tall] = a
        msg_odd[base : base + tall] = b

    halos = []
    for slot in range(STRIPS, SLOTS):
        north, south = swap(lat_even, rows_even[slot], rows_odd[slot])
        halos.append((south, north))
    put(0, 0, *halos[0])
    put(1, 1, *halos[1])
    put(2, 3, *halos[2])
    own_tracer[0], own_tracer[1] = tall_strips(
        2, turn(halos[0][0], -1, 0), turn(halos[0][1], 1, 0)
    )


def rotation_at(row, rows_here):
    total_rows = rows_here * lax.axis_size("lat")
    row = (row + lax.axis_index("lat") * rows_here).astype(F32)
    angle = jnp.pi / 180.0 * (-80.0 + 160.0 * (row + 0.5) / total_rows)
    return coriolis_scale * jnp.sin(angle)


def around(x):
    return east_of(x), west_of(x), north_of(x), south_of(x)


def count_wet(sides, level):
    total = None
    for side in sides:
        term = jnp.where(side > level, 1.0, 0.0)
        total = term if total is None else total + term
    return total


def spread(x, sides, count, coefficient, zonal, merid):
    east, west, north, south = sides
    laplace = east + west + north + south - count * x
    return (
        (time_step * coefficient) * laplace
        - zonal * (east - west)
        - merid * (north - south)
    )


carry = 0.5 * time_step * advection_scale


def advance_flow(u, v, wet, count, half_turn, around=around):
    zonal, merid = (carry * u, carry * v)
    new_u = u + (spread(u, around(u), count, viscosity, zonal, merid) + half_turn * v)
    new_v = v + (spread(v, around(v), count, viscosity, zonal, merid) - half_turn * u)
    return jnp.where(wet, new_u, 0.0), jnp.where(wet, new_v, 0.0)


def is_sum_u(row, southern):
    first = TILE - 5 if southern else 1
    return (row >= first) & (row < first + 4)


def pack_rows(state, kmt, guess, msg_odd, msg_even, ends, wet_ends, guess_ends, sems):
    levels, rows_here, breadth = state.shape[1:]
    even = is_even("lat")
    parts = [slice(k, k + levels // 4) for k in range(0, levels, levels // 4)]
    copies = []
    for part in [None] + parts:
        copies.append([])
        for number, rows in enumerate((slice(0, TILE), slice(rows_here - TILE, rows_here))):
            held = slice(number * TILE, (number + 1) * TILE)
            if part is not None:
                pairs_of_refs = [(state.at[:, part, rows, :], ends.at[:, part, held, :])]
            else:
                pairs_of_refs = [
                    (kmt.at[rows, :], wet_ends.at[held, :]),
                    (guess.at[rows, :], guess_ends.at[held, :]),
                ]
            for source, target in pairs_of_refs:
                item = pltpu.make_async_copy(source, target, sems.at[sum(map(len, copies))])
                item.start()
                copies[-1].append(item)
    row = lax.broadcasted_iota(jnp.int32, (2 * TILE, LANES), 0)
    rotation = rotation_at(jnp.where(row < TILE, row, row + rows_here - 2 * TILE), rows_here)
    half_turn = time_step * rotation[:, :1]
    group = lane_of((2 * TILE, LANES)) // TILE
    row = lax.broadcasted_iota(jnp.int32, (2 * TILE, breadth), 0)
    borrowed = (row == TILE - 1) | (row == TILE)
    for item in copies[0]:
        item.wait()

    top = row == 2 * TILE - 1

    def within(x):
        east, west, north, south = around(x)
        return east, west, jnp.where(top, 0.0, north), jnp.where(row == 0, 0.0, south)

    depth = wet_ends[...].astype(F32)
    beside = within(depth)
    cut = slice(0, LANES), slice(breadth - LANES, breadth)
    starts = guess_ends[...]
    others = pack_others(group, depth, starts, cut)

    def body(k, carried):
        sum_u, sum_v, strips_u, strips_v = carried
        level = k.astype(F32)
        wet = depth > level
        raw_u, raw_v, raw_t = [ends[field, k] for field in range(3)]
        u = jnp.where(wet, raw_u, 0.0)
        v = jnp.where(wet, raw_v, 0.0)
        new_u, new_v = advance_flow(
            u, v, wet, count_wet(beside, level), half_turn, within
        )
        moved = jnp.concatenate([turn(raw_t[:TILE], -1, 0), turn(raw_t[TILE:], 1, 0)], axis=0)
        lent = jnp.where(borrowed, moved, raw_u)
        strips_u = place(group, k, lent[:, cut[0]], lent[:, cut[1]], strips_u)
        strips_v = place(group, k, raw_v[:, cut[0]], raw_v[:, cut[1]], strips_v)
        return sum_u + new_u, sum_v + new_v, strips_u, strips_v

    empty = jnp.zeros((2 * TILE, breadth), F32)
    blank = (jnp.zeros((2 * TILE, LANES), F32),) * 2
    carried = (empty, empty, blank, blank)
    for part, items in zip(parts, copies[1:]):
        for item in items:
            item.wait()
        carried = lax.fori_loop(part.start, part.stop, body, carried, unroll=4)
    sum_u, sum_v, strips_u, strips_v = carried

    def put(slot, low, high):
        a, b = swap(even, high, low)
        msg_even[slot] = a
        msg_odd[slot] = b

    row = lax.rem(lax.broadcasted_iota(jnp.int32, (2 * TILE, breadth), 0), TILE)
    first = jnp.concatenate(
        [is_sum_u(row[:TILE], False), is_sum_u(row[TILE:], True)], axis=0
    )
    moved = jnp.concatenate([turn(sum_v[:TILE], 4, 0), turn(sum_v[TILE:], 4, 0)], axis=0)
    spare = starts[:TILE], starts[TILE:]
    for shift, at, total in ((-2, TILE - 2, sum_u), (-1, TILE - 1, sum_v)):
        spare = (
            jnp.where(row[:TILE] == at, turn(total[:TILE], shift, 0), spare[0]),
            jnp.where(
                row[TILE:] == at - TILE + 2, turn(total[TILE:], shift + 3, 0), spare[1]
            ),
        )
    starts = jnp.concatenate(spare, axis=0)
    whole = [depth, starts, jnp.where(first, sum_u, moved)]
    whole += [jnp.concatenate(pair, axis=1) for pair in (strips_u, strips_v, others)]
    for slot, value in enumerate(whole, KMT):
        put(slot, value[:TILE], value[TILE:])
    row = lax.broadcasted_iota(jnp.int32, (TILE, breadth), 0)
    for field, first in ((0, U_ROWS), (1, V_ROWS), (2, T_ROWS)):
        for tile in range(levels // TILE):
            low = high = jnp.zeros((TILE, breadth), F32)
            for q in range(TILE):
                value = ends[field, tile * TILE + q]
                here = row == q
                low = jnp.where(here, turn(value[:TILE], q, 0), low)
                high = jnp.where(here, turn(value[TILE:], q + 1, 0), high)
            put(first + tile, low, high)


def halo_rows(rows_even, rows_odd, first, k):
    tile = first + k // TILE
    north, south = swap(is_even("lat"), rows_even[tile], rows_odd[tile])
    at = lax.rem(k, TILE)
    south = pltpu.roll(south, lax.rem(2 * TILE - 1 - at, TILE), 0)
    north = pltpu.roll(north, lax.rem(TILE - at, TILE), 0)
    return south, north


def advance_inner(state, kmt, rows_odd, rows_even, flow, tracer, flow_u, flow_v, turning):
    levels, rows_here, breadth = state.shape[1:]
    tall = rows_here + 2 * TILE
    lat_even = is_even("lat")

    def halos(slot):
        north, south = swap(lat_even, rows_even[slot], rows_odd[slot])
        return south, north

    south, north = halos(KMT)
    depth = stacked(south, kmt[...].astype(F32), north)
    beside = around(depth)
    row = lax.broadcasted_iota(jnp.int32, (tall, LANES), 0)
    rotation = rotation_at(row - TILE, rows_here)
    turning[...] = rotation
    half_turn = time_step * rotation[:, :1]
    own = slice(TILE, TILE + rows_here)
    flow_u[...] = jnp.zeros_like(flow_u)
    flow_v[...] = jnp.zeros_like(flow_v)

    def body(k, _):
        level = k.astype(F32)
        wet = depth > level
        count = count_wet(beside, level)
        u_south, u_north = halo_rows(rows_even, rows_odd, U_ROWS, k)
        v_south, v_north = halo_rows(rows_even, rows_odd, V_ROWS, k)
        t_south, t_north = halo_rows(rows_even, rows_odd, T_ROWS, k)
        u = jnp.where(wet, stacked(u_south, state[0, k], u_north), 0.0)
        v = jnp.where(wet, stacked(v_south, state[1, k], v_north), 0.0)
        new_u, new_v = advance_flow(u, v, wet, count, half_turn)
        flow_u[own] += new_u[own]
        flow_v[own] += new_v[own]
        for tile, inner, shift, sign in (
            (slice(0, TILE), slice(TILE, 2 * TILE), -1, 1.0),
            (slice(tall - TILE, tall), slice(tall - 2 * TILE, tall - TILE), 1, -1.0),
        ):
            open_to = turn(jnp.where(wet[inner], 1.0, 0.0), shift, 0)
            across = sign * carry * v[tile]
            for value, flow_sum in ((u, flow_u), (v, flow_v)):
                other = turn(value[inner], shift, 0)
                term = (time_step * viscosity) * (other - open_to * value[tile]) - across * other
                flow_sum[tile] += jnp.where(wet[tile], term, 0.0)
        flow[0, k] = new_u[own]
        flow[1, k] = new_v[own]
        here = state[2, k]
        stack_t = jnp.where(wet, stacked(t_south, here, t_north), 0.0)
        middle = stack_t[own]
        sides = (east_of(middle), west_of(middle), north_of(stack_t)[own], south_of(stack_t)[own])
        change = spread(
            middle, sides, count[own], diffusivity, carry * u[own], carry * v[own]
        )
        above = state[2, jnp.maximum(k - 1, 0)]
        below = state[2, jnp.minimum(k + 1, levels - 1)]
        vertical = (above - here) + jnp.where(depth[own] > level + 1.0, below - here, 0.0)
        tracer[k] = jnp.where(
            wet[own], here + (change + (time_step * vertical_mix) * vertical), 0.0
        )
        return 0

    lax.fori_loop(0, levels, body, 0)
    row = lax.broadcasted_iota(jnp.int32, (tall, breadth), 0)
    outer = (row < TILE - 1) | (row > TILE + rows_here)
    edge = (row == TILE - 1) | (row == TILE + rows_here)
    inner = jnp.zeros((rows_here, breadth), F32)
    sums, spare = halos(SUMS), halos(GUESS)
    for number, flow_sum in enumerate((flow_u, flow_v)):
        further = stacked(turn(sums[0], -4 * number, 0), inner, turn(sums[1], -4 * number, 0))
        next_row = stacked(
            turn(spare[0], -1 - number, 0), inner, turn(spare[1], 2 - number, 0)
        )
        total = flow_sum[...]
        total = jnp.where(edge, total + next_row, total)
        flow_sum[...] = jnp.where(outer, further, total)


def fill_ends(x, west, east):
    lane = lane_of((x.shape[0], LANES))
    tiles = [x[:, i : i + LANES] for i in range(0, x.shape[1], LANES)]
    if west is not None:
        tiles[0] = jnp.where(lane == 0, west, tiles[0])
    if east is not None:
        tiles[-1] = jnp.where(lane == LANES - 1, east, tiles[-1])
    return jnp.concatenate(tiles, axis=1)


def roll_to(x, source, target, k):
    return turn(x, target - source - TILE * k, 1)


def krylov(
    sent_even, sent_odd, got_odd, got_even, flow_u, flow_v, kmt, guess,
    rows_even, rows_odd, turning, own_tracer, edges, basis, moments,
):
    levels = LEVELS
    rows_here, breadth = kmt.shape
    tall = rows_here + 2 * TILE
    lat_even = is_even("lat")
    lon_even = is_even("lon")
    lane = lane_of((tall, LANES))
    place = lax.rem(lane, TILE)
    group = lane // TILE
    level = group.astype(F32)
    own = slice(TILE, TILE + rows_here)
    half_turn = time_step * turning[...]

    def received(slot):
        rows = slice(slot * tall, (slot + 1) * tall)
        from_east, from_west = swap(lon_even, got_even[rows], got_odd[rows])
        return from_west, from_east

    def strips(slot):
        rows = slice(slot * tall, (slot + 1) * tall)
        to_east, to_west = swap(lon_even, sent_even[rows], sent_odd[rows])
        from_west, from_east = received(slot)
        west = jnp.where(place < HALO, from_west, turn(to_west, 4, 1))
        east = jnp.where(place >= TILE - HALO, from_east, turn(to_east, -4, 1))
        return west, east

    u_sides, v_sides, other = [strips(slot) for slot in range(3)]
    from_west, from_east = received(0)
    t_sides = (
        jnp.where(place == HALO - 1, turn(from_west, -1, 1), turn(own_tracer[0], 4, 1)),
        jnp.where(place == TILE - HALO, turn(from_east, 1, 1), turn(own_tracer[1], -4, 1)),
    )
    sums = []
    for side in range(2):
        depth = jnp.where(group == 1, turn(other[side], TILE, 1), other[side])
        wet = depth > level
        count = count_wet(around(depth), level)
        u = jnp.where(wet, u_sides[side], 0.0)
        v = jnp.where(wet, v_sides[side], 0.0)
        new_u, new_v = advance_flow(u, v, wet, count, half_turn)
        here = jnp.where(wet, t_sides[side], 0.0)
        change = spread(here, around(here), count, diffusivity, carry * u, carry * v)
        above = jnp.where(group > 0, turn(here, TILE, 1) - here, 0.0)
        below = jnp.where(depth > level + 1.0, turn(here, -TILE, 1) - here, 0.0)
        new_t = jnp.where(
            wet, here + (change + (time_step * vertical_mix) * (above + below)), 0.0
        )
        edges[side, 0] = new_u[own]
        edges[side, 1] = new_v[own]
        edges[side, 2] = new_t[own]
        sums.append((new_u, new_v))

    def fold(x, step):
        return x + turn(x, step, 1)

    (u_west, v_west), (u_east, v_east) = [
        [fold(x, LANES // 2) for x in side] for side in sums
    ]
    half = lane < LANES // 2
    west = fold(jnp.where(half, u_west, v_west), LANES // 4)
    east = fold(jnp.where(half, u_east, v_east), -LANES // 4)
    quarter = lax.rem(lane // (LANES // 4), 2) == 1
    folded = fold(fold(jnp.where(quarter, west, east), 2 * TILE), TILE)

    def assemble(field, west, west_at, east, east_at, seam):
        west = turn(west, -HALO - west_at, 1)
        east = turn(east, -2 - east_at, 1)
        halo = jnp.where(lane < LANES // 2, east, west)
        tiles = [field[:, i : i + LANES] for i in range(0, breadth, LANES)]
        if seam:
            tiles[0] = jnp.where(lane == 0, west, tiles[0])
            tiles[-1] = jnp.where(lane == LANES - 1, east, tiles[-1])
        return jnp.concatenate(tiles + [halo], axis=1)

    def tall_field(slot, value):
        north, south = swap(lat_even, rows_even[slot], rows_odd[slot])
        return stacked(south, value, north)

    last = LANES // 4 - TILE
    wide_u = assemble(flow_u[...], folded, LANES // 4 + last, folded, last, True)
    wide_v = assemble(flow_v[...], folded, 3 * LANES // 4 + last, folded, LANES // 2 + last, True)
    wet_levels = assemble(
        tall_field(KMT, kmt[...].astype(F32)), other[0], 0, other[1], 0, False
    )
    first = assemble(tall_field(GUESS, guess[...]), other[0], TILE, other[1], TILE, False)

    divergence = 0.5 * (east_of(wide_u) - west_of(wide_u)) + 0.5 * (
        north_of(wide_v) - south_of(wide_v)
    )
    depth = wet_levels * (1.0 / levels)
    ocean = wet_levels > 0.0
    to_east = edge_weight * jnp.minimum(depth, east_of(depth))
    to_north = edge_weight * jnp.minimum(depth, north_of(depth))
    depth_north = north_of(depth)
    to_ne = corner_weight * jnp.minimum(depth, east_of(depth_north))
    to_nw = corner_weight * jnp.minimum(depth, west_of(depth_north))
    to_west = west_of(to_east)
    to_south = south_of(to_north)
    to_sw = south_of(west_of(to_ne))
    to_se = south_of(east_of(to_nw))
    diagonal = storage + (
        (to_east + to_west) + (to_north + to_south) + ((to_ne + to_nw) + (to_se + to_sw))
    )

    def neighbours(x):
        up, down = (north_of(x), south_of(x))
        eastern = to_east * x + to_ne_w * up + to_se_w * down
        western = to_west * x + to_nw_e * up + to_sw_e * down
        return to_north * up + to_south * down + (east_of(eastern) + west_of(western))

    to_ne_w = west_of(to_ne)
    to_se_w = west_of(to_se)
    to_nw_e = east_of(to_nw)
    to_sw_e = east_of(to_sw)
    to_east, to_west = (west_of(to_east), east_of(to_west))

    start = jnp.where(ocean, first, 0.0)
    rhs = jnp.where(ocean, storage * (start - time_step * divergence), 0.0)
    residual = rhs - (diagonal * start - neighbours(start))
    inverse = 1.0 / diagonal
    vectors = [residual * inverse]
    basis[0] = start
    basis[1] = vectors[0]
    for k in range(1, ITERS):
        vectors.append(neighbours(vectors[-1]) * inverse)
        basis[k + 1] = vectors[k]
    last = neighbours(vectors[-1])

    def inner(x):
        return x[own, :breadth]

    weighted = [inner(diagonal * x) for x in vectors] + [inner(last)]
    held = [inner(x) for x in vectors]
    slot = lane_of((TILE, LANES))
    total = jnp.zeros((TILE, LANES), F32)
    for m in range(2 * ITERS):
        product = held[m // 2] * weighted[(m + 1) // 2]
        folded = None
        for i in range(0, rows_here, TILE):
            for j in range(0, breadth, LANES):
                part = product[i : i + TILE, j : j + LANES]
                folded = part if folded is None else folded + part
        total = jnp.where(slot == m, jnp.sum(folded, axis=1, keepdims=True), total)
    moments[...] = jnp.sum(total, axis=0, keepdims=True)


def over(a, b):
    return a / jnp.where(b > 1e-37, b, 1.0)


def finish(shares, basis, edges, kmt, flow, tracer, out, pressure, done, held, sems, held_sem):
    levels, rows_here, breadth = tracer.shape
    own = slice(TILE, TILE + rows_here)
    chunks = sems.shape[1]
    size = levels // chunks

    def send(first, last, c):
        part = pl.ds(c * size, size)
        fields = slice(first, last)
        return pltpu.make_async_copy(
            done.at[fields, part], out.at[fields, part], sems.at[first // 2, c]
        )

    def ended(value, field, k):
        return fill_ends(
            value,
            roll_to(edges[0, field], HALO, 0, k),
            roll_to(edges[1, field], 1, LANES - 1, k),
        )

    totals = shares[...]
    while totals.shape[0] % (2 * TILE) == 0:
        part = totals.shape[0] // 2
        totals = totals[:part] + totals[part:]
    totals = jnp.sum(totals.reshape(-1, TILE, LANES), axis=0)
    for step in (1, 2, 4):
        totals = totals + turn(totals, step, 0)
    lane = lane_of((TILE, LANES))

    def everywhere(m):
        one = jnp.sum(jnp.where(lane == m, totals, 0.0), axis=1, keepdims=True)
        return jnp.broadcast_to(one, (TILE, LANES))

    res = [everywhere(m) for m in range(2 * ITERS)]
    dirn = list(res)
    one, zero = (jnp.ones((TILE, LANES), F32), jnp.zeros((TILE, LANES), F32))
    res_in = [one] + [zero] * (ITERS - 1)
    dir_in = list(res_in)
    height_in = [zero] * ITERS
    for k in range(ITERS):
        step = over(res[k], dirn[k] - dirn[k + 1])
        step = jnp.clip(step, 1.0 / HIGHEST, 1.0 / LOWEST)
        height_in = [h + step * d for h, d in zip(height_in, dir_in)]
        if k + 1 < ITERS:
            new = [res[m] - step * (dirn[m] - dirn[m + 1]) for m in range(len(dirn) - 1)]
            ratio = jnp.clip((step * over(1.0, res[k])) * new[k + 1], 0.0, HIGHEST / LOWEST)
            dirn = [n + ratio * d for n, d in zip(new, dirn)]
            res = new
            moved = [zero] + dir_in[:-1]
            res_in = [r - step * (d - m) for r, d, m in zip(res_in, dir_in, moved)]
            dir_in = [r + ratio * d for r, d in zip(res_in, dir_in)]

    for k in range(levels):
        done[2, k] = ended(tracer[k], 2, k)
    for c in range(chunks):
        send(2, 3, c).start()

    def tile_of(i, j):
        cut = slice(i, i + TILE), slice(j, j + LANES)
        value = basis[0, *cut]
        for k in range(ITERS):
            value = value + height_in[k] * basis[k + 1, *cut]
        return value

    tall, wide = basis.shape[1:]
    height = jnp.concatenate(
        [
            jnp.concatenate([tile_of(i, j) for j in range(0, wide, LANES)], axis=1)
            for i in range(0, tall, TILE)
        ],
        axis=0,
    )
    held[...] = gravity * height[own, :breadth]
    pressure_out = pltpu.make_async_copy(held, pressure, held_sem.at[0])
    pressure_out.start()
    pull = 0.5 * time_step * gravity
    slope_east = pull * (east_of(height) - west_of(height))[own, :breadth]
    slope_north = pull * (north_of(height) - south_of(height))[own, :breadth]
    wet_levels = kmt[...]
    for c in range(chunks):
        for k in range(c * size, (c + 1) * size):
            wet = wet_levels > k
            for field, slope in ((0, slope_east), (1, slope_north)):
                done[field, k] = jnp.where(wet, ended(flow[field, k], field, k) - slope, 0.0)
        send(0, 2, c).start()
    pressure_out.wait()
    for c in range(chunks):
        send(2, 3, c).wait()
        send(0, 2, c).wait()


def pairs(axis):
    peers = lax.axis_size(axis)
    even = [(i, i ^ 1) for i in range(peers)]
    odd = [(i, ((i + 1) ^ 1) - 1) for i in range(1, peers - 1)]
    if axis == "lon":
        odd += [(0, peers - 1), (peers - 1, 0)]
    return even, odd


def exchange(axis, to_even, to_odd):
    even, odd = pairs(axis)
    from_odd = lax.ppermute(to_odd, axis, odd)
    return lax.ppermute(to_even, axis, even), from_odd


def on_device(state, kmt, first_guess):
    _, levels, rows_here, breadth = state.shape
    tall = rows_here + 2 * TILE
    wide = breadth + LANES
    shape = lambda *dims: jax.ShapeDtypeStruct(dims, F32)

    devices = lax.axis_size("lon") * lax.axis_size("lat")
    hbm = pl.BlockSpec(memory_space=pltpu.HBM)
    vmem = pl.BlockSpec(memory_space=pltpu.VMEM)
    to_odd, to_even = pl.pallas_call(
        pack_rows,
        in_specs=[hbm] * 3,
        out_specs=[vmem] * 2,
        out_shape=[pltpu.VMEM((SLOTS, TILE, breadth), F32)] * 2,
        scratch_shapes=[
            pltpu.VMEM((3, levels, 2 * TILE, breadth), F32),
            pltpu.VMEM((2 * TILE, breadth), jnp.int32),
            pltpu.VMEM((2 * TILE, breadth), F32),
            pltpu.SemaphoreType.DMA((12,)),
        ],
        compiler_params=params(VMEM_FIRST),
    )(state, kmt, first_guess)
    rows_even, rows_odd = exchange("lat", to_even, to_odd)

    held, strips = pl.pallas_call(
        pack_own,
        in_specs=[hbm, vmem, vmem],
        out_shape=[pltpu.VMEM(state.shape, F32), pltpu.VMEM((2, 4, rows_here, LANES), F32)],
        scratch_shapes=[pltpu.SemaphoreType.DMA((3,))],
        compiler_params=params(VMEM_OWN),
        cost_estimate=cost(state.size),
    )(state, kmt, first_guess)
    length = 3 * tall
    sent_odd, sent_even, own_tracer = pl.pallas_call(
        pack_cols,
        out_shape=[shape(length, LANES)] * 2 + [shape(2, tall, LANES)],
        compiler_params=params(),
    )(strips, rows_odd, rows_even)
    got_even, got_odd = exchange("lon", sent_even, sent_odd)

    flow, tracer, flow_u, flow_v, turning = pl.pallas_call(
        advance_inner,
        out_shape=[
            shape(2, levels, rows_here, breadth),
            shape(levels, rows_here, breadth),
            shape(tall, breadth),
            shape(tall, breadth),
            shape(tall, LANES),
        ],
        compiler_params=params(),
        cost_estimate=cost(state.size),
    )(held, kmt, rows_odd, rows_even)

    edges, basis, moments = pl.pallas_call(
        krylov,
        out_shape=[
            shape(2, 3, rows_here, LANES),
            shape(ITERS + 1, tall, wide),
            shape(1, LANES),
        ],
        compiler_params=params(),
    )(
        sent_even, sent_odd, got_odd, got_even, flow_u, flow_v, kmt, first_guess,
        rows_even, rows_odd, turning, own_tracer,
    )

    shares = jnp.broadcast_to(moments[None], (devices, 1, LANES))
    shares = lax.all_to_all(shares, ("lon", "lat"), 0, 0)
    return pl.pallas_call(
        finish,
        in_specs=[vmem] * 6,
        out_specs=[hbm, hbm],
        out_shape=[shape(3, levels, rows_here, breadth), shape(rows_here, breadth)],
        scratch_shapes=[
            pltpu.VMEM((3, levels, rows_here, breadth), F32),
            pltpu.VMEM((rows_here, breadth), F32),
            pltpu.SemaphoreType.DMA((2, 4)),
            pltpu.SemaphoreType.DMA((1,)),
        ],
        compiler_params=params(),
    )(shares.reshape(devices, LANES), basis, edges, kmt, flow, tracer)


def solution(mesh):
    placed = (P(None, None, "lat", "lon"), P("lat", "lon"), P("lat", "lon"))
    return jax.shard_map(
        on_device,
        mesh=mesh,
        in_specs=placed,
        out_specs=(P(None, None, "lat", "lon"), P("lat", "lon")),
        check_vma=False,
    )
```

```python
import jax
import jax.numpy as jnp
from jax import lax
from jax.experimental import pallas as pl
from jax.experimental.pallas import tpu as pltpu
from jax.sharding import PartitionSpec as P

ITERS = 4
F32 = jnp.float32

viscosity = 0.12
diffusivity = 0.1
advection_scale = 0.5
vertical_mix = 0.2
coriolis_scale = 0.6
time_step = 0.5
storage = 0.5
gravity = 1.5
edge_weight = 2.0 / 3.0
corner_weight = 1.0 / 6.0

TILE = 8
LANES = 128
LEVELS = LANES // TILE
HALO = 6

U_ROWS = 0
V_ROWS = U_ROWS + LEVELS // TILE
T_ROWS = V_ROWS + LEVELS // TILE
KMT, GUESS, SUMS, STRIPS = range(T_ROWS + LEVELS // TILE, T_ROWS + LEVELS // TILE + 4)
SLOTS = STRIPS + 3

LOWEST = storage / (storage + 4 * edge_weight + 4 * corner_weight)
HIGHEST = 2.0 - LOWEST
VMEM_LIMIT = 16 * 1024 * 1024
VMEM_FIRST = 64520000
VMEM_OWN = 60000000


def params(limit=VMEM_LIMIT):
    return pltpu.CompilerParams(vmem_limit_bytes=limit)


def cost(size):
    return pl.CostEstimate(flops=60 * size, bytes_accessed=8 * size, transcendentals=0)


def turn(x, shift, axis):
    return pltpu.roll(x, shift % x.shape[axis], axis)


def east_of(x):
    return turn(x, -1, 1)


def west_of(x):
    return turn(x, 1, 1)


def north_of(x):
    return turn(x, -1, 0)


def south_of(x):
    return turn(x, 1, 0)


def lane_of(shape):
    return lax.broadcasted_iota(jnp.int32, shape, len(shape) - 1)


def is_even(axis):
    return lax.rem(lax.axis_index(axis), 2) == 0


def swap(first, a, b):
    return jnp.where(first, a, b), jnp.where(first, b, a)


def stacked(south, own, north):
    return jnp.concatenate([south, own, north], axis=0)


def place(group, k, west, east, acc):
    to_west, to_east = acc
    to_west = jnp.where(group == k, pltpu.roll(west, 2 + TILE * k, 1), to_west)
    to_east = jnp.where(
        group == k, pltpu.roll(east, lax.rem(HALO + TILE * k, LANES), 1), to_east
    )
    return to_west, to_east


def over_groups(x):
    for step in (TILE, 2 * TILE, 4 * TILE, 8 * TILE):
        x = x + pltpu.roll(x, step, 1)
    return x


def pack_others(group, wet, guess, cut):
    blank = (jnp.zeros_like(wet[:, cut[0]]),) * 2
    wet = place(group, jnp.int32(0), wet[:, cut[0]], wet[:, cut[1]], blank)
    wet = tuple(over_groups(x) for x in wet)
    return place(group, jnp.int32(1), guess[:, cut[0]], guess[:, cut[1]], wet)


def pack_own(state_hbm, kmt, guess, state, strips, sems):
    levels, rows_here, breadth = state.shape[1:]
    copies = [
        pltpu.make_async_copy(state_hbm.at[field], state.at[field], sems.at[field])
        for field in range(3)
    ]
    for item in copies:
        item.start()
    group = lane_of((rows_here, LANES)) // TILE
    ends = slice(0, LANES), slice(breadth - LANES, breadth)
    blank = (jnp.zeros((rows_here, LANES), F32),) * 2
    for field in range(3):
        copies[field].wait()

        def body(k, acc, field=field):
            west, east = [state[field, k, :, cols] for cols in ends]
            return place(group, k, west, east, acc)

        acc = lax.fori_loop(0, levels, body, blank, unroll=4)
        strips[0, field], strips[1, field] = acc
    slot = lax.rem(lane_of((rows_here, LANES)), TILE)
    strips[0, 0] = jnp.where(slot == 1, turn(strips[0, 2], -1, 1), strips[0, 0])
    strips[1, 0] = jnp.where(slot == HALO, turn(strips[1, 2], 1, 1), strips[1, 0])
    strips[0, 3], strips[1, 3] = pack_others(group, kmt[...].astype(F32), guess[...], ends)


def pack_cols(strips, rows_odd, rows_even, msg_odd, msg_even, own_tracer):
    tall = strips.shape[2] + 2 * TILE
    lat_even = is_even("lat")
    lon_even = is_even("lon")

    def tall_strips(field, south, north):
        return [
            stacked(
                south[:, i * LANES : (i + 1) * LANES],
                strips[i, field],
                north[:, i * LANES : (i + 1) * LANES],
            )
            for i in range(2)
        ]

    def put(number, field, south, north):
        base = number * tall
        to_west, to_east = tall_strips(field, south, north)
        a, b = swap(lon_even, to_east, to_west)
        msg_even[base : base + tall] = a
        msg_odd[base : base + tall] = b

    halos = []
    for slot in range(STRIPS, SLOTS):
        north, south = swap(lat_even, rows_even[slot], rows_odd[slot])
        halos.append((south, north))
    put(0, 0, *halos[0])
    put(1, 1, *halos[1])
    put(2, 3, *halos[2])
    own_tracer[0], own_tracer[1] = tall_strips(
        2, turn(halos[0][0], -1, 0), turn(halos[0][1], 1, 0)
    )


def rotation_at(row, rows_here):
    total_rows = rows_here * lax.axis_size("lat")
    row = (row + lax.axis_index("lat") * rows_here).astype(F32)
    angle = jnp.pi / 180.0 * (-80.0 + 160.0 * (row + 0.5) / total_rows)
    return coriolis_scale * jnp.sin(angle)


def around(x):
    return east_of(x), west_of(x), north_of(x), south_of(x)


def count_wet(sides, level):
    total = None
    for side in sides:
        term = jnp.where(side > level, 1.0, 0.0)
        total = term if total is None else total + term
    return total


def spread(x, sides, count, coefficient, zonal, merid):
    east, west, north, south = sides
    laplace = east + west + north + south - count * x
    return (
        (time_step * coefficient) * laplace
        - zonal * (east - west)
        - merid * (north - south)
    )


carry = 0.5 * time_step * advection_scale


def advance_flow(u, v, wet, count, half_turn, around=around):
    zonal, merid = (carry * u, carry * v)
    new_u = u + (spread(u, around(u), count, viscosity, zonal, merid) + half_turn * v)
    new_v = v + (spread(v, around(v), count, viscosity, zonal, merid) - half_turn * u)
    return jnp.where(wet, new_u, 0.0), jnp.where(wet, new_v, 0.0)


def is_sum_u(row, southern):
    first = TILE - 5 if southern else 1
    return (row >= first) & (row < first + 4)


def pack_rows(state, kmt, guess, msg_odd, msg_even, ends, wet_ends, guess_ends, sems):
    levels, rows_here, breadth = state.shape[1:]
    even = is_even("lat")
    parts = [slice(k, k + levels // 4) for k in range(0, levels, levels // 4)]
    copies = []
    for part in [None] + parts:
        copies.append([])
        for number, rows in enumerate((slice(0, TILE), slice(rows_here - TILE, rows_here))):
            held = slice(number * TILE, (number + 1) * TILE)
            if part is not None:
                pairs_of_refs = [(state.at[:, part, rows, :], ends.at[:, part, held, :])]
            else:
                pairs_of_refs = [
                    (kmt.at[rows, :], wet_ends.at[held, :]),
                    (guess.at[rows, :], guess_ends.at[held, :]),
                ]
            for source, target in pairs_of_refs:
                item = pltpu.make_async_copy(source, target, sems.at[sum(map(len, copies))])
                item.start()
                copies[-1].append(item)
    row = lax.broadcasted_iota(jnp.int32, (2 * TILE, LANES), 0)
    rotation = rotation_at(jnp.where(row < TILE, row, row + rows_here - 2 * TILE), rows_here)
    half_turn = time_step * rotation[:, :1]
    group = lane_of((2 * TILE, LANES)) // TILE
    row = lax.broadcasted_iota(jnp.int32, (2 * TILE, breadth), 0)
    borrowed = (row == TILE - 1) | (row == TILE)
    for item in copies[0]:
        item.wait()

    top = row == 2 * TILE - 1

    def within(x):
        east, west, north, south = around(x)
        return east, west, jnp.where(top, 0.0, north), jnp.where(row == 0, 0.0, south)

    depth = wet_ends[...].astype(F32)
    beside = within(depth)
    cut = slice(0, LANES), slice(breadth - LANES, breadth)
    starts = guess_ends[...]
    others = pack_others(group, depth, starts, cut)

    def body(k, carried):
        sum_u, sum_v, strips_u, strips_v = carried
        level = k.astype(F32)
        wet = depth > level
        raw_u, raw_v, raw_t = [ends[field, k] for field in range(3)]
        u = jnp.where(wet, raw_u, 0.0)
        v = jnp.where(wet, raw_v, 0.0)
        new_u, new_v = advance_flow(
            u, v, wet, count_wet(beside, level), half_turn, within
        )
        moved = jnp.concatenate([turn(raw_t[:TILE], -1, 0), turn(raw_t[TILE:], 1, 0)], axis=0)
        lent = jnp.where(borrowed, moved, raw_u)
        strips_u = place(group, k, lent[:, cut[0]], lent[:, cut[1]], strips_u)
        strips_v = place(group, k, raw_v[:, cut[0]], raw_v[:, cut[1]], strips_v)
        return sum_u + new_u, sum_v + new_v, strips_u, strips_v

    empty = jnp.zeros((2 * TILE, breadth), F32)
    blank = (jnp.zeros((2 * TILE, LANES), F32),) * 2
    carried = (empty, empty, blank, blank)
    for part, items in zip(parts, copies[1:]):
        for item in items:
            item.wait()
        carried = lax.fori_loop(part.start, part.stop, body, carried, unroll=4)
    sum_u, sum_v, strips_u, strips_v = carried

    def put(slot, low, high):
        a, b = swap(even, high, low)
        msg_even[slot] = a
        msg_odd[slot] = b

    row = lax.rem(lax.broadcasted_iota(jnp.int32, (2 * TILE, breadth), 0), TILE)
    first = jnp.concatenate(
        [is_sum_u(row[:TILE], False), is_sum_u(row[TILE:], True)], axis=0
    )
    moved = jnp.concatenate([turn(sum_v[:TILE], 4, 0), turn(sum_v[TILE:], 4, 0)], axis=0)
    spare = starts[:TILE], starts[TILE:]
    for shift, at, total in ((-2, TILE - 2, sum_u), (-1, TILE - 1, sum_v)):
        spare = (
            jnp.where(row[:TILE] == at, turn(total[:TILE], shift, 0), spare[0]),
            jnp.where(
                row[TILE:] == at - TILE + 2, turn(total[TILE:], shift + 3, 0), spare[1]
            ),
        )
    starts = jnp.concatenate(spare, axis=0)
    whole = [depth, starts, jnp.where(first, sum_u, moved)]
    whole += [jnp.concatenate(pair, axis=1) for pair in (strips_u, strips_v, others)]
    for slot, value in enumerate(whole, KMT):
        put(slot, value[:TILE], value[TILE:])
    row = lax.broadcasted_iota(jnp.int32, (TILE, breadth), 0)
    for field, first in ((0, U_ROWS), (1, V_ROWS), (2, T_ROWS)):
        for tile in range(levels // TILE):
            low = high = jnp.zeros((TILE, breadth), F32)
            for q in range(TILE):
                value = ends[field, tile * TILE + q]
                here = row == q
                low = jnp.where(here, turn(value[:TILE], q, 0), low)
                high = jnp.where(here, turn(value[TILE:], q + 1, 0), high)
            put(first + tile, low, high)


def halo_rows(rows_even, rows_odd, first, k):
    tile = first + k // TILE
    north, south = swap(is_even("lat"), rows_even[tile], rows_odd[tile])
    at = lax.rem(k, TILE)
    south = pltpu.roll(south, lax.rem(2 * TILE - 1 - at, TILE), 0)
    north = pltpu.roll(north, lax.rem(TILE - at, TILE), 0)
    return south, north


def advance_inner(state, kmt, rows_odd, rows_even, flow, tracer, flow_u, flow_v, turning):
    levels, rows_here, breadth = state.shape[1:]
    tall = rows_here + 2 * TILE
    lat_even = is_even("lat")

    def halos(slot):
        north, south = swap(lat_even, rows_even[slot], rows_odd[slot])
        return south, north

    south, north = halos(KMT)
    depth = stacked(south, kmt[...].astype(F32), north)
    beside = around(depth)
    row = lax.broadcasted_iota(jnp.int32, (tall, LANES), 0)
    rotation = rotation_at(row - TILE, rows_here)
    turning[...] = rotation
    half_turn = time_step * rotation[:, :1]
    own = slice(TILE, TILE + rows_here)
    flow_u[...] = jnp.zeros_like(flow_u)
    flow_v[...] = jnp.zeros_like(flow_v)

    def body(k, _):
        level = k.astype(F32)
        wet = depth > level
        count = count_wet(beside, level)
        u_south, u_north = halo_rows(rows_even, rows_odd, U_ROWS, k)
        v_south, v_north = halo_rows(rows_even, rows_odd, V_ROWS, k)
        t_south, t_north = halo_rows(rows_even, rows_odd, T_ROWS, k)
        u = jnp.where(wet, stacked(u_south, state[0, k], u_north), 0.0)
        v = jnp.where(wet, stacked(v_south, state[1, k], v_north), 0.0)
        new_u, new_v = advance_flow(u, v, wet, count, half_turn)
        flow_u[own] += new_u[own]
        flow_v[own] += new_v[own]
        for tile, inner, shift, sign in (
            (slice(0, TILE), slice(TILE, 2 * TILE), -1, 1.0),
            (slice(tall - TILE, tall), slice(tall - 2 * TILE, tall - TILE), 1, -1.0),
        ):
            open_to = turn(jnp.where(wet[inner], 1.0, 0.0), shift, 0)
            across = sign * carry * v[tile]
            for value, flow_sum in ((u, flow_u), (v, flow_v)):
                other = turn(value[inner], shift, 0)
                term = (time_step * viscosity) * (other - open_to * value[tile]) - across * other
                flow_sum[tile] += jnp.where(wet[tile], term, 0.0)
        flow[0, k] = new_u[own]
        flow[1, k] = new_v[own]
        here = state[2, k]
        stack_t = jnp.where(wet, stacked(t_south, here, t_north), 0.0)
        middle = stack_t[own]
        sides = (east_of(middle), west_of(middle), north_of(stack_t)[own], south_of(stack_t)[own])
        change = spread(
            middle, sides, count[own], diffusivity, carry * u[own], carry * v[own]
        )
        above = state[2, jnp.maximum(k - 1, 0)]
        below = state[2, jnp.minimum(k + 1, levels - 1)]
        vertical = (above - here) + jnp.where(depth[own] > level + 1.0, below - here, 0.0)
        tracer[k] = jnp.where(
            wet[own], here + (change + (time_step * vertical_mix) * vertical), 0.0
        )
        return 0

    lax.fori_loop(0, levels, body, 0, unroll=2)
    row = lax.broadcasted_iota(jnp.int32, (tall, breadth), 0)
    outer = (row < TILE - 1) | (row > TILE + rows_here)
    edge = (row == TILE - 1) | (row == TILE + rows_here)
    inner = jnp.zeros((rows_here, breadth), F32)
    sums, spare = halos(SUMS), halos(GUESS)
    for number, flow_sum in enumerate((flow_u, flow_v)):
        further = stacked(turn(sums[0], -4 * number, 0), inner, turn(sums[1], -4 * number, 0))
        next_row = stacked(
            turn(spare[0], -1 - number, 0), inner, turn(spare[1], 2 - number, 0)
        )
        total = flow_sum[...]
        total = jnp.where(edge, total + next_row, total)
        flow_sum[...] = jnp.where(outer, further, total)


def fill_ends(x, west, east):
    lane = lane_of((x.shape[0], LANES))
    tiles = [x[:, i : i + LANES] for i in range(0, x.shape[1], LANES)]
    if west is not None:
        tiles[0] = jnp.where(lane == 0, west, tiles[0])
    if east is not None:
        tiles[-1] = jnp.where(lane == LANES - 1, east, tiles[-1])
    return jnp.concatenate(tiles, axis=1)


def roll_to(x, source, target, k):
    return turn(x, target - source - TILE * k, 1)


def krylov(
    sent_even, sent_odd, got_odd, got_even, flow_u, flow_v, kmt, guess,
    rows_even, rows_odd, turning, own_tracer, edges, basis, moments,
):
    levels = LEVELS
    rows_here, breadth = kmt.shape
    tall = rows_here + 2 * TILE
    lat_even = is_even("lat")
    lon_even = is_even("lon")
    lane = lane_of((tall, LANES))
    place = lax.rem(lane, TILE)
    group = lane // TILE
    level = group.astype(F32)
    own = slice(TILE, TILE + rows_here)
    half_turn = time_step * turning[...]

    def received(slot):
        rows = slice(slot * tall, (slot + 1) * tall)
        from_east, from_west = swap(lon_even, got_even[rows], got_odd[rows])
        return from_west, from_east

    def strips(slot):
        rows = slice(slot * tall, (slot + 1) * tall)
        to_east, to_west = swap(lon_even, sent_even[rows], sent_odd[rows])
        from_west, from_east = received(slot)
        west = jnp.where(place < HALO, from_west, turn(to_west, 4, 1))
        east = jnp.where(place >= TILE - HALO, from_east, turn(to_east, -4, 1))
        return west, east

    u_sides, v_sides, other = [strips(slot) for slot in range(3)]
    from_west, from_east = received(0)
    t_sides = (
        jnp.where(place == HALO - 1, turn(from_west, -1, 1), turn(own_tracer[0], 4, 1)),
        jnp.where(place == TILE - HALO, turn(from_east, 1, 1), turn(own_tracer[1], -4, 1)),
    )
    sums = []
    for side in range(2):
        depth = jnp.where(group == 1, turn(other[side], TILE, 1), other[side])
        wet = depth > level
        count = count_wet(around(depth), level)
        u = jnp.where(wet, u_sides[side], 0.0)
        v = jnp.where(wet, v_sides[side], 0.0)
        new_u, new_v = advance_flow(u, v, wet, count, half_turn)
        here = jnp.where(wet, t_sides[side], 0.0)
        change = spread(here, around(here), count, diffusivity, carry * u, carry * v)
        above = jnp.where(group > 0, turn(here, TILE, 1) - here, 0.0)
        below = jnp.where(depth > level + 1.0, turn(here, -TILE, 1) - here, 0.0)
        new_t = jnp.where(
            wet, here + (change + (time_step * vertical_mix) * (above + below)), 0.0
        )
        edges[side, 0] = new_u[own]
        edges[side, 1] = new_v[own]
        edges[side, 2] = new_t[own]
        sums.append((new_u, new_v))

    def fold(x, step):
        return x + turn(x, step, 1)

    (u_west, v_west), (u_east, v_east) = [
        [fold(x, LANES // 2) for x in side] for side in sums
    ]
    half = lane < LANES // 2
    west = fold(jnp.where(half, u_west, v_west), LANES // 4)
    east = fold(jnp.where(half, u_east, v_east), -LANES // 4)
    quarter = lax.rem(lane // (LANES // 4), 2) == 1
    folded = fold(fold(jnp.where(quarter, west, east), 2 * TILE), TILE)

    def assemble(field, west, west_at, east, east_at, seam):
        west = turn(west, -HALO - west_at, 1)
        east = turn(east, -2 - east_at, 1)
        halo = jnp.where(lane < LANES // 2, east, west)
        tiles = [field[:, i : i + LANES] for i in range(0, breadth, LANES)]
        if seam:
            tiles[0] = jnp.where(lane == 0, west, tiles[0])
            tiles[-1] = jnp.where(lane == LANES - 1, east, tiles[-1])
        return jnp.concatenate(tiles + [halo], axis=1)

    def tall_field(slot, value):
        north, south = swap(lat_even, rows_even[slot], rows_odd[slot])
        return stacked(south, value, north)

    last = LANES // 4 - TILE
    wide_u = assemble(flow_u[...], folded, LANES // 4 + last, folded, last, True)
    wide_v = assemble(flow_v[...], folded, 3 * LANES // 4 + last, folded, LANES // 2 + last, True)
    wet_levels = assemble(
        tall_field(KMT, kmt[...].astype(F32)), other[0], 0, other[1], 0, False
    )
    first = assemble(tall_field(GUESS, guess[...]), other[0], TILE, other[1], TILE, False)

    divergence = 0.5 * (east_of(wide_u) - west_of(wide_u)) + 0.5 * (
        north_of(wide_v) - south_of(wide_v)
    )
    depth = wet_levels * (1.0 / levels)
    ocean = wet_levels > 0.0
    to_east = edge_weight * jnp.minimum(depth, east_of(depth))
    to_north = edge_weight * jnp.minimum(depth, north_of(depth))
    depth_north = north_of(depth)
    to_ne = corner_weight * jnp.minimum(depth, east_of(depth_north))
    to_nw = corner_weight * jnp.minimum(depth, west_of(depth_north))
    to_west = west_of(to_east)
    to_south = south_of(to_north)
    to_sw = south_of(west_of(to_ne))
    to_se = south_of(east_of(to_nw))
    diagonal = storage + (
        (to_east + to_west) + (to_north + to_south) + ((to_ne + to_nw) + (to_se + to_sw))
    )

    def neighbours(x):
        up, down = (north_of(x), south_of(x))
        eastern = to_east * x + to_ne_w * up + to_se_w * down
        western = to_west * x + to_nw_e * up + to_sw_e * down
        return to_north * up + to_south * down + (east_of(eastern) + west_of(western))

    to_ne_w = west_of(to_ne)
    to_se_w = west_of(to_se)
    to_nw_e = east_of(to_nw)
    to_sw_e = east_of(to_sw)
    to_east, to_west = (west_of(to_east), east_of(to_west))

    start = jnp.where(ocean, first, 0.0)
    rhs = jnp.where(ocean, storage * (start - time_step * divergence), 0.0)
    residual = rhs - (diagonal * start - neighbours(start))
    inverse = 1.0 / diagonal
    vectors = [residual * inverse]
    basis[0] = start
    basis[1] = vectors[0]
    for k in range(1, ITERS):
        vectors.append(neighbours(vectors[-1]) * inverse)
        basis[k + 1] = vectors[k]
    last = neighbours(vectors[-1])

    def inner(x):
        return x[own, :breadth]

    weighted = [inner(diagonal * x) for x in vectors] + [inner(last)]
    held = [inner(x) for x in vectors]
    slot = lane_of((TILE, LANES))
    total = jnp.zeros((TILE, LANES), F32)
    for m in range(2 * ITERS):
        product = held[m // 2] * weighted[(m + 1) // 2]
        folded = None
        for i in range(0, rows_here, TILE):
            for j in range(0, breadth, LANES):
                part = product[i : i + TILE, j : j + LANES]
                folded = part if folded is None else folded + part
        total = jnp.where(slot == m, jnp.sum(folded, axis=1, keepdims=True), total)
    moments[...] = jnp.sum(total, axis=0, keepdims=True)


def over(a, b):
    return a / jnp.where(b > 1e-37, b, 1.0)


def finish(shares, basis, edges, kmt, flow, tracer, out, pressure, done, held, sems, held_sem):
    levels, rows_here, breadth = tracer.shape
    own = slice(TILE, TILE + rows_here)
    chunks = sems.shape[1]
    size = levels // chunks

    def send(first, last, c):
        part = pl.ds(c * size, size)
        fields = slice(first, last)
        return pltpu.make_async_copy(
            done.at[fields, part], out.at[fields, part], sems.at[first // 2, c]
        )

    def ended(value, field, k):
        return fill_ends(
            value,
            roll_to(edges[0, field], HALO, 0, k),
            roll_to(edges[1, field], 1, LANES - 1, k),
        )

    totals = shares[...]
    while totals.shape[0] % (2 * TILE) == 0:
        part = totals.shape[0] // 2
        totals = totals[:part] + totals[part:]
    totals = jnp.sum(totals.reshape(-1, TILE, LANES), axis=0)
    for step in (1, 2, 4):
        totals = totals + turn(totals, step, 0)
    lane = lane_of((TILE, LANES))

    def everywhere(m):
        one = jnp.sum(jnp.where(lane == m, totals, 0.0), axis=1, keepdims=True)
        return jnp.broadcast_to(one, (TILE, LANES))

    res = [everywhere(m) for m in range(2 * ITERS)]
    dirn = list(res)
    one, zero = (jnp.ones((TILE, LANES), F32), jnp.zeros((TILE, LANES), F32))
    res_in = [one] + [zero] * (ITERS - 1)
    dir_in = list(res_in)
    height_in = [zero] * ITERS
    for k in range(ITERS):
        step = over(res[k], dirn[k] - dirn[k + 1])
        step = jnp.clip(step, 1.0 / HIGHEST, 1.0 / LOWEST)
        height_in = [h + step * d for h, d in zip(height_in, dir_in)]
        if k + 1 < ITERS:
            new = [res[m] - step * (dirn[m] - dirn[m + 1]) for m in range(len(dirn) - 1)]
            ratio = jnp.clip((step * over(1.0, res[k])) * new[k + 1], 0.0, HIGHEST / LOWEST)
            dirn = [n + ratio * d for n, d in zip(new, dirn)]
            res = new
            moved = [zero] + dir_in[:-1]
            res_in = [r - step * (d - m) for r, d, m in zip(res_in, dir_in, moved)]
            dir_in = [r + ratio * d for r, d in zip(res_in, dir_in)]

    for k in range(levels):
        done[2, k] = ended(tracer[k], 2, k)
    for c in range(chunks):
        send(2, 3, c).start()

    def tile_of(i, j):
        cut = slice(i, i + TILE), slice(j, j + LANES)
        value = basis[0, *cut]
        for k in range(ITERS):
            value = value + height_in[k] * basis[k + 1, *cut]
        return value

    tall, wide = basis.shape[1:]
    height = jnp.concatenate(
        [
            jnp.concatenate([tile_of(i, j) for j in range(0, wide, LANES)], axis=1)
            for i in range(0, tall, TILE)
        ],
        axis=0,
    )
    held[...] = gravity * height[own, :breadth]
    pressure_out = pltpu.make_async_copy(held, pressure, held_sem.at[0])
    pressure_out.start()
    pull = 0.5 * time_step * gravity
    slope_east = pull * (east_of(height) - west_of(height))[own, :breadth]
    slope_north = pull * (north_of(height) - south_of(height))[own, :breadth]
    wet_levels = kmt[...]
    for c in range(chunks):
        for k in range(c * size, (c + 1) * size):
            wet = wet_levels > k
            for field, slope in ((0, slope_east), (1, slope_north)):
                done[field, k] = jnp.where(wet, ended(flow[field, k], field, k) - slope, 0.0)
        send(0, 2, c).start()
    pressure_out.wait()
    for c in range(chunks):
        send(2, 3, c).wait()
        send(0, 2, c).wait()


def pairs(axis):
    peers = lax.axis_size(axis)
    even = [(i, i ^ 1) for i in range(peers)]
    odd = [(i, ((i + 1) ^ 1) - 1) for i in range(1, peers - 1)]
    if axis == "lon":
        odd += [(0, peers - 1), (peers - 1, 0)]
    return even, odd


def exchange(axis, to_even, to_odd):
    even, odd = pairs(axis)
    from_odd = lax.ppermute(to_odd, axis, odd)
    return lax.ppermute(to_even, axis, even), from_odd


def on_device(state, kmt, first_guess):
    _, levels, rows_here, breadth = state.shape
    tall = rows_here + 2 * TILE
    wide = breadth + LANES
    shape = lambda *dims: jax.ShapeDtypeStruct(dims, F32)

    devices = lax.axis_size("lon") * lax.axis_size("lat")
    hbm = pl.BlockSpec(memory_space=pltpu.HBM)
    vmem = pl.BlockSpec(memory_space=pltpu.VMEM)
    to_odd, to_even = pl.pallas_call(
        pack_rows,
        in_specs=[hbm] * 3,
        out_specs=[vmem] * 2,
        out_shape=[pltpu.VMEM((SLOTS, TILE, breadth), F32)] * 2,
        scratch_shapes=[
            pltpu.VMEM((3, levels, 2 * TILE, breadth), F32),
            pltpu.VMEM((2 * TILE, breadth), jnp.int32),
            pltpu.VMEM((2 * TILE, breadth), F32),
            pltpu.SemaphoreType.DMA((12,)),
        ],
        compiler_params=params(VMEM_FIRST),
    )(state, kmt, first_guess)
    rows_even, rows_odd = exchange("lat", to_even, to_odd)

    held, strips = pl.pallas_call(
        pack_own,
        in_specs=[hbm, vmem, vmem],
        out_shape=[pltpu.VMEM(state.shape, F32), pltpu.VMEM((2, 4, rows_here, LANES), F32)],
        scratch_shapes=[pltpu.SemaphoreType.DMA((3,))],
        compiler_params=params(VMEM_OWN),
        cost_estimate=cost(state.size),
    )(state, kmt, first_guess)
    length = 3 * tall
    sent_odd, sent_even, own_tracer = pl.pallas_call(
        pack_cols,
        out_shape=[shape(length, LANES)] * 2 + [shape(2, tall, LANES)],
        compiler_params=params(),
    )(strips, rows_odd, rows_even)
    got_even, got_odd = exchange("lon", sent_even, sent_odd)

    flow, tracer, flow_u, flow_v, turning = pl.pallas_call(
        advance_inner,
        out_shape=[
            shape(2, levels, rows_here, breadth),
            shape(levels, rows_here, breadth),
            shape(tall, breadth),
            shape(tall, breadth),
            shape(tall, LANES),
        ],
        compiler_params=params(),
        cost_estimate=cost(state.size),
    )(held, kmt, rows_odd, rows_even)

    edges, basis, moments = pl.pallas_call(
        krylov,
        out_shape=[
            shape(2, 3, rows_here, LANES),
            shape(ITERS + 1, tall, wide),
            shape(1, LANES),
        ],
        compiler_params=params(),
    )(
        sent_even, sent_odd, got_odd, got_even, flow_u, flow_v, kmt, first_guess,
        rows_even, rows_odd, turning, own_tracer,
    )

    shares = jnp.broadcast_to(moments[None], (devices, 1, LANES))
    shares = lax.all_to_all(shares, ("lon", "lat"), 0, 0)
    return pl.pallas_call(
        finish,
        in_specs=[vmem] * 6,
        out_specs=[hbm, hbm],
        out_shape=[shape(3, levels, rows_here, breadth), shape(rows_here, breadth)],
        scratch_shapes=[
            pltpu.VMEM((3, levels, rows_here, breadth), F32),
            pltpu.VMEM((rows_here, breadth), F32),
            pltpu.SemaphoreType.DMA((2, 4)),
            pltpu.SemaphoreType.DMA((1,)),
        ],
        compiler_params=params(),
    )(shares.reshape(devices, LANES), basis, edges, kmt, flow, tracer)


def solution(mesh):
    placed = (P(None, None, "lat", "lon"), P("lat", "lon"), P("lat", "lon"))
    return jax.shard_map(
        on_device,
        mesh=mesh,
        in_specs=placed,
        out_specs=(P(None, None, "lat", "lon"), P("lat", "lon")),
        check_vma=False,
    )
```
